256 devices in a mesh: lang: 4 (over x), fsdp: 16 (over z, core), dp: 4 (over y).
Axes of the slice: x: 4, y: 4, z: 8, core: 2. Of those that a mesh axis runs over, the one named last changes fastest.
Arguments:
- tokens_in: bfloat16 [1024, 8192], P('dp'), may hold values from -6 to 6
- cotangent: bfloat16 [1024, 16384], P('dp', ('lang', 'fsdp')), may hold values from -6 to 6
- gate_base: bfloat16 [8192, 16384], P('dp', ('lang', 'fsdp')), may hold values from -0.0625 to 0.0625
- up_base: bfloat16 [8192, 16384], P('dp', ('lang', 'fsdp')), may hold values from -0.0625 to 0.0625
- lang_delta: bfloat16 [4, 16, 4, 4, 32768], P('lang', 'fsdp'), may hold values from -0.1796875 to 0.1796875
- lang_cell: int32 [4, 16, 4, 4], P('lang', 'fsdp'), may hold values from -1 to 127, as said below
- group_lang: int32 [4], P('dp'), may hold values from 0 to 3
- task_delta: bfloat16 [1024, 32768], P(('lang', 'fsdp')), may hold values from -0.1796875 to 0.1796875
- task_slab: int32 [1024, 1], P(('lang', 'fsdp')), may hold values from 0 to 15; in each aligned block of 16 rows (0 to 15, 16 to 31, ...) at most 2 rows name the same one
- task_cell: int32 [1024, 1], P(('lang', 'fsdp')), may hold values from 0 to 127
Outputs:
- grad_input: bfloat16 [1024, 8192], P('dp', ('lang', 'fsdp'))
- task_grad: float32 [1024, 32768], P(('lang', 'fsdp'))
The draws below stay inside these ranges and needn't reach their ends.
Inputs may be any that keep to these rules, and one draw needn't show every extreme that they name: `lang_cell`: -1 marks an empty slot; every other entry is a cell of the slab. In every draw the list of slab 0 is full for every language. `task_slab`: among the 16 task blocks of one device, no slab is named more than 2 times; some slab is named exactly 2 times.
All inputs are finite; a program needn't handle non-finite values.
Results may differ from the reference program's by a relative error of at most 0.0063.
Values may be sent and summed in bfloat16 or wider, within the bound.
No kernel may reach another device: no remote copies, remote signals or barrier semaphores. Data moves between devices by JAX's collectives and lax.ppermute only.
A program may use at most 128 MiB of HBM per device.

```python
import math
import jax
import jax.numpy as jnp
import numpy as np
from jax import lax

D = 8192
FF = 16384
BLK = 128
TG = 256
NLB = 4
NTD = 16
LANGS = 4
FSDP_WAYS = 16
SLAB_BLOCKS = 2
CAP = 2
TOKENS = 1024
TASKS = 1024
N_LANG = 4
N_FSDP = 16
N_DP = 4


def draw_lang_cell(key, part):
    key = jax.random.fold_in(key, 11)
    key_cells, key_counts = jax.random.split(key)
    cell_total = D // BLK * (FF // (N_LANG * N_FSDP) // BLK)
    cell_ids = jax.random.randint(key_cells, (N_LANG, N_FSDP, N_LANG, NLB), 0, cell_total)
    how_many = jax.random.randint(key_counts, (N_LANG, N_FSDP, N_LANG, 1), 1, NLB + 1)
    how_many = how_many.at[:, 0, 0, 0].set(NLB)
    slot_index = jnp.arange(NLB, dtype=jnp.int32)[None, None, None, :]
    return jnp.where(slot_index < how_many, cell_ids, -1).astype(jnp.int32)


def with_ends(entries, key, smallest, largest):
    dims = entries.shape
    place = [jax.random.randint(jax.random.fold_in(key, axis), (), 0, dims[axis]) for axis in range(len(dims))]
    entries = entries.at[tuple(place)].set(smallest)
    longest = dims.index(max(dims))
    place[longest] = (place[longest] + 1) % dims[longest]
    return entries.at[tuple(place)].set(largest)


def levels(key, dims, cuts, least, high):
    loudness, own = 1.0, jax.random.fold_in(key, 6)
    for dim, shards_of in cuts:
        draws = jnp.exp(jax.random.uniform(jax.random.fold_in(own, dim), (shards_of,), jnp.float32, least / len(cuts), high / len(cuts)))
        loudness = loudness * jnp.repeat(draws, dims[dim] // shards_of).reshape([-1 if axis == dim else 1 for axis in range(len(dims))])
    return loudness


def shared_out(rng, own, number, rows, amount, top, bound, skew):
    sequence = jax.random.permutation(rng, amount)
    packed, ordinary = load_shares(amount, rows * top, bound, skew, True), load_shares(amount, rows * top, bound, skew, False)
    places = jnp.arange(amount)

    def named(tallies, rotation):
        used = int((tallies > 0).sum())
        fixed = max(1, used // 4)
        shifted = fixed + (places - fixed + rotation * (used - fixed)) % max(1, amount - fixed)
        return jnp.zeros((amount,), jnp.int32).at[sequence[jnp.where(places < fixed, places, shifted)]].set(jnp.asarray(tallies, jnp.int32))

    tallies = jnp.where(number % 4 == 0, named(packed, number // 4), named(ordinary, number - number // 4 - 1))
    mixed = jax.random.permutation(jax.random.fold_in(own, 3), amount)
    source_of, receiver = mixed[0:amount // 2 * 2:2], mixed[1:amount // 2 * 2:2]
    room = jnp.minimum(tallies[source_of] - 1, bound - tallies[receiver]) // 2
    room = jnp.where((source_of == sequence[0]) | (receiver == sequence[0]) | (tallies[receiver] == 0), 0, jnp.maximum(room, 0))
    shifted = jax.random.randint(jax.random.fold_in(own, 4), (amount // 2,), 0, 1 << 20) % (room + 1)
    tallies = tallies.at[source_of].add(-shifted).at[receiver].add(shifted)
    members = jnp.searchsorted(jnp.cumsum(tallies), jnp.arange(rows * top), side="right").astype(jnp.int32)
    table = members.reshape(top, rows).T
    table = table[jax.random.permutation(jax.random.fold_in(own, 1), rows)]
    rotation = jax.random.randint(jax.random.fold_in(own, 2), (rows, 1), 0, top)
    return jnp.take_along_axis(table, (jnp.arange(top)[None, :] + rotation) % top, axis=1)


def load_shares(count, total, bound, slope, full):
    loads = [(1 << 20) // math.isqrt(standing ** slope) + 1 for standing in range(1, count + 1)]
    largest = bound if full else min(bound, max(-(-total // count), total * loads[0] // sum(loads)))
    least = 1 if total - largest >= count - 1 else 0
    counts, spare = [largest] + [least] * (count - 1), total - largest - least * (count - 1)
    while spare > 0:
        candidates = [i for i in range(1, count) if counts[i] < largest] or [i for i in range(1, count) if counts[i] < bound]
        pool, budget = sum([loads[i] for i in candidates]), spare
        for i in candidates:
            extra = min(bound - counts[i], max(1, budget * loads[i] // pool), spare)
            counts[i] = counts[i] + extra
            spare = spare - extra
    return np.array(counts)


def gaussian(stream_key, shape, scale, bound, pieces=(), held_as=jnp.bfloat16):
    loudness = levels(stream_key, shape, pieces, -0.22, 0.18) if pieces else 1.0
    entries = jax.random.normal(stream_key, shape, jnp.float32) * scale * loudness
    return jnp.minimum(jnp.maximum(entries, -bound), bound).astype(held_as)


def setup_inputs(seed: int = 0) -> dict:
    splits = jax.random.split(jax.random.key(seed), 11)
    tokens_in = gaussian(splits[0], (TOKENS, D), 1.0, 6.0, ((0, 4),))
    cotangent = gaussian(splits[1], (TOKENS, FF), 1.0, 6.0, ((0, 4), (1, 64)))
    gate_base = gaussian(splits[2], (D, FF), D ** -0.5, 0.0625, ((0, 4), (1, 64)))
    up_base = gaussian(splits[3], (D, FF), D ** -0.5, 0.0625, ((0, 4), (1, 64)))
    lang_delta = gaussian(splits[4], (LANGS, FSDP_WAYS, LANGS, NLB, 2 * BLK * BLK), 0.03, 0.1796875, ((0, 4), (1, 16)))
    lang_cell = draw_lang_cell(jax.random.fold_in(splits[10], 71), 0)
    group_lang = with_ends(jax.random.randint(splits[6], (N_DP,), 0, LANGS), jax.random.fold_in(splits[6], 1), 0, LANGS - 1).astype(jnp.int32)
    task_delta = gaussian(splits[7], (TASKS, 2 * BLK * BLK), 0.03, 0.1796875, ((0, 64),))
    task_slab_keys = jax.random.split(jax.random.fold_in(splits[8], 1), TASKS // NTD)
    task_slab_turns = jax.random.permutation(jax.random.fold_in(splits[8], 3), TASKS // NTD)
    task_slab = jax.vmap(lambda own, number: shared_out(jax.random.fold_in(splits[8], 2), own, number, NTD, FSDP_WAYS, 1, CAP, 2))(task_slab_keys, task_slab_turns).reshape((TASKS, 1))
    task_cell = with_ends(jax.random.randint(splits[9], (TASKS, 1), 0, D // BLK * SLAB_BLOCKS), jax.random.fold_in(splits[9], 1), 0, (D // BLK * SLAB_BLOCKS) - 1).astype(jnp.int32)
    return dict(tokens_in=tokens_in, cotangent=cotangent, gate_base=gate_base, up_base=up_base, lang_delta=lang_delta, lang_cell=lang_cell, group_lang=group_lang, task_delta=task_delta, task_slab=task_slab, task_cell=task_cell)


def compose_matrix(base_matrix, row_ids, col_ids, tile_vals):
    changes = jnp.zeros((D // BLK, FF // BLK, BLK, BLK), jnp.float32)
    changes = changes.at[row_ids, col_ids].add(tile_vals.reshape(-1, BLK, BLK))
    changes = changes.transpose(0, 2, 1, 3).reshape(D, FF)
    return (base_matrix.astype(jnp.float32) + changes).astype(jnp.bfloat16)


def backward_parts(gate_pre, up_pre, cot_rows):
    sigmoid_g = jax.nn.sigmoid(gate_pre)
    upstream = cot_rows.astype(jnp.float32)
    d_gate = upstream * up_pre * sigmoid_g * (1.0 + gate_pre * (1.0 - sigmoid_g))
    d_up = upstream * gate_pre * sigmoid_g
    return d_gate.astype(jnp.bfloat16), d_up.astype(jnp.bfloat16)


def reference(tokens_in, cotangent, gate_base, up_base, lang_delta, lang_cell, group_lang, task_delta, task_slab, task_cell):
    tile_size = BLK * BLK
    slab_width = FF // (N_LANG * N_FSDP) // BLK
    slab_number = jnp.arange(N_LANG, dtype=jnp.int32)[None, :] * N_FSDP + jnp.arange(N_FSDP, dtype=jnp.int32)[:, None]
    holder = jnp.arange(task_delta.shape[0], dtype=jnp.int32) // NTD
    task_rows = task_cell[:, 0] // slab_width
    task_cols = ((holder // N_FSDP) * N_FSDP + task_slab[:, 0]) * slab_width + task_cell[:, 0] % slab_width
    task_vals = task_delta.astype(jnp.float32)
    grad_parts = []
    task_sum = jnp.zeros(task_delta.shape, jnp.float32)
    for group_id in range(N_DP):
        language = group_lang[group_id]
        cell_ids = lax.dynamic_index_in_dim(lang_cell, language, 0, keepdims=False)
        lang_vals = lax.dynamic_index_in_dim(lang_delta, language, 0, keepdims=False).astype(jnp.float32)
        filled = cell_ids >= 0
        clamped = jnp.where(filled, cell_ids, 0)
        row_ids = (clamped // slab_width).reshape(-1)
        col_ids = (slab_number[:, :, None] * slab_width + clamped % slab_width).reshape(-1)
        lang_vals = jnp.where(filled[..., None], lang_vals, 0.0).reshape(-1, 2 * tile_size)
        all_rows = jnp.concatenate([row_ids, task_rows])
        all_cols = jnp.concatenate([col_ids, task_cols])
        all_vals = jnp.concatenate([lang_vals, task_vals], axis=0)
        gate_matrix = compose_matrix(gate_base, all_rows, all_cols, all_vals[:, :tile_size])
        up_matrix = compose_matrix(up_base, all_rows, all_cols, all_vals[:, tile_size:])
        tokens_group = tokens_in[group_id * TG:(group_id + 1) * TG]
        cot_group = cotangent[group_id * TG:(group_id + 1) * TG]
        gate_pre = jnp.dot(tokens_group, gate_matrix, preferred_element_type=jnp.float32)
        up_pre = jnp.dot(tokens_group, up_matrix, preferred_element_type=jnp.float32)
        d_gate, d_up = backward_parts(gate_pre, up_pre, cot_group)
        input_grad = jnp.dot(d_gate, gate_matrix.T, preferred_element_type=jnp.float32)
        input_grad = input_grad + jnp.dot(d_up, up_matrix.T, preferred_element_type=jnp.float32)
        grad_parts.append(input_grad.astype(jnp.bfloat16))
        x_tiles = tokens_group.reshape(TG, D // BLK, BLK)[:, task_rows, :].astype(jnp.float32)
        g_tiles = d_gate.reshape(TG, FF // BLK, BLK)[:, task_cols, :].astype(jnp.float32)
        u_tiles = d_up.reshape(TG, FF // BLK, BLK)[:, task_cols, :].astype(jnp.float32)
        gate_grad = jnp.einsum('tmi,tmj->mij', x_tiles, g_tiles).reshape(-1, tile_size)
        up_grad = jnp.einsum('tmi,tmj->mij', x_tiles, u_tiles).reshape(-1, tile_size)
        task_sum = task_sum + jnp.concatenate([gate_grad, up_grad], axis=1)
    return jnp.concatenate(grad_parts, axis=0), task_sum
```

```python
import jax
import jax.numpy as jnp
from jax import lax
from jax.experimental import pallas as pl
from jax.experimental.pallas import tpu as pltpu
from jax.sharding import Mesh, PartitionSpec as P

BLK = 128
CAP = 2
PAD = 16
MIB = 1024 * 1024


def ring(axis, step):
    n = lax.axis_size(axis)
    return [(i, (i + step) % n) for i in range(n)]


def with_cells(tiles, cells):
    rows = jnp.broadcast_to(cells.astype(jnp.bfloat16)[..., None, None], cells.shape + (PAD, BLK))
    return jnp.concatenate([tiles, rows], axis=-2)


def place_kernel(dest_ref, tiles_ref, cells_ref, out_ref):
    n_out = out_ref.shape[0]

    def clear(i, carry):
        out_ref[i] = jnp.full(out_ref.shape[1:], -1.0, jnp.bfloat16)
        return carry

    lax.fori_loop(0, n_out, clear, 0)

    def put(i, carry):
        slot = dest_ref[i]
        out_ref[slot, 0 : 2 * BLK, :] = tiles_ref[i]
        out_ref[slot, 2 * BLK :, :] = jnp.full(
            (PAD, BLK), cells_ref[i].astype(jnp.float32), jnp.float32
        ).astype(jnp.bfloat16)
        return carry

    lax.fori_loop(0, tiles_ref.shape[0], put, 0)


def place(dest, tiles, cells, n_out):
    smem = pl.BlockSpec(memory_space=pltpu.SMEM)
    vmem = pl.BlockSpec(memory_space=pltpu.VMEM)
    return pl.pallas_call(
        place_kernel,
        out_shape=jax.ShapeDtypeStruct((n_out, 2 * BLK + PAD, BLK), jnp.bfloat16),
        in_specs=[smem, vmem, smem],
        out_specs=vmem,
        compiler_params=pltpu.CompilerParams(vmem_limit_bytes=16 * MIB),
        name="place",
    )(dest, tiles, cells)


def core_kernel(
    n_task,
    info_ref,
    cells_ref,
    leader_ref,
    x_ref,
    xt_ref,
    cot_ref,
    task_ref,
    lang_ref,
    g0,
    g1,
    g2,
    g3,
    u0,
    u1,
    u2,
    u3,
    grads_ref,
    tgrads_ref,
    gate_m,
    up_m,
    acc,
    gate_pre,
    up_pre,
    d_gate,
    d_up,
    d_cols,
    sems,
):
    f32, bf16 = jnp.float32, jnp.bfloat16
    ways = 4
    part = g0.shape[0]
    me = info_ref[0]
    copies = []
    for k, (g, u) in enumerate(((g0, u0), (g1, u1), (g2, u2), (g3, u3))):
        start = pl.multiple_of(lax.rem(me + k, ways) * part, part)
        copies.append(pltpu.make_async_copy(g, gate_m.at[pl.ds(start, part)], sems.at[2 * k]))
        copies.append(pltpu.make_async_copy(u, up_m.at[pl.ds(start, part)], sems.at[2 * k + 1]))
    for c in copies:
        c.start()
    for c in copies:
        c.wait()

    n_slots = acc.shape[0]

    def spot(cell):
        row = pl.multiple_of(lax.shift_right_logical(cell, 1) * BLK, BLK)
        col = pl.multiple_of(lax.bitwise_and(cell, 1) * BLK, BLK)
        return pl.ds(row, BLK), pl.ds(col, BLK)

    def gather_from(tiles, first):
        def step(i, carry):
            s = i + first
            cell = cells_ref[s]
            lead = leader_ref[s]

            @pl.when((cell >= 0) & (lead == s))
            def _():
                at = spot(cell)
                acc[s, 0:BLK] = gate_m[at].astype(f32) + tiles[i, 0:BLK].astype(f32)
                acc[s, BLK:] = up_m[at].astype(f32) + tiles[i, BLK : 2 * BLK].astype(f32)

            @pl.when((cell >= 0) & (lead != s))
            def _():
                acc[lead] += tiles[i, 0 : 2 * BLK].astype(f32)

            return carry

        return step

    lax.fori_loop(0, n_task, gather_from(task_ref, 0), 0)
    lax.fori_loop(0, n_slots - n_task, gather_from(lang_ref, n_task), 0)

    def write_back(s, carry):
        cell = cells_ref[s]

        @pl.when((cell >= 0) & (leader_ref[s] == s))
        def _():
            at = spot(cell)
            gate_m[at] = acc[s, 0:BLK].astype(bf16)
            up_m[at] = acc[s, BLK:].astype(bf16)

        return carry

    lax.fori_loop(0, n_slots, write_back, 0)

    depth = 1024
    gate_pre[...] = jnp.zeros_like(gate_pre)
    up_pre[...] = jnp.zeros_like(up_pre)

    def forward(k, carry):
        ks = pl.ds(pl.multiple_of(k * depth, depth), depth)
        xk = x_ref[:, ks]
        gate_pre[...] += jnp.dot(xk, gate_m[ks, :], preferred_element_type=f32)
        up_pre[...] += jnp.dot(xk, up_m[ks, :], preferred_element_type=f32)
        return carry

    lax.fori_loop(0, x_ref.shape[1] // depth, forward, 0)

    g, u = gate_pre[...], up_pre[...]
    s = jax.nn.sigmoid(g)
    c = cot_ref[...].astype(f32)
    dg = (c * u * s * (1.0 + g * (1.0 - s))).astype(bf16)
    du = (c * g * s).astype(bf16)
    d_gate[...] = dg
    d_up[...] = du
    for h in range(2):
        d_cols[h, :, 0:BLK] = dg[:, h * BLK : (h + 1) * BLK]
        d_cols[h, :, BLK:] = du[:, h * BLK : (h + 1) * BLK]

    def task_step(i, carry):
        cell = jnp.maximum(cells_ref[i], 0)
        row = pl.multiple_of(lax.shift_right_logical(cell, 1) * BLK, BLK)
        half = lax.bitwise_and(cell, 1)
        r = jnp.dot(xt_ref[pl.ds(row, BLK), :], d_cols[half], preferred_element_type=f32)
        r = r.astype(bf16)
        tgrads_ref[0, i] = r[0 : BLK // 2, 0:BLK]
        tgrads_ref[1, i] = r[BLK // 2 :, 0:BLK]
        tgrads_ref[2, i] = r[0 : BLK // 2, BLK:]
        tgrads_ref[3, i] = r[BLK // 2 :, BLK:]
        return carry

    lax.fori_loop(0, n_task, task_step, 0)

    last = (((1,), (1,)), ((), ()))

    def backward(m, carry):
        rows = pl.ds(pl.multiple_of(m * 2 * BLK, 2 * BLK), 2 * BLK)
        r = lax.dot_general(d_gate[...], gate_m[rows, :], last, preferred_element_type=f32)
        r += lax.dot_general(d_up[...], up_m[rows, :], last, preferred_element_type=f32)
        r = r.astype(bf16)
        grads_ref[0, m] = r[:, 0:BLK]
        grads_ref[1, m] = r[:, BLK:]
        return carry

    lax.fori_loop(0, grads_ref.shape[1], backward, 0)


def core_step(info, cells, leader, x, xt, cot, task, lang, gates, ups):
    bf16, f32 = jnp.bfloat16, jnp.float32
    n_task, n_slots = task.shape[0], cells.shape[0]
    tokens, width = x.shape
    cols = cot.shape[1]
    smem = pl.BlockSpec(memory_space=pltpu.SMEM)
    vmem = pl.BlockSpec(memory_space=pltpu.VMEM)
    hbm = pl.BlockSpec(memory_space=pl.ANY)
    return pl.pallas_call(
        lambda *refs: core_kernel(n_task, *refs),
        out_shape=(
            jax.ShapeDtypeStruct((2, width // (2 * BLK), tokens, BLK), bf16),
            jax.ShapeDtypeStruct((4, n_task, BLK // 2, BLK), bf16),
        ),
        in_specs=[smem] * 3 + [vmem] * 5 + [hbm] * 8,
        out_specs=(vmem, vmem),
        scratch_shapes=[
            pltpu.VMEM((width, cols), bf16),
            pltpu.VMEM((width, cols), bf16),
            pltpu.VMEM((n_slots, 2 * BLK, BLK), f32),
            pltpu.VMEM((tokens, cols), f32),
            pltpu.VMEM((tokens, cols), f32),
            pltpu.VMEM((tokens, cols), bf16),
            pltpu.VMEM((tokens, cols), bf16),
            pltpu.VMEM((2, tokens, 2 * BLK), bf16),
            pltpu.SemaphoreType.DMA((8,)),
        ],
        compiler_params=pltpu.CompilerParams(vmem_limit_bytes=48 * MIB),
        cost_estimate=pl.CostEstimate(
            flops=10 * tokens * width * cols, bytes_accessed=24 * MIB, transcendentals=tokens * cols
        ),
        name="core_step",
    )(info, cells, leader, x, xt, cot, task, lang, *gates, *ups)


def on_device(
    tokens_in,
    cotangent,
    gate_base,
    up_base,
    lang_delta,
    lang_cell,
    group_lang,
    task_delta,
    task_slab,
    task_cell,
):
    f32, bf16 = jnp.float32, jnp.bfloat16
    fsdp = ("z", "core")
    n_lang, n_z, n_core, n_dp = (lax.axis_size(a) for a in ("lang", "z", "core", "dp"))
    n_fsdp = n_z * n_core
    language = group_lang[0]
    my_lang, my_core, my_dp = (lax.axis_index(a) for a in ("lang", "core", "dp"))
    held = task_delta.shape[0]

    gate_left = lax.ppermute(gate_base, "dp", ring("dp", 1))
    gate_right = lax.ppermute(gate_base, "dp", ring("dp", -1))
    up_left = lax.ppermute(up_base, "dp", ring("dp", 1))
    up_right = lax.ppermute(up_base, "dp", ring("dp", -1))
    gate_far = lax.ppermute(gate_left, "dp", ring("dp", 1))
    up_far = lax.ppermute(up_right, "dp", ring("dp", -1))

    target = task_slab[:, 0]
    place_in = jnp.arange(held, dtype=jnp.int32)
    same = (target[:, None] == target[None, :]) & (place_in[None, :] < place_in[:, None])
    slot_of = jnp.sum(same.astype(jnp.int32), axis=1)
    dest = target * CAP + slot_of
    send_task = place(dest, task_delta.reshape(held, 2 * BLK, BLK), task_cell[:, 0], n_fsdp * CAP)
    got_task = lax.all_to_all(send_task, fsdp, split_axis=0, concat_axis=0, tiled=True)
    task_cells = got_task[:, 2 * BLK, 0].astype(jnp.int32)

    lang_tiles = lang_delta[0, 0].reshape(lang_delta.shape[2:4] + (2 * BLK, BLK))
    send_lang = with_cells(lang_tiles, lang_cell[0, 0])
    pick = lax.rem(my_lang - language + n_lang, n_lang)
    chosen = None
    for k in range(n_lang):
        piece = lax.dynamic_index_in_dim(send_lang, lax.rem(my_lang + k, n_lang), 0, keepdims=False)
        if k:
            piece = lax.ppermute(piece, "lang", ring("lang", k))
        chosen = piece if chosen is None else jnp.where(pick == k, piece, chosen)
    lang_cells = chosen[:, 2 * BLK, 0].astype(jnp.int32)

    cells = jnp.concatenate([task_cells, lang_cells])
    n_slots = cells.shape[0]
    index = jnp.arange(n_slots, dtype=jnp.int32)
    leader = jnp.min(jnp.where(cells[:, None] == cells[None, :], index[None, :], n_slots), axis=1)

    grads, tgrads = core_step(
        my_dp[None].astype(jnp.int32),
        cells,
        leader,
        tokens_in,
        tokens_in.T,
        cotangent,
        got_task,
        chosen,
        (gate_base, gate_right, gate_far, gate_left),
        (up_base, up_right, up_far, up_left),
    )

    tsum = lax.all_to_all(tgrads, "dp", split_axis=0, concat_axis=0, tiled=True)
    tsum = jnp.sum(tsum.astype(f32), axis=0).astype(bf16)
    back = lax.all_to_all(tsum, fsdp, split_axis=0, concat_axis=0, tiled=True)
    slots = jnp.arange(n_fsdp * CAP, dtype=jnp.int32)
    one_hot = (dest[:, None] == slots[None, :]).astype(bf16)
    mine = jnp.einsum("is,srk->irk", one_hot, back, preferred_element_type=f32).astype(bf16)
    quarters = [mine] + [lax.ppermute(mine, "dp", ring("dp", -k)) for k in range(1, n_dp)]
    stacked = jnp.stack(quarters, axis=0)
    stacked = jnp.stack(
        [
            lax.dynamic_index_in_dim(stacked, lax.rem(q - my_dp + n_dp, n_dp), 0, keepdims=False)
            for q in range(n_dp)
        ],
        axis=1,
    )
    task_grad = stacked.astype(f32).reshape(task_delta.shape)

    keep = lax.dynamic_index_in_dim(grads, my_core, 0, keepdims=False)
    give = lax.dynamic_index_in_dim(grads, 1 - my_core, 0, keepdims=False)
    pair = keep.astype(f32) + lax.ppermute(give, "core", ring("core", 1)).astype(f32)
    pair = pair.astype(bf16).reshape(n_lang, n_z, *grads.shape[2:])
    over_lang = lax.all_to_all(pair, "lang", split_axis=0, concat_axis=0, tiled=True)
    over_lang = jnp.sum(over_lang.astype(f32), axis=0).astype(bf16)
    over_z = lax.all_to_all(over_lang, "z", split_axis=0, concat_axis=0, tiled=True)
    grad_input = jnp.sum(over_z.astype(f32), axis=0).astype(bf16)
    return (grad_input, task_grad)


def solution(mesh):
    lang, fsdp, dp = (mesh.shape[a] for a in ("lang", "fsdp", "dp"))
    fine = Mesh(mesh.devices.reshape(lang, fsdp // 2, 2, dp), ("lang", "z", "core", "dp"))
    cols = ("lang", "z", "core")
    return jax.shard_map(
        on_device,
        mesh=fine,
        in_specs=(
            P("dp", None),
            P("dp", cols),
            P("dp", cols),
            P("dp", cols),
            P("lang", ("z", "core"), None, None, None),
            P("lang", ("z", "core"), None, None),
            P("dp"),
            P(cols, None),
            P(cols, None),
            P(cols, None),
        ),
        out_specs=(P("dp", cols), P(cols, None)),
        check_vma=False,
    )
```

```python
import jax
import jax.numpy as jnp
from jax import lax
from jax.experimental import pallas as pl
from jax.experimental.pallas import tpu as pltpu
from jax.sharding import Mesh, PartitionSpec as P

BLK = 128
CAP = 2
PAD = 16
MIB = 1024 * 1024


def ring(axis, step):
    n = lax.axis_size(axis)
    return [(i, (i + step) % n) for i in range(n)]


def with_cells(tiles, cells):
    rows = jnp.broadcast_to(cells.astype(jnp.bfloat16)[..., None, None], cells.shape + (PAD, BLK))
    return jnp.concatenate([tiles, rows], axis=-2)


def place_kernel(slab_ref, cells_ref, tiles_ref, out_ref, used_ref):
    def clear(i, carry):
        out_ref[i, 2 * BLK :, :] = jnp.full((PAD, BLK), -1.0, jnp.bfloat16)
        return carry

    lax.fori_loop(0, out_ref.shape[0], clear, 0)

    def unused(i, carry):
        used_ref[i] = 0
        return carry

    lax.fori_loop(0, used_ref.shape[0], unused, 0)

    def put(i, carry):
        slab = slab_ref[i]
        slot = slab * CAP + used_ref[slab]
        used_ref[slab] += 1
        out_ref[slot, 0 : 2 * BLK, :] = tiles_ref[i]
        out_ref[slot, 2 * BLK :, :] = jnp.full(
            (PAD, BLK), cells_ref[i].astype(jnp.float32), jnp.float32
        ).astype(jnp.bfloat16)
        return carry

    lax.fori_loop(0, tiles_ref.shape[0], put, 0)


def place(slab, cells, tiles, n_slabs):
    smem = pl.BlockSpec(memory_space=pltpu.SMEM)
    vmem = pl.BlockSpec(memory_space=pltpu.VMEM)
    return pl.pallas_call(
        place_kernel,
        out_shape=jax.ShapeDtypeStruct((n_slabs * CAP, 2 * BLK + PAD, BLK), jnp.bfloat16),
        in_specs=[smem, smem, vmem],
        out_specs=vmem,
        scratch_shapes=[pltpu.SMEM((n_slabs,), jnp.int32)],
        compiler_params=pltpu.CompilerParams(vmem_limit_bytes=16 * MIB),
        cost_estimate=pl.CostEstimate(flops=0, bytes_accessed=3 * MIB, transcendentals=0),
        name="place",
    )(slab, cells, tiles)


def forward_kernel(
    n_task,
    info_ref,
    x_ref,
    xt_ref,
    cot_ref,
    task_ref,
    lang_ref,
    g0,
    g1,
    g2,
    g3,
    u0,
    u1,
    u2,
    u3,
    own_ref,
    up_first,
    up_second,
    down_first,
    down_second,
    dg_ref,
    du_ref,
    gate_out,
    up_out,
    gate_m,
    up_m,
    acc,
    gate_pre,
    up_pre,
    d_cols,
    cell_rows,
    cells_ref,
    first_ref,
    leader_ref,
    sems,
):
    f32, bf16 = jnp.float32, jnp.bfloat16
    ways = 4
    part = g0.shape[0]
    me = info_ref[0]
    gates, ups = (g0, g1, g2, g3), (u0, u1, u2, u3)
    copies = []
    for k in range(ways):
        to = pl.ds(pl.multiple_of(lax.rem(me + k, ways) * part, part), part)
        copies.append(pltpu.make_async_copy(gates[k], gate_m.at[to], sems.at[2 * k]))
        copies.append(pltpu.make_async_copy(ups[k], up_m.at[to], sems.at[2 * k + 1]))
    for c in copies:
        c.start()

    n_slots = acc.shape[0]
    for i in range(n_slots):
        tiles, j = (task_ref, i) if i < n_task else (lang_ref, i - n_task)
        row = tiles[j, 2 * BLK : 2 * BLK + PAD, :].astype(f32).astype(jnp.int32)
        cell_rows[i : i + 1, :] = row[0:1]
    cell_copy = pltpu.make_async_copy(cell_rows, cells_ref, sems.at[8])
    cell_copy.start()
    cell_copy.wait()

    def no_first(i, carry):
        first_ref[i] = -1
        return carry

    lax.fori_loop(0, first_ref.shape[0], no_first, 0)

    def find_leader(s, carry):
        cell = jnp.maximum(cells_ref[s, 0], 0)
        known = first_ref[cell]
        lead = jnp.where(known < 0, s, known)
        leader_ref[s] = lead

        @pl.when(cells_ref[s, 0] >= 0)
        def _():
            first_ref[cell] = lead

        return carry

    lax.fori_loop(0, n_slots, find_leader, 0)
    for c in copies:
        c.wait()

    def spot(cell):
        row = pl.multiple_of(lax.shift_right_logical(cell, 1) * BLK, BLK)
        col = pl.multiple_of(lax.bitwise_and(cell, 1) * BLK, BLK)
        return pl.ds(row, BLK), pl.ds(col, BLK)

    def gather_from(tiles, first):
        def step(i, carry):
            s = i + first
            cell = cells_ref[s, 0]
            lead = leader_ref[s]

            @pl.when((cell >= 0) & (lead == s))
            def _():
                at = spot(cell)
                acc[s, 0:BLK] = gate_m[at].astype(f32) + tiles[i, 0:BLK].astype(f32)
                acc[s, BLK:] = up_m[at].astype(f32) + tiles[i, BLK : 2 * BLK].astype(f32)

            @pl.when((cell >= 0) & (lead != s))
            def _():
                acc[lead] += tiles[i, 0 : 2 * BLK].astype(f32)

            return carry

        return step

    lax.fori_loop(0, n_task, gather_from(task_ref, 0), 0)
    lax.fori_loop(0, n_slots - n_task, gather_from(lang_ref, n_task), 0)

    def write_back(s, carry):
        cell = cells_ref[s, 0]

        @pl.when((cell >= 0) & (leader_ref[s] == s))
        def _():
            at = spot(cell)
            gate_m[at] = acc[s, 0:BLK].astype(bf16)
            up_m[at] = acc[s, BLK:].astype(bf16)

        return carry

    lax.fori_loop(0, n_slots, write_back, 0)

    out_copies = (
        pltpu.make_async_copy(gate_m, gate_out, sems.at[0]),
        pltpu.make_async_copy(up_m, up_out, sems.at[1]),
    )
    for c in out_copies:
        c.start()

    depth = 1024
    gate_pre[...] = jnp.zeros_like(gate_pre)
    up_pre[...] = jnp.zeros_like(up_pre)

    def forward(k, carry):
        ks = pl.ds(pl.multiple_of(k * depth, depth), depth)
        xk = x_ref[:, ks]
        gate_pre[...] += jnp.dot(xk, gate_m[ks, :], preferred_element_type=f32)
        up_pre[...] += jnp.dot(xk, up_m[ks, :], preferred_element_type=f32)
        return carry

    lax.fori_loop(0, x_ref.shape[1] // depth, forward, 0)

    g, u = gate_pre[...], up_pre[...]
    s = jax.nn.sigmoid(g)
    c = cot_ref[...].astype(f32)
    dg = (c * u * s * (1.0 + g * (1.0 - s))).astype(bf16)
    du = (c * g * s).astype(bf16)
    dg_ref[...] = dg
    du_ref[...] = du
    for h in range(2):
        d_cols[h, :, 0:BLK] = dg[:, h * BLK : (h + 1) * BLK]
        d_cols[h, :, BLK:] = du[:, h * BLK : (h + 1) * BLK]

    def task_step(i, carry):
        cell = jnp.maximum(cells_ref[i, 0], 0)
        row = pl.multiple_of(lax.shift_right_logical(cell, 1) * BLK, BLK)
        side = lax.bitwise_and(cell, 1)
        r = jnp.dot(xt_ref[pl.ds(row, BLK), :], d_cols[side], preferred_element_type=f32)
        r = r.astype(bf16)
        low, high = r[0 : BLK // 2], r[BLK // 2 :]
        quarters = (low[:, 0:BLK], high[:, 0:BLK], low[:, BLK:], high[:, BLK:])

        def quarter(k):
            q = lax.rem(me + k, ways)
            even = jnp.where(q == 0, quarters[0], quarters[2])
            odd = jnp.where(q == 1, quarters[1], quarters[3])
            return jnp.where(lax.bitwise_and(q, 1) == 0, even, odd)

        own_ref[i] = quarter(0)
        half = n_task // 2

        @pl.when(i < half)
        def _():
            up_second[i] = quarter(1)
            up_first[i] = quarter(2)
            down_first[i] = quarter(3)

        @pl.when(i >= half)
        def _():
            up_first[i] = quarter(1)
            down_first[i] = quarter(2)
            down_second[i - half] = quarter(3)

        return carry

    lax.fori_loop(0, n_task, task_step, 0)
    for c in out_copies:
        c.wait()


def forward_step(info, x, xt, cot, task, lang, gates, ups):
    bf16, f32 = jnp.bfloat16, jnp.float32
    n_task, n_slots = task.shape[0], task.shape[0] + lang.shape[0]
    tokens, width = x.shape
    cols = cot.shape[1]
    smem = pl.BlockSpec(memory_space=pltpu.SMEM)
    vmem = pl.BlockSpec(memory_space=pltpu.VMEM)
    hbm = pl.BlockSpec(memory_space=pl.ANY)
    return pl.pallas_call(
        lambda *refs: forward_kernel(n_task, *refs),
        out_shape=(
            jax.ShapeDtypeStruct((n_task, BLK // 2, BLK), bf16),
            *[
                jax.ShapeDtypeStruct((n, BLK // 2, BLK), bf16)
                for n in (n_task, n_task // 2, n_task, n_task // 2)
            ],
            *[jax.ShapeDtypeStruct((tokens, cols), bf16)] * 2,
            *[jax.ShapeDtypeStruct((width, cols), bf16)] * 2,
        ),
        in_specs=[smem] + [vmem] * 5 + [hbm] * 8,
        out_specs=(*[vmem] * 7, hbm, hbm),
        scratch_shapes=[
            pltpu.VMEM((width, cols), bf16),
            pltpu.VMEM((width, cols), bf16),
            pltpu.VMEM((n_slots, 2 * BLK, BLK), f32),
            pltpu.VMEM((tokens, cols), f32),
            pltpu.VMEM((tokens, cols), f32),
            pltpu.VMEM((2, tokens, 2 * BLK), bf16),
            pltpu.VMEM((-(-n_slots // 8) * 8, BLK), jnp.int32),
            pltpu.SMEM((-(-n_slots // 8) * 8, BLK), jnp.int32),
            pltpu.SMEM((width // BLK * cols // BLK,), jnp.int32),
            pltpu.SMEM((n_slots,), jnp.int32),
            pltpu.SemaphoreType.DMA((9,)),
        ],
        compiler_params=pltpu.CompilerParams(vmem_limit_bytes=40 * MIB),
        cost_estimate=pl.CostEstimate(
            flops=6 * tokens * width * cols, bytes_accessed=24 * MIB, transcendentals=tokens * cols
        ),
        name="forward_step",
    )(info, x, xt, cot, task, lang, *gates, *ups)


def backward_kernel(info_ref, dg_ref, du_ref, gate_ref, up_ref, keep_ref, give_ref):
    last = (((1,), (1,)), ((), ()))
    f32, bf16 = jnp.float32, jnp.bfloat16
    first_core = info_ref[0] == 0
    for m in range(keep_ref.shape[0]):
        rows = pl.ds(m * 2 * BLK, 2 * BLK)
        r = lax.dot_general(dg_ref[...], gate_ref[rows, :], last, preferred_element_type=f32)
        r += lax.dot_general(du_ref[...], up_ref[rows, :], last, preferred_element_type=f32)
        r = r.astype(bf16)
        low, high = r[:, 0:BLK], r[:, BLK:]
        keep_ref[m] = jnp.where(first_core, low, high)
        give_ref[m] = jnp.where(first_core, high, low)


def backward_step(info, dg, du, gate, up):
    bf16 = jnp.bfloat16
    width, cols = gate.shape
    tokens = dg.shape[0]
    steps, n_lang = 8, 4
    per = steps // n_lang
    pairs = width // (2 * BLK)
    out = jax.ShapeDtypeStruct((pairs, tokens, BLK), bf16)
    out_block = pl.BlockSpec((pairs // steps, tokens, BLK), lambda i, info: (i, 0, 0))
    whole = pl.BlockSpec((tokens, cols), lambda i, info: (0, 0))
    rows = pl.BlockSpec(
        (width // steps, cols), lambda i, info: (lax.rem(i + info[1] * per, steps), 0)
    )
    return pl.pallas_call(
        backward_kernel,
        grid_spec=pltpu.PrefetchScalarGridSpec(
            num_scalar_prefetch=1,
            grid=(steps,),
            in_specs=[whole, whole, rows, rows],
            out_specs=(out_block, out_block),
        ),
        out_shape=(out, out),
        compiler_params=pltpu.CompilerParams(vmem_limit_bytes=24 * MIB),
        cost_estimate=pl.CostEstimate(
            flops=4 * tokens * width * cols, bytes_accessed=12 * MIB, transcendentals=0
        ),
        name="backward_step",
    )(info, dg, du, gate, up)


def ring_first(axis, up_first, down_first):
    return (
        lax.ppermute(up_first, axis, ring(axis, 1)),
        lax.ppermute(down_first, axis, ring(axis, -1)),
    )


def ring_rest(axis, own, up_second, down_second, from_left, from_right):
    f32, bf16 = jnp.float32, jnp.bfloat16
    half = own.shape[0] // 2
    up_second = (up_second.astype(f32) + from_left[:half].astype(f32)).astype(bf16)
    down_second = (down_second.astype(f32) + from_right[half:].astype(f32)).astype(bf16)
    low_left = lax.ppermute(up_second, axis, ring(axis, 1))
    high_right = lax.ppermute(down_second, axis, ring(axis, -1))
    low = own[:half].astype(f32) + low_left.astype(f32) + from_right[:half].astype(f32)
    high = own[half:].astype(f32) + high_right.astype(f32) + from_left[half:].astype(f32)
    return jnp.concatenate([low, high], axis=0).astype(bf16)


def on_device(
    tokens_in,
    cotangent,
    gate_base,
    up_base,
    lang_delta,
    lang_cell,
    group_lang,
    task_delta,
    task_slab,
    task_cell,
):
    f32, bf16 = jnp.float32, jnp.bfloat16
    fsdp = ("z", "core")
    n_lang, n_z, n_core, n_dp = (lax.axis_size(a) for a in ("lang", "z", "core", "dp"))
    n_fsdp = n_z * n_core
    language = group_lang[0]
    my_lang, my_core, my_dp = (lax.axis_index(a) for a in ("lang", "core", "dp"))
    held = task_delta.shape[0]

    gate_left = lax.ppermute(gate_base, "dp", ring("dp", 1))
    gate_right = lax.ppermute(gate_base, "dp", ring("dp", -1))
    up_left = lax.ppermute(up_base, "dp", ring("dp", 1))
    up_right = lax.ppermute(up_base, "dp", ring("dp", -1))
    gate_far = lax.ppermute(gate_left, "dp", ring("dp", 1))
    up_far = lax.ppermute(up_right, "dp", ring("dp", -1))

    target = task_slab[:, 0]
    send_task = place(target, task_cell[:, 0], task_delta.reshape(held, 2 * BLK, BLK), n_fsdp)
    got_task = lax.all_to_all(send_task, fsdp, split_axis=0, concat_axis=0, tiled=True)
    lang_tiles = lang_delta[0, 0].reshape(lang_delta.shape[2:4] + (2 * BLK, BLK))
    send_lang = with_cells(lang_tiles, lang_cell[0, 0])
    pick = lax.rem(my_lang - language + n_lang, n_lang)
    chosen = None
    for k in range(n_lang):
        piece = lax.dynamic_index_in_dim(send_lang, lax.rem(my_lang + k, n_lang), 0, keepdims=False)
        if k:
            piece = lax.ppermute(piece, "lang", ring("lang", k))
        chosen = piece if chosen is None else jnp.where(pick == k, piece, chosen)

    *pieces, d_gate, d_up, gate_matrix, up_matrix = forward_step(
        my_dp[None].astype(jnp.int32),
        tokens_in,
        tokens_in.T,
        cotangent,
        got_task,
        chosen,
        (gate_base, gate_right, gate_far, gate_left),
        (up_base, up_right, up_far, up_left),
    )
    task_first = ring_first("dp", pieces[1], pieces[3])
    keep, give = backward_step(
        jnp.stack([my_core, my_lang]).astype(jnp.int32), d_gate, d_up, gate_matrix, up_matrix
    )
    got = lax.ppermute(give, "core", ring("core", 1))
    tsum = ring_rest("dp", pieces[0], pieces[2], pieces[4], *task_first)

    def both(first, last):
        first, last = first * n_z // 2, last * n_z // 2
        return (keep[first:last].astype(f32) + got[first:last].astype(f32)).astype(bf16)

    up_first = jnp.concatenate([both(4, 5), both(3, 4)], axis=0)
    down_first = jnp.concatenate([both(6, 7), both(5, 6)], axis=0)
    main_first = ring_first("lang", up_first, down_first)
    tsum, _, _ = lax.optimization_barrier((tsum, up_first, down_first))
    back = lax.all_to_all(tsum, fsdp, split_axis=0, concat_axis=0, tiled=True)
    over_lang = ring_rest("lang", both(0, 2), both(2, 3), both(7, 8), *main_first)
    back, _, _ = lax.optimization_barrier((back, *main_first))
    place_in = jnp.arange(held, dtype=jnp.int32)
    same = (target[:, None] == target[None, :]) & (place_in[None, :] < place_in[:, None])
    dest = target * CAP + jnp.sum(same.astype(jnp.int32), axis=1)
    slots = jnp.arange(n_fsdp * CAP, dtype=jnp.int32)
    one_hot = (dest[:, None] == slots[None, :]).astype(bf16)
    mine = jnp.einsum("is,srk->irk", one_hot, back, preferred_element_type=f32).astype(bf16)
    from_right = lax.ppermute(mine, "dp", ring("dp", -1))
    from_left = lax.ppermute(mine, "dp", ring("dp", 1))
    mid = held // 2
    far_low = lax.ppermute(from_left[:mid], "dp", ring("dp", 1))
    far_high = lax.ppermute(from_right[mid:], "dp", ring("dp", -1))
    from_far = jnp.concatenate([far_low, far_high], axis=0)
    stacked = jnp.stack([mine, from_right, from_far, from_left], axis=0)
    stacked = jnp.stack(
        [
            lax.dynamic_index_in_dim(stacked, lax.rem(q - my_dp + n_dp, n_dp), 0, keepdims=False)
            for q in range(n_dp)
        ],
        axis=1,
    )
    task_grad = stacked.astype(f32).reshape(task_delta.shape)

    my_z = lax.axis_index("z")
    total = lax.dynamic_index_in_dim(over_lang, my_z, 0, keepdims=False).astype(f32)
    for k in (4, 1, 7, 2, 6, 3, 5):
        piece = lax.dynamic_index_in_dim(over_lang, lax.rem(my_z + k, n_z), 0, keepdims=False)
        total += lax.ppermute(piece, "z", ring("z", k)).astype(f32)
    grad_input = total.astype(bf16)
    return (grad_input, task_grad)


def solution(mesh):
    lang, fsdp, dp = (mesh.shape[a] for a in ("lang", "fsdp", "dp"))
    fine = Mesh(mesh.devices.reshape(lang, fsdp // 2, 2, dp), ("lang", "z", "core", "dp"))
    cols = ("lang", "z", "core")
    return jax.shard_map(
        on_device,
        mesh=fine,
        in_specs=(
            P("dp", None),
            P("dp", cols),
            P("dp", cols),
            P("dp", cols),
            P("lang", ("z", "core"), None, None, None),
            P("lang", ("z", "core"), None, None),
            P("dp"),
            P(cols, None),
            P(cols, None),
            P(cols, None),
        ),
        out_specs=(P("dp", cols), P(cols, None)),
        check_vma=False,
    )
```

```python
import jax
import jax.numpy as jnp
from jax import lax
from jax.experimental import pallas as pl
from jax.experimental.pallas import tpu as pltpu
from jax.sharding import Mesh, PartitionSpec as P

BLK = 128
CAP = 2
PAD = 16
MIB = 1024 * 1024


def ring(axis, step):
    n = lax.axis_size(axis)
    return [(i, (i + step) % n) for i in range(n)]


def with_cells(tiles, cells):
    rows = jnp.broadcast_to(cells.astype(jnp.bfloat16)[..., None, None], cells.shape + (PAD, BLK))
    return jnp.concatenate([tiles, rows], axis=-2)


def place_kernel(slab_ref, cells_ref, tiles_ref, out_ref, used_ref):
    def clear(i, carry):
        out_ref[i, 2 * BLK :, :] = jnp.full((PAD, BLK), -1.0, jnp.bfloat16)
        return carry

    lax.fori_loop(0, out_ref.shape[0], clear, 0)

    def unused(i, carry):
        used_ref[i] = 0
        return carry

    lax.fori_loop(0, used_ref.shape[0], unused, 0)

    def put(i, carry):
        slab = slab_ref[i]
        slot = slab * CAP + used_ref[slab]
        used_ref[slab] += 1
        out_ref[slot, 0 : 2 * BLK, :] = tiles_ref[i]
        out_ref[slot, 2 * BLK :, :] = jnp.full(
            (PAD, BLK), cells_ref[i].astype(jnp.float32), jnp.float32
        ).astype(jnp.bfloat16)
        return carry

    lax.fori_loop(0, tiles_ref.shape[0], put, 0)


def place(slab, cells, tiles, n_slabs):
    smem = pl.BlockSpec(memory_space=pltpu.SMEM)
    vmem = pl.BlockSpec(memory_space=pltpu.VMEM)
    return pl.pallas_call(
        place_kernel,
        out_shape=jax.ShapeDtypeStruct((n_slabs * CAP, 2 * BLK + PAD, BLK), jnp.bfloat16),
        in_specs=[smem, smem, vmem],
        out_specs=vmem,
        scratch_shapes=[pltpu.SMEM((n_slabs,), jnp.int32)],
        compiler_params=pltpu.CompilerParams(vmem_limit_bytes=16 * MIB),
        cost_estimate=pl.CostEstimate(flops=0, bytes_accessed=3 * MIB, transcendentals=0),
        name="place",
    )(slab, cells, tiles)


def device_kernel(
    n_task,
    info_ref,
    cot_ref,
    task_ref,
    lang_ref,
    x_hbm,
    xt_hbm,
    gate_hbm,
    up_own,
    up_right,
    up_left,
    far_low,
    far_high,
    own_ref,
    up_first,
    up_second,
    down_first,
    down_second,
    keep_ref,
    give_ref,
    x_ref,
    xt_ref,
    gate_m,
    up_m,
    acc,
    gate_pre,
    up_pre,
    d_gate,
    d_up,
    d_cols,
    cell_rows,
    cells_ref,
    first_ref,
    leader_ref,
    sems,
):
    f32, bf16 = jnp.float32, jnp.bfloat16
    ways = 4
    part, half_part = up_own.shape[0], far_low.shape[0]
    me, core, lang = info_ref[0], info_ref[1], info_ref[2]

    def rows_of(k, skip, size):
        return pl.ds(pl.multiple_of(lax.rem(me + k, ways) * part + skip, size), size)

    copies = [
        pltpu.make_async_copy(gate_hbm, gate_m, sems.at[0]),
        pltpu.make_async_copy(up_own, up_m.at[rows_of(0, 0, part)], sems.at[1]),
        pltpu.make_async_copy(up_right, up_m.at[rows_of(1, 0, part)], sems.at[2]),
        pltpu.make_async_copy(up_left, up_m.at[rows_of(3, 0, part)], sems.at[3]),
        pltpu.make_async_copy(far_low, up_m.at[rows_of(2, 0, half_part)], sems.at[4]),
        pltpu.make_async_copy(far_high, up_m.at[rows_of(2, half_part, half_part)], sems.at[5]),
    ]
    x_copy = pltpu.make_async_copy(x_hbm, x_ref, sems.at[6])
    xt_copy = pltpu.make_async_copy(xt_hbm, xt_ref, sems.at[7])
    for c in (*copies, x_copy, xt_copy):
        c.start()

    n_slots = acc.shape[0]
    for i in range(n_slots):
        tiles, j = (task_ref, i) if i < n_task else (lang_ref, i - n_task)
        row = tiles[j, 2 * BLK : 2 * BLK + PAD, :].astype(f32).astype(jnp.int32)
        cell_rows[i : i + 1, :] = row[0:1]
    cell_copy = pltpu.make_async_copy(cell_rows, cells_ref, sems.at[8])
    cell_copy.start()
    cell_copy.wait()

    def no_first(i, carry):
        first_ref[i] = -1
        return carry

    lax.fori_loop(0, first_ref.shape[0], no_first, 0)

    def find_leader(s, carry):
        cell = jnp.maximum(cells_ref[s, 0], 0)
        known = first_ref[cell]
        lead = jnp.where(known < 0, s, known)
        leader_ref[s] = lead

        @pl.when(cells_ref[s, 0] >= 0)
        def _():
            first_ref[cell] = lead

        return carry

    lax.fori_loop(0, n_slots, find_leader, 0)
    for c in copies:
        c.wait()

    def spot(cell):
        row = pl.multiple_of(lax.shift_right_logical(cell, 1) * BLK, BLK)
        col = pl.multiple_of(lax.bitwise_and(cell, 1) * BLK, BLK)
        return pl.ds(row, BLK), pl.ds(col, BLK)

    def gather_from(tiles, first):
        def step(i, carry):
            s = i + first
            cell = cells_ref[s, 0]
            lead = leader_ref[s]

            @pl.when((cell >= 0) & (lead == s))
            def _():
                at = spot(cell)
                acc[s, 0:BLK] = gate_m[at].astype(f32) + tiles[i, 0:BLK].astype(f32)
                acc[s, BLK:] = up_m[at].astype(f32) + tiles[i, BLK : 2 * BLK].astype(f32)

            @pl.when((cell >= 0) & (lead != s))
            def _():
                acc[lead] += tiles[i, 0 : 2 * BLK].astype(f32)

            return carry

        return step

    lax.fori_loop(0, n_task, gather_from(task_ref, 0), 0)
    lax.fori_loop(0, n_slots - n_task, gather_from(lang_ref, n_task), 0)

    def write_back(s, carry):
        cell = cells_ref[s, 0]

        @pl.when((cell >= 0) & (leader_ref[s] == s))
        def _():
            at = spot(cell)
            gate_m[at] = acc[s, 0:BLK].astype(bf16)
            up_m[at] = acc[s, BLK:].astype(bf16)

        return carry

    lax.fori_loop(0, n_slots, write_back, 0)

    depth = 1024
    gate_pre[...] = jnp.zeros_like(gate_pre)
    up_pre[...] = jnp.zeros_like(up_pre)

    def forward(k, carry):
        ks = pl.ds(pl.multiple_of(k * depth, depth), depth)
        xk = x_ref[:, ks]
        gate_pre[...] += jnp.dot(xk, gate_m[ks, :], preferred_element_type=f32)
        up_pre[...] += jnp.dot(xk, up_m[ks, :], preferred_element_type=f32)
        return carry

    x_copy.wait()
    lax.fori_loop(0, x_ref.shape[1] // depth, forward, 0)

    g, u = gate_pre[...], up_pre[...]
    s = jax.nn.sigmoid(g)
    c = cot_ref[...].astype(f32)
    dg = (c * u * s * (1.0 + g * (1.0 - s))).astype(bf16)
    du = (c * g * s).astype(bf16)
    d_gate[...] = dg
    d_up[...] = du
    for h in range(2):
        d_cols[h, :, 0:BLK] = dg[:, h * BLK : (h + 1) * BLK]
        d_cols[h, :, BLK:] = du[:, h * BLK : (h + 1) * BLK]

    def task_step(i, carry):
        cell = jnp.maximum(cells_ref[i, 0], 0)
        row = pl.multiple_of(lax.shift_right_logical(cell, 1) * BLK, BLK)
        side = lax.bitwise_and(cell, 1)
        r = jnp.dot(xt_ref[pl.ds(row, BLK), :], d_cols[side], preferred_element_type=f32)
        r = r.astype(bf16)
        low, high = r[0 : BLK // 2], r[BLK // 2 :]
        quarters = (low[:, 0:BLK], high[:, 0:BLK], low[:, BLK:], high[:, BLK:])

        def quarter(k):
            q = lax.rem(me + k, ways)
            even = jnp.where(q == 0, quarters[0], quarters[2])
            odd = jnp.where(q == 1, quarters[1], quarters[3])
            return jnp.where(lax.bitwise_and(q, 1) == 0, even, odd)

        own_ref[i] = quarter(0)
        half = n_task // 2

        @pl.when(i < half)
        def _():
            up_second[i] = quarter(1)
            up_first[i] = quarter(2)
            down_first[i] = quarter(3)

        @pl.when(i >= half)
        def _():
            up_first[i] = quarter(1)
            down_first[i] = quarter(2)
            down_second[i - half] = quarter(3)

        return carry

    xt_copy.wait()
    lax.fori_loop(0, n_task, task_step, 0)

    last = (((1,), (1,)), ((), ()))
    per = keep_ref.shape[0] // ways

    def backward(m, carry):
        at = lax.rem(m + lang * per, keep_ref.shape[0])
        rows = pl.ds(pl.multiple_of(at * 2 * BLK, 2 * BLK), 2 * BLK)
        r = lax.dot_general(d_gate[...], gate_m[rows, :], last, preferred_element_type=f32)
        r += lax.dot_general(d_up[...], up_m[rows, :], last, preferred_element_type=f32)
        r = r.astype(bf16)
        low, high = r[:, 0:BLK], r[:, BLK:]
        keep_ref[m] = jnp.where(core == 0, low, high)
        give_ref[m] = jnp.where(core == 0, high, low)
        return carry

    lax.fori_loop(0, keep_ref.shape[0], backward, 0)


def device_step(info, cot, task, lang, x, xt, gate, ups):
    bf16, f32 = jnp.bfloat16, jnp.float32
    n_task, n_slots = task.shape[0], task.shape[0] + lang.shape[0]
    tokens, width = x.shape
    cols = cot.shape[1]
    padded = -(-n_slots // 8) * 8
    vmem = pl.BlockSpec(memory_space=pltpu.VMEM)
    hbm = pl.BlockSpec(memory_space=pl.ANY)
    main = jax.ShapeDtypeStruct((width // (2 * BLK), tokens, BLK), bf16)
    return pl.pallas_call(
        lambda *refs: device_kernel(n_task, *refs),
        out_shape=(
            *[
                jax.ShapeDtypeStruct((n, BLK // 2, BLK), bf16)
                for n in (n_task, n_task, n_task // 2, n_task, n_task // 2)
            ],
            main,
            main,
        ),
        in_specs=[pl.BlockSpec(memory_space=pltpu.SMEM)] + [vmem] * 3 + [hbm] * 8,
        out_specs=[vmem] * 7,
        scratch_shapes=[
            pltpu.VMEM(x.shape, bf16),
            pltpu.VMEM(xt.shape, bf16),
            pltpu.VMEM((width, cols), bf16),
            pltpu.VMEM((width, cols), bf16),
            pltpu.VMEM((n_slots, 2 * BLK, BLK), f32),
            pltpu.VMEM((tokens, cols), f32),
            pltpu.VMEM((tokens, cols), f32),
            pltpu.VMEM((tokens, cols), bf16),
            pltpu.VMEM((tokens, cols), bf16),
            pltpu.VMEM((2, tokens, 2 * BLK), bf16),
            pltpu.VMEM((padded, BLK), jnp.int32),
            pltpu.SMEM((padded, BLK), jnp.int32),
            pltpu.SMEM((width // BLK * cols // BLK,), jnp.int32),
            pltpu.SMEM((n_slots,), jnp.int32),
            pltpu.SemaphoreType.DMA((9,)),
        ],
        compiler_params=pltpu.CompilerParams(vmem_limit_bytes=44 * MIB),
        cost_estimate=pl.CostEstimate(
            flops=10 * tokens * width * cols, bytes_accessed=24 * MIB, transcendentals=tokens * cols
        ),
        name="device_step",
    )(info, cot, task, lang, x, xt, gate, *ups)


def ring_first(axis, up_first, down_first):
    return (
        lax.ppermute(up_first, axis, ring(axis, 1)),
        lax.ppermute(down_first, axis, ring(axis, -1)),
    )


def ring_rest(axis, own, up_second, down_second, from_left, from_right):
    f32, bf16 = jnp.float32, jnp.bfloat16
    half = own.shape[0] // 2
    up_second = (up_second.astype(f32) + from_left[:half].astype(f32)).astype(bf16)
    down_second = (down_second.astype(f32) + from_right[half:].astype(f32)).astype(bf16)
    low_left = lax.ppermute(up_second, axis, ring(axis, 1))
    high_right = lax.ppermute(down_second, axis, ring(axis, -1))
    low = own[:half].astype(f32) + low_left.astype(f32) + from_right[:half].astype(f32)
    high = own[half:].astype(f32) + high_right.astype(f32) + from_left[half:].astype(f32)
    return jnp.concatenate([low, high], axis=0).astype(bf16)


def on_device(
    tokens_in,
    cotangent,
    gate_base,
    up_base,
    lang_delta,
    lang_cell,
    group_lang,
    task_delta,
    task_slab,
    task_cell,
):
    f32, bf16 = jnp.float32, jnp.bfloat16
    fsdp = ("z", "core")
    n_lang, n_z, n_core, n_dp = (lax.axis_size(a) for a in ("lang", "z", "core", "dp"))
    n_fsdp = n_z * n_core
    language = group_lang[0]
    my_lang, my_core, my_dp = (lax.axis_index(a) for a in ("lang", "core", "dp"))
    held = task_delta.shape[0]

    gate = lax.all_gather(gate_base, "dp", axis=0, tiled=True)
    up_left = lax.ppermute(up_base, "dp", ring("dp", 1))
    up_right = lax.ppermute(up_base, "dp", ring("dp", -1))
    mid = up_base.shape[0] // 2
    far_low = lax.ppermute(up_left[:mid], "dp", ring("dp", 1))
    far_high = lax.ppermute(up_right[mid:], "dp", ring("dp", -1))

    target = task_slab[:, 0]
    send_task = place(target, task_cell[:, 0], task_delta.reshape(held, 2 * BLK, BLK), n_fsdp)
    got_task = lax.all_to_all(send_task, fsdp, split_axis=0, concat_axis=0, tiled=True)
    lang_tiles = lang_delta[0, 0].reshape(lang_delta.shape[2:4] + (2 * BLK, BLK))
    send_lang = with_cells(lang_tiles, lang_cell[0, 0])
    pick = lax.rem(my_lang - language + n_lang, n_lang)
    chosen = None
    for k in range(n_lang):
        piece = lax.dynamic_index_in_dim(send_lang, lax.rem(my_lang + k, n_lang), 0, keepdims=False)
        if k:
            piece = lax.ppermute(piece, "lang", ring("lang", k))
        chosen = piece if chosen is None else jnp.where(pick == k, piece, chosen)

    *pieces, keep, give = device_step(
        jnp.stack([my_dp, my_core, my_lang]).astype(jnp.int32),
        cotangent,
        got_task,
        chosen,
        tokens_in,
        tokens_in.T,
        gate,
        (up_base, up_right, up_left, far_low, far_high),
    )
    got = lax.ppermute(give, "core", ring("core", 1))
    task_first = ring_first("dp", pieces[1], pieces[3])

    def both(first, last):
        first, last = first * n_z // 2, last * n_z // 2
        return (keep[first:last].astype(f32) + got[first:last].astype(f32)).astype(bf16)

    up_first = jnp.concatenate([both(4, 5), both(3, 4)], axis=0)
    down_first = jnp.concatenate([both(6, 7), both(5, 6)], axis=0)
    main_first = ring_first("lang", up_first, down_first)
    task_left, task_right, _, _ = lax.optimization_barrier((*task_first, up_first, down_first))
    tsum = ring_rest("dp", pieces[0], pieces[2], pieces[4], task_left, task_right)
    tsum, _, _ = lax.optimization_barrier((tsum, *main_first))
    back = lax.all_to_all(tsum, fsdp, split_axis=0, concat_axis=0, tiled=True)
    over_lang = ring_rest("lang", both(0, 2), both(2, 3), both(7, 8), *main_first)
    back, _ = lax.optimization_barrier((back, over_lang))
    place_in = jnp.arange(held, dtype=jnp.int32)
    same = (target[:, None] == target[None, :]) & (place_in[None, :] < place_in[:, None])
    dest = target * CAP + jnp.sum(same.astype(jnp.int32), axis=1)
    slots = jnp.arange(n_fsdp * CAP, dtype=jnp.int32)
    one_hot = (dest[:, None] == slots[None, :]).astype(bf16)
    mine = jnp.einsum("is,srk->irk", one_hot, back, preferred_element_type=f32).astype(bf16)
    from_right = lax.ppermute(mine, "dp", ring("dp", -1))
    from_left = lax.ppermute(mine, "dp", ring("dp", 1))
    mid = held // 2
    far_low = lax.ppermute(from_left[:mid], "dp", ring("dp", 1))
    far_high = lax.ppermute(from_right[mid:], "dp", ring("dp", -1))
    from_far = jnp.concatenate([far_low, far_high], axis=0)
    stacked = jnp.stack([mine, from_right, from_far, from_left], axis=0)
    stacked = jnp.stack(
        [
            lax.dynamic_index_in_dim(stacked, lax.rem(q - my_dp + n_dp, n_dp), 0, keepdims=False)
            for q in range(n_dp)
        ],
        axis=1,
    )
    task_grad = stacked.astype(f32).reshape(task_delta.shape)

    over_z = lax.all_to_all(over_lang, "z", split_axis=0, concat_axis=0, tiled=True)
    grad_input = jnp.sum(over_z.astype(f32), axis=0).astype(bf16)
    return (grad_input, task_grad)


def solution(mesh):
    lang, fsdp, dp = (mesh.shape[a] for a in ("lang", "fsdp", "dp"))
    fine = Mesh(mesh.devices.reshape(lang, fsdp // 2, 2, dp), ("lang", "z", "core", "dp"))
    cols = ("lang", "z", "core")
    return jax.shard_map(
        on_device,
        mesh=fine,
        in_specs=(
            P("dp", None),
            P("dp", cols),
            P("dp", cols),
            P("dp", cols),
            P("lang", ("z", "core"), None, None, None),
            P("lang", ("z", "core"), None, None),
            P("dp"),
            P(cols, None),
            P(cols, None),
            P(cols, None),
        ),
        out_specs=(P("dp", cols), P(cols, None)),
        check_vma=False,
    )
```

```python
import jax
import jax.numpy as jnp
from jax import lax
from jax.experimental import pallas as pl
from jax.experimental.pallas import tpu as pltpu
from jax.sharding import Mesh, PartitionSpec as P

BLK = 128
CAP = 2
PAD = 16
MIB = 1024 * 1024


def ring(axis, step):
    n = lax.axis_size(axis)
    return [(i, (i + step) % n) for i in range(n)]


def with_cells(tiles, cells):
    rows = jnp.broadcast_to(cells.astype(jnp.bfloat16)[..., None, None], cells.shape + (PAD, BLK))
    return jnp.concatenate([tiles, rows], axis=-2)


def place_kernel(slab_ref, cells_ref, tiles_ref, out_ref, used_ref):
    def clear(i, carry):
        out_ref[i, 2 * BLK :, :] = jnp.full((PAD, BLK), -1.0, jnp.bfloat16)
        return carry

    lax.fori_loop(0, out_ref.shape[0], clear, 0)

    def unused(i, carry):
        used_ref[i] = 0
        return carry

    lax.fori_loop(0, used_ref.shape[0], unused, 0)

    def put(i, carry):
        slab = slab_ref[i]
        slot = slab * CAP + used_ref[slab]
        used_ref[slab] += 1
        out_ref[slot, 0 : 2 * BLK, :] = tiles_ref[i]
        out_ref[slot, 2 * BLK :, :] = jnp.full(
            (PAD, BLK), cells_ref[i].astype(jnp.float32), jnp.float32
        ).astype(jnp.bfloat16)
        return carry

    lax.fori_loop(0, tiles_ref.shape[0], put, 0)


def place(slab, cells, tiles, n_slabs):
    smem = pl.BlockSpec(memory_space=pltpu.SMEM)
    vmem = pl.BlockSpec(memory_space=pltpu.VMEM)
    return pl.pallas_call(
        place_kernel,
        out_shape=jax.ShapeDtypeStruct((n_slabs * CAP, 2 * BLK + PAD, BLK), jnp.bfloat16),
        in_specs=[smem, smem, vmem],
        out_specs=vmem,
        scratch_shapes=[pltpu.SMEM((n_slabs,), jnp.int32)],
        compiler_params=pltpu.CompilerParams(vmem_limit_bytes=16 * MIB),
        cost_estimate=pl.CostEstimate(flops=0, bytes_accessed=3 * MIB, transcendentals=0),
        name="place",
    )(slab, cells, tiles)


def device_kernel(
    n_task,
    info_ref,
    cot_ref,
    task_ref,
    lang_ref,
    x_hbm,
    xt_hbm,
    g0,
    g1,
    g2,
    g3,
    u0,
    u1,
    u2,
    u3,
    _step,
    own_ref,
    up_first,
    up_second,
    down_first,
    down_second,
    keep_ref,
    give_ref,
    x_ref,
    xt_ref,
    gate_m,
    up_m,
    acc,
    gate_pre,
    up_pre,
    d_gate,
    d_up,
    d_cols,
    cell_rows,
    cells_ref,
    first_ref,
    leader_ref,
    sems,
):
    f32, bf16 = jnp.float32, jnp.bfloat16
    ways = 4
    part = g0.shape[0]
    me, core = info_ref[0], info_ref[1]
    copies = []
    for k, (g, u) in enumerate(((g0, u0), (g1, u1), (g2, u2), (g3, u3))):
        to = pl.ds(pl.multiple_of(lax.rem(me + k, ways) * part, part), part)
        copies.append(pltpu.make_async_copy(g, gate_m.at[to], sems.at[k]))
        copies.append(pltpu.make_async_copy(u, up_m.at[to], sems.at[ways + k]))
    x_copy = pltpu.make_async_copy(x_hbm, x_ref, sems.at[8])
    xt_copy = pltpu.make_async_copy(xt_hbm, xt_ref, sems.at[9])
    for c in (*copies, x_copy, xt_copy):
        c.start()

    n_slots = acc.shape[0]
    for i in range(n_slots):
        tiles, j = (task_ref, i) if i < n_task else (lang_ref, i - n_task)
        row = tiles[j, 2 * BLK : 2 * BLK + PAD, :].astype(f32).astype(jnp.int32)
        cell_rows[i : i + 1, :] = row[0:1]
    cell_copy = pltpu.make_async_copy(cell_rows, cells_ref, sems.at[10])
    cell_copy.start()
    cell_copy.wait()

    def no_first(i, carry):
        first_ref[i] = -1
        return carry

    lax.fori_loop(0, first_ref.shape[0], no_first, 0)

    def find_leader(s, carry):
        cell = jnp.maximum(cells_ref[s, 0], 0)
        known = first_ref[cell]
        lead = jnp.where(known < 0, s, known)
        leader_ref[s] = lead

        @pl.when(cells_ref[s, 0] >= 0)
        def _():
            first_ref[cell] = lead

        return carry

    lax.fori_loop(0, n_slots, find_leader, 0)
    for c in copies:
        c.wait()

    def spot(cell):
        row = pl.multiple_of(lax.shift_right_logical(cell, 1) * BLK, BLK)
        col = pl.multiple_of(lax.bitwise_and(cell, 1) * BLK, BLK)
        return pl.ds(row, BLK), pl.ds(col, BLK)

    def gather_from(tiles, first):
        def step(i, carry):
            s = i + first
            cell = cells_ref[s, 0]
            lead = leader_ref[s]

            @pl.when((cell >= 0) & (lead == s))
            def _():
                at = spot(cell)
                acc[s, 0:BLK] = gate_m[at].astype(f32) + tiles[i, 0:BLK].astype(f32)
                acc[s, BLK:] = up_m[at].astype(f32) + tiles[i, BLK : 2 * BLK].astype(f32)

            @pl.when((cell >= 0) & (lead != s))
            def _():
                acc[lead] += tiles[i, 0 : 2 * BLK].astype(f32)

            return carry

        return step

    lax.fori_loop(0, n_task, gather_from(task_ref, 0), 0)
    lax.fori_loop(0, n_slots - n_task, gather_from(lang_ref, n_task), 0)

    def write_back(s, carry):
        cell = cells_ref[s, 0]

        @pl.when((cell >= 0) & (leader_ref[s] == s))
        def _():
            at = spot(cell)
            gate_m[at] = acc[s, 0:BLK].astype(bf16)
            up_m[at] = acc[s, BLK:].astype(bf16)

        return carry

    lax.fori_loop(0, n_slots, write_back, 0)

    depth = 1024
    gate_pre[...] = jnp.zeros_like(gate_pre)
    up_pre[...] = jnp.zeros_like(up_pre)

    def forward(k, carry):
        ks = pl.ds(pl.multiple_of(k * depth, depth), depth)
        xk = x_ref[:, ks]
        gate_pre[...] += jnp.dot(xk, gate_m[ks, :], preferred_element_type=f32)
        up_pre[...] += jnp.dot(xk, up_m[ks, :], preferred_element_type=f32)
        return carry

    x_copy.wait()
    lax.fori_loop(0, x_ref.shape[1] // depth, forward, 0)

    g, u = gate_pre[...], up_pre[...]
    s = jax.nn.sigmoid(g)
    c = cot_ref[...].astype(f32)
    dg = (c * u * s * (1.0 + g * (1.0 - s))).astype(bf16)
    du = (c * g * s).astype(bf16)
    d_gate[...] = dg
    d_up[...] = du
    for h in range(2):
        d_cols[h, :, 0:BLK] = dg[:, h * BLK : (h + 1) * BLK]
        d_cols[h, :, BLK:] = du[:, h * BLK : (h + 1) * BLK]

    def task_step(i, carry):
        cell = jnp.maximum(cells_ref[i, 0], 0)
        row = pl.multiple_of(lax.shift_right_logical(cell, 1) * BLK, BLK)
        side = lax.bitwise_and(cell, 1)
        r = jnp.dot(xt_ref[pl.ds(row, BLK), :], d_cols[side], preferred_element_type=f32)
        r = r.astype(bf16)
        low, high = r[0 : BLK // 2], r[BLK // 2 :]
        quarters = (low[:, 0:BLK], high[:, 0:BLK], low[:, BLK:], high[:, BLK:])

        def quarter(k):
            q = lax.rem(me + k, ways)
            even = jnp.where(q == 0, quarters[0], quarters[2])
            odd = jnp.where(q == 1, quarters[1], quarters[3])
            return jnp.where(lax.bitwise_and(q, 1) == 0, even, odd)

        own_ref[i] = quarter(0)
        half = n_task // 2

        @pl.when(i < half)
        def _():
            up_second[i] = quarter(1)
            up_first[i] = quarter(2)
            down_first[i] = quarter(3)

        @pl.when(i >= half)
        def _():
            up_first[i] = quarter(1)
            down_first[i] = quarter(2)
            down_second[i - half] = quarter(3)

        return carry

    xt_copy.wait()
    lax.fori_loop(0, n_task, task_step, 0)

    last = (((1,), (1,)), ((), ()))

    def backward(m, carry):
        rows = pl.ds(pl.multiple_of(m * 2 * BLK, 2 * BLK), 2 * BLK)
        r = lax.dot_general(d_gate[...], gate_m[rows, :], last, preferred_element_type=f32)
        r += lax.dot_general(d_up[...], up_m[rows, :], last, preferred_element_type=f32)
        r = r.astype(bf16)
        low, high = r[:, 0:BLK], r[:, BLK:]
        keep_ref[m] = jnp.where(core == 0, low, high)
        give_ref[m] = jnp.where(core == 0, high, low)
        return carry

    lax.fori_loop(0, keep_ref.shape[0], backward, 0)


def device_step(info, cot, task, lang, x, xt, gates, ups, step):
    bf16, f32 = jnp.bfloat16, jnp.float32
    n_task, n_slots = task.shape[0], task.shape[0] + lang.shape[0]
    tokens, width = x.shape
    cols = cot.shape[1]
    padded = -(-n_slots // 8) * 8
    vmem = pl.BlockSpec(memory_space=pltpu.VMEM)
    hbm = pl.BlockSpec(memory_space=pl.ANY)
    main = jax.ShapeDtypeStruct((width // (2 * BLK), tokens, BLK), bf16)
    return pl.pallas_call(
        lambda *refs: device_kernel(n_task, *refs),
        out_shape=(
            *[
                jax.ShapeDtypeStruct((n, BLK // 2, BLK), bf16)
                for n in (n_task, n_task, n_task // 2, n_task, n_task // 2)
            ],
            main,
            main,
        ),
        in_specs=[pl.BlockSpec(memory_space=pltpu.SMEM)] + [vmem] * 3 + [hbm] * 11,
        out_specs=[vmem] * 7,
        scratch_shapes=[
            pltpu.VMEM(x.shape, bf16),
            pltpu.VMEM(xt.shape, bf16),
            pltpu.VMEM((width, cols), bf16),
            pltpu.VMEM((width, cols), bf16),
            pltpu.VMEM((n_slots, 2 * BLK, BLK), f32),
            pltpu.VMEM((tokens, cols), f32),
            pltpu.VMEM((tokens, cols), f32),
            pltpu.VMEM((tokens, cols), bf16),
            pltpu.VMEM((tokens, cols), bf16),
            pltpu.VMEM((2, tokens, 2 * BLK), bf16),
            pltpu.VMEM((padded, BLK), jnp.int32),
            pltpu.SMEM((padded, BLK), jnp.int32),
            pltpu.SMEM((width // BLK * cols // BLK,), jnp.int32),
            pltpu.SMEM((n_slots,), jnp.int32),
            pltpu.SemaphoreType.DMA((11,)),
        ],
        compiler_params=pltpu.CompilerParams(vmem_limit_bytes=56 * MIB),
        cost_estimate=pl.CostEstimate(
            flops=10 * tokens * width * cols, bytes_accessed=24 * MIB, transcendentals=tokens * cols
        ),
        name="device_step",
    )(info, cot, task, lang, x, xt, *gates, *ups, step)


def pace_kernel(*refs):
    refs[-1][...] = jnp.zeros_like(refs[-1])


def pace(*arrays):
    return pl.pallas_call(
        pace_kernel,
        out_shape=jax.ShapeDtypeStruct((8, BLK), jnp.float32),
        in_specs=[pl.BlockSpec(memory_space=pl.ANY)] * len(arrays),
        out_specs=pl.BlockSpec(memory_space=pltpu.VMEM),
        compiler_params=pltpu.CompilerParams(vmem_limit_bytes=MIB),
        cost_estimate=pl.CostEstimate(flops=10**11, bytes_accessed=4096, transcendentals=0),
        name="pace",
    )(*arrays)


def ring_first(axis, up_first, down_first):
    return (
        lax.ppermute(up_first, axis, ring(axis, 1)),
        lax.ppermute(down_first, axis, ring(axis, -1)),
    )


def ring_rest(axis, own, up_second, down_second, from_left, from_right):
    f32, bf16 = jnp.float32, jnp.bfloat16
    half = own.shape[0] // 2
    up_second = (up_second.astype(f32) + from_left[:half].astype(f32)).astype(bf16)
    down_second = (down_second.astype(f32) + from_right[half:].astype(f32)).astype(bf16)
    low_left = lax.ppermute(up_second, axis, ring(axis, 1))
    high_right = lax.ppermute(down_second, axis, ring(axis, -1))
    low = own[:half].astype(f32) + low_left.astype(f32) + from_right[:half].astype(f32)
    high = own[half:].astype(f32) + high_right.astype(f32) + from_left[half:].astype(f32)
    return jnp.concatenate([low, high], axis=0).astype(bf16)


def on_device(
    tokens_in,
    cotangent,
    gate_base,
    up_base,
    lang_delta,
    lang_cell,
    group_lang,
    task_delta,
    task_slab,
    task_cell,
):
    f32, bf16 = jnp.float32, jnp.bfloat16
    fsdp = ("z", "core")
    n_lang, n_z, n_core, n_dp = (lax.axis_size(a) for a in ("lang", "z", "core", "dp"))
    n_fsdp = n_z * n_core
    language = group_lang[0]
    my_lang, my_core, my_dp = (lax.axis_index(a) for a in ("lang", "core", "dp"))
    held = task_delta.shape[0]

    gate_left = lax.ppermute(gate_base, "dp", ring("dp", 1))
    up_right = lax.ppermute(up_base, "dp", ring("dp", -1))
    up_left = lax.ppermute(up_base, "dp", ring("dp", 1))
    gate_right = lax.ppermute(gate_base, "dp", ring("dp", -1))
    step = pace(gate_left, gate_right, up_left, up_right)
    gate_on, up_on, step = lax.optimization_barrier((gate_left, up_right, step))
    gate_far = lax.ppermute(gate_on, "dp", ring("dp", 1))
    up_far = lax.ppermute(up_on, "dp", ring("dp", -1))

    target = task_slab[:, 0]
    send_task = place(target, task_cell[:, 0], task_delta.reshape(held, 2 * BLK, BLK), n_fsdp)
    got_task = lax.all_to_all(send_task, fsdp, split_axis=0, concat_axis=0, tiled=True)
    lang_tiles = lang_delta[0, 0].reshape(lang_delta.shape[2:4] + (2 * BLK, BLK))
    send_lang = with_cells(lang_tiles, lang_cell[0, 0])
    pick = lax.rem(my_lang - language + n_lang, n_lang)
    chosen = None
    for k in range(n_lang):
        piece = lax.dynamic_index_in_dim(send_lang, lax.rem(my_lang + k, n_lang), 0, keepdims=False)
        if k:
            piece = lax.ppermute(piece, "lang", ring("lang", k))
        chosen = piece if chosen is None else jnp.where(pick == k, piece, chosen)

    *pieces, keep, give = device_step(
        jnp.stack([my_dp, my_core]).astype(jnp.int32),
        cotangent,
        got_task,
        chosen,
        tokens_in,
        tokens_in.T,
        (gate_base, gate_right, gate_far, gate_left),
        (up_base, up_right, up_far, up_left),
        step,
    )
    got = lax.ppermute(give, "core", ring("core", 1))
    task_first = ring_first("dp", pieces[1], pieces[3])

    pair = (keep.astype(f32) + got.astype(f32)).astype(bf16)
    pair = pair.reshape(n_lang, n_z, *keep.shape[1:])
    over_lang = lax.all_to_all(pair, "lang", split_axis=0, concat_axis=0, tiled=True)
    tsum = ring_rest("dp", pieces[0], pieces[2], pieces[4], *task_first)
    tsum, over_lang = lax.optimization_barrier((tsum, over_lang))
    over_lang = jnp.sum(over_lang.astype(f32), axis=0).astype(bf16)
    back = lax.all_to_all(tsum, fsdp, split_axis=0, concat_axis=0, tiled=True)
    place_in = jnp.arange(held, dtype=jnp.int32)
    same = (target[:, None] == target[None, :]) & (place_in[None, :] < place_in[:, None])
    dest = target * CAP + jnp.sum(same.astype(jnp.int32), axis=1)
    slots = jnp.arange(n_fsdp * CAP, dtype=jnp.int32)
    one_hot = (dest[:, None] == slots[None, :]).astype(bf16)
    mine = jnp.einsum("is,srk->irk", one_hot, back, preferred_element_type=f32).astype(bf16)
    others = [lax.ppermute(mine, "dp", ring("dp", -k)) for k in (2, 1, 3)]
    stacked = jnp.stack([mine, others[1], others[0], others[2]], axis=0)
    stacked = jnp.stack(
        [
            lax.dynamic_index_in_dim(stacked, lax.rem(q - my_dp + n_dp, n_dp), 0, keepdims=False)
            for q in range(n_dp)
        ],
        axis=1,
    )
    task_grad = stacked.astype(f32).reshape(task_delta.shape)

    over_z = lax.all_to_all(over_lang, "z", split_axis=0, concat_axis=0, tiled=True)
    grad_input = jnp.sum(over_z.astype(f32), axis=0).astype(bf16)
    return (grad_input, task_grad)


def solution(mesh):
    lang, fsdp, dp = (mesh.shape[a] for a in ("lang", "fsdp", "dp"))
    fine = Mesh(mesh.devices.reshape(lang, fsdp // 2, 2, dp), ("lang", "z", "core", "dp"))
    cols = ("lang", "z", "core")
    return jax.shard_map(
        on_device,
        mesh=fine,
        in_specs=(
            P("dp", None),
            P("dp", cols),
            P("dp", cols),
            P("dp", cols),
            P("lang", ("z", "core"), None, None, None),
            P("lang", ("z", "core"), None, None),
            P("dp"),
            P(cols, None),
            P(cols, None),
            P(cols, None),
        ),
        out_specs=(P("dp", cols), P(cols, None)),
        check_vma=False,
    )
```

```python
import jax
import jax.numpy as jnp
from jax import lax
from jax.experimental import pallas as pl
from jax.experimental.pallas import tpu as pltpu
from jax.sharding import Mesh, PartitionSpec as P

BLK = 128
CAP = 2
PAD = 16
MIB = 1024 * 1024


def ring(axis, step):
    n = lax.axis_size(axis)
    return [(i, (i + step) % n) for i in range(n)]


def with_cells(tiles, cells):
    rows = jnp.broadcast_to(cells.astype(jnp.bfloat16)[..., None, None], cells.shape + (PAD, BLK))
    return jnp.concatenate([tiles, rows], axis=-2)


def place_kernel(slab_ref, cells_ref, tiles_ref, out_ref, used_ref):
    def clear(i, carry):
        out_ref[i, 2 * BLK :, :] = jnp.full((PAD, BLK), -1.0, jnp.bfloat16)
        return carry

    lax.fori_loop(0, out_ref.shape[0], clear, 0)

    def unused(i, carry):
        used_ref[i] = 0
        return carry

    lax.fori_loop(0, used_ref.shape[0], unused, 0)

    def put(i, carry):
        slab = slab_ref[i]
        slot = slab * CAP + used_ref[slab]
        used_ref[slab] += 1
        out_ref[slot, 0 : 2 * BLK, :] = tiles_ref[i]
        out_ref[slot, 2 * BLK :, :] = jnp.full(
            (PAD, BLK), cells_ref[i].astype(jnp.float32), jnp.float32
        ).astype(jnp.bfloat16)
        return carry

    lax.fori_loop(0, tiles_ref.shape[0], put, 0)


def place(slab, cells, tiles, n_slabs):
    smem = pl.BlockSpec(memory_space=pltpu.SMEM)
    vmem = pl.BlockSpec(memory_space=pltpu.VMEM)
    return pl.pallas_call(
        place_kernel,
        out_shape=jax.ShapeDtypeStruct((n_slabs * CAP, 2 * BLK + PAD, BLK), jnp.bfloat16),
        in_specs=[smem, smem, vmem],
        out_specs=vmem,
        scratch_shapes=[pltpu.SMEM((n_slabs,), jnp.int32)],
        compiler_params=pltpu.CompilerParams(vmem_limit_bytes=16 * MIB),
        cost_estimate=pl.CostEstimate(flops=0, bytes_accessed=3 * MIB, transcendentals=0),
        name="place",
    )(slab, cells, tiles)


def take_own_kernel(slab_ref, back_ref, _mark, out_ref, used_ref):
    def unused(i, carry):
        used_ref[i] = 0
        return carry

    lax.fori_loop(0, used_ref.shape[0], unused, 0)

    def take(i, carry):
        slab = slab_ref[i]
        out_ref[i] = back_ref[slab * CAP + used_ref[slab]]
        used_ref[slab] += 1
        return carry

    lax.fori_loop(0, out_ref.shape[0], take, 0)


def take_own(slab, back, mark):
    smem = pl.BlockSpec(memory_space=pltpu.SMEM)
    vmem = pl.BlockSpec(memory_space=pltpu.VMEM)
    return pl.pallas_call(
        take_own_kernel,
        out_shape=jax.ShapeDtypeStruct(slab.shape + back.shape[1:], back.dtype),
        in_specs=[smem, vmem, pl.BlockSpec(memory_space=pl.ANY)],
        out_specs=vmem,
        scratch_shapes=[pltpu.SMEM((back.shape[0] // CAP,), jnp.int32)],
        compiler_params=pltpu.CompilerParams(vmem_limit_bytes=4 * MIB),
        cost_estimate=pl.CostEstimate(flops=0, bytes_accessed=MIB, transcendentals=0),
        name="take_own",
    )(slab, back, mark)


def device_kernel(
    n_task,
    info_ref,
    cot_ref,
    task_ref,
    lang_ref,
    x_hbm,
    xt_hbm,
    g0,
    g1,
    g2,
    g3,
    u0,
    u1,
    u2,
    u3,
    _step,
    own_out,
    up_first,
    up_second,
    down_first,
    down_second,
    keep_out,
    give_out,
    x_ref,
    xt_ref,
    gate_m,
    up_m,
    acc,
    gate_pre,
    up_pre,
    d_gate,
    d_up,
    d_cols,
    task_out,
    main_out,
    cell_rows,
    cells_ref,
    first_ref,
    leader_ref,
    in_sems,
    out_sems,
):
    f32, bf16 = jnp.float32, jnp.bfloat16
    ways = 4
    part = g0.shape[0]
    me, core, lang = info_ref[0], info_ref[1], info_ref[2]
    order = (0, 3, 1, 2)
    x_copy = pltpu.make_async_copy(x_hbm, x_ref, in_sems.at[8])
    xt_copy = pltpu.make_async_copy(xt_hbm, xt_ref, in_sems.at[9])
    x_copy.start()
    copies, starts = {}, {}
    for k, (g, u) in enumerate(((g0, u0), (g1, u1), (g2, u2), (g3, u3))):
        starts[k] = pl.multiple_of(lax.rem(me + k, ways) * part, part)
        to = pl.ds(starts[k], part)
        copies[k] = (
            pltpu.make_async_copy(g, gate_m.at[to], in_sems.at[k]),
            pltpu.make_async_copy(u, up_m.at[to], in_sems.at[ways + k]),
        )
    for k in order:
        for c in copies[k]:
            c.start()
    xt_copy.start()

    n_slots = acc.shape[0]
    for i in range(n_slots):
        tiles, j = (task_ref, i) if i < n_task else (lang_ref, i - n_task)
        row = tiles[j, 2 * BLK : 2 * BLK + PAD, :].astype(f32).astype(jnp.int32)
        cell_rows[i : i + 1, :] = row[0:1]
    cell_copy = pltpu.make_async_copy(cell_rows, cells_ref, in_sems.at[10])
    cell_copy.start()
    gate_pre[...] = jnp.zeros_like(gate_pre)
    up_pre[...] = jnp.zeros_like(up_pre)

    def no_first(i, carry):
        first_ref[i] = -1
        return carry

    lax.fori_loop(0, first_ref.shape[0], no_first, 0)
    cell_copy.wait()

    def find_leader(s, carry):
        cell = jnp.maximum(cells_ref[s, 0], 0)
        known = first_ref[cell]
        lead = jnp.where(known < 0, s, known)
        leader_ref[s] = lead

        @pl.when(cells_ref[s, 0] >= 0)
        def _():
            first_ref[cell] = lead

        return carry

    lax.fori_loop(0, n_slots, find_leader, 0)

    def spot(cell):
        row = pl.multiple_of(lax.shift_right_logical(cell, 1) * BLK, BLK)
        col = pl.multiple_of(lax.bitwise_and(cell, 1) * BLK, BLK)
        return pl.ds(row, BLK), pl.ds(col, BLK)

    def inside(cell, first_cell):
        return (cell >= first_cell) & (cell < first_cell + 2 * part // BLK)

    def gather_from(tiles, first, first_cell):
        def step(i, carry):
            s = i + first
            cell = cells_ref[s, 0]
            lead = leader_ref[s]
            here = inside(cell, first_cell)

            @pl.when(here & (lead == s))
            def _():
                at = spot(cell)
                acc[s, 0:BLK] = gate_m[at].astype(f32) + tiles[i, 0:BLK].astype(f32)
                acc[s, BLK:] = up_m[at].astype(f32) + tiles[i, BLK : 2 * BLK].astype(f32)

            @pl.when(here & (lead != s))
            def _():
                acc[lead] += tiles[i, 0 : 2 * BLK].astype(f32)

            return carry

        return step

    depth = 1024
    for k in order:
        for c in copies[k]:
            c.wait()
        first_cell = starts[k] // BLK * 2
        lax.fori_loop(0, n_task, gather_from(task_ref, 0, first_cell), 0)
        lax.fori_loop(0, n_slots - n_task, gather_from(lang_ref, n_task, first_cell), 0)

        def write_back(s, carry, first_cell=first_cell):
            cell = cells_ref[s, 0]

            @pl.when(inside(cell, first_cell) & (leader_ref[s] == s))
            def _():
                at = spot(cell)
                gate_m[at] = acc[s, 0:BLK].astype(bf16)
                up_m[at] = acc[s, BLK:].astype(bf16)

            return carry

        lax.fori_loop(0, n_slots, write_back, 0)
        if k == order[0]:
            x_copy.wait()
        for step in range(part // depth):
            rows = pl.ds(pl.multiple_of(starts[k] + step * depth, depth), depth)
            xk = x_ref[:, rows]
            gate_pre[...] += jnp.dot(xk, gate_m[rows, :], preferred_element_type=f32)
            up_pre[...] += jnp.dot(xk, up_m[rows, :], preferred_element_type=f32)

    g, u = gate_pre[...], up_pre[...]
    s = jax.nn.sigmoid(g)
    c = cot_ref[...].astype(f32)
    dg = (c * u * s * (1.0 + g * (1.0 - s))).astype(bf16)
    du = (c * g * s).astype(bf16)
    d_gate[...] = dg
    d_up[...] = du
    for h in range(2):
        d_cols[h, :, 0:BLK] = dg[:, h * BLK : (h + 1) * BLK]
        d_cols[h, :, BLK:] = du[:, h * BLK : (h + 1) * BLK]
    xt_copy.wait()

    def task_step(i, carry):
        cell = jnp.maximum(cells_ref[i, 0], 0)
        row = pl.multiple_of(lax.shift_right_logical(cell, 1) * BLK, BLK)
        side = lax.bitwise_and(cell, 1)
        r = jnp.dot(xt_ref[pl.ds(row, BLK), :], d_cols[side], preferred_element_type=f32)
        r = r.astype(bf16)
        task_out[0, i] = r[0 : BLK // 2, 0:BLK]
        task_out[1, i] = r[BLK // 2 :, 0:BLK]
        task_out[2, i] = r[0 : BLK // 2, BLK:]
        task_out[3, i] = r[BLK // 2 :, BLK:]
        return carry

    lax.fori_loop(0, n_task, task_step, 0, unroll=4)
    q = [lax.rem(me + k, ways) for k in range(ways)]
    half = n_task // 2
    low, high = pl.ds(0, half), pl.ds(half, half)
    moves = [
        (task_out.at[q[0]], own_out),
        (task_out.at[q[2], low], up_first.at[low]),
        (task_out.at[q[1], high], up_first.at[high]),
        (task_out.at[q[3], low], down_first.at[low]),
        (task_out.at[q[2], high], down_first.at[high]),
        (task_out.at[q[1], low], up_second),
        (task_out.at[q[3], high], down_second),
    ]
    out_copies = [
        pltpu.make_async_copy(src, dst, out_sems.at[n]) for n, (src, dst) in enumerate(moves)
    ]
    for copy in out_copies:
        copy.start()

    last = (((1,), (1,)), ((), ()))
    per = keep_out.shape[0] // ways

    def backward(m, carry):
        rows = pl.ds(pl.multiple_of(m * 2 * BLK, 2 * BLK), 2 * BLK)
        r = lax.dot_general(d_gate[...], gate_m[rows, :], last, preferred_element_type=f32)
        r += lax.dot_general(d_up[...], up_m[rows, :], last, preferred_element_type=f32)
        r = r.astype(bf16)
        main_out[0, m] = r[:, 0:BLK]
        main_out[1, m] = r[:, BLK:]
        return carry

    for n in range(ways):
        lax.fori_loop(n * per, (n + 1) * per, backward, 0, unroll=4)
        src = pl.ds(n * per, per)
        dst = pl.ds(lax.rem(n + ways - lang, ways) * per, per)
        for way, out in ((core, keep_out), (1 - core, give_out)):
            copy = pltpu.make_async_copy(
                main_out.at[way, src], out.at[dst], out_sems.at[len(out_copies)]
            )
            copy.start()
            out_copies.append(copy)
    for copy in out_copies:
        copy.wait()


def device_step(info, cot, task, lang, x, xt, gates, ups, step):
    bf16, f32 = jnp.bfloat16, jnp.float32
    n_task, n_slots = task.shape[0], task.shape[0] + lang.shape[0]
    tokens, width = x.shape
    cols = cot.shape[1]
    padded = -(-n_slots // 8) * 8
    vmem = pl.BlockSpec(memory_space=pltpu.VMEM)
    hbm = pl.BlockSpec(memory_space=pl.ANY)
    pairs = width // (2 * BLK)
    main = jax.ShapeDtypeStruct((pairs, tokens, BLK), bf16)
    return pl.pallas_call(
        lambda *refs: device_kernel(n_task, *refs),
        out_shape=(
            *[
                jax.ShapeDtypeStruct((n, BLK // 2, BLK), bf16)
                for n in (n_task, n_task, n_task // 2, n_task, n_task // 2)
            ],
            main,
            main,
        ),
        in_specs=[pl.BlockSpec(memory_space=pltpu.SMEM)] + [vmem] * 3 + [hbm] * 11,
        out_specs=[hbm] * 7,
        scratch_shapes=[
            pltpu.VMEM(x.shape, bf16),
            pltpu.VMEM(xt.shape, bf16),
            pltpu.VMEM((width, cols), bf16),
            pltpu.VMEM((width, cols), bf16),
            pltpu.VMEM((n_slots, 2 * BLK, BLK), f32),
            pltpu.VMEM((tokens, cols), f32),
            pltpu.VMEM((tokens, cols), f32),
            pltpu.VMEM((tokens, cols), bf16),
            pltpu.VMEM((tokens, cols), bf16),
            pltpu.VMEM((2, tokens, 2 * BLK), bf16),
            pltpu.VMEM((4, n_task, BLK // 2, BLK), bf16),
            pltpu.VMEM((2, pairs, tokens, BLK), bf16),
            pltpu.VMEM((padded, BLK), jnp.int32),
            pltpu.SMEM((padded, BLK), jnp.int32),
            pltpu.SMEM((width // BLK * cols // BLK,), jnp.int32),
            pltpu.SMEM((n_slots,), jnp.int32),
            pltpu.SemaphoreType.DMA((11,)),
            pltpu.SemaphoreType.DMA((15,)),
        ],
        compiler_params=pltpu.CompilerParams(vmem_limit_bytes=56 * MIB),
        cost_estimate=pl.CostEstimate(
            flops=10 * tokens * width * cols, bytes_accessed=24 * MIB, transcendentals=tokens * cols
        ),
        name="device_step",
    )(info, cot, task, lang, x, xt, *gates, *ups, step)


def pace_kernel(*refs):
    refs[-1][...] = jnp.zeros_like(refs[-1])


def pace(*arrays, flops=10**11):
    return pl.pallas_call(
        pace_kernel,
        out_shape=jax.ShapeDtypeStruct((8, BLK), jnp.float32),
        in_specs=[pl.BlockSpec(memory_space=pl.ANY)] * len(arrays),
        out_specs=pl.BlockSpec(memory_space=pltpu.VMEM),
        compiler_params=pltpu.CompilerParams(vmem_limit_bytes=MIB),
        cost_estimate=pl.CostEstimate(flops=flops, bytes_accessed=4096, transcendentals=0),
        name="pace",
    )(*arrays)


def ring_first(axis, up_first, down_first):
    return (
        lax.ppermute(up_first, axis, ring(axis, 1)),
        lax.ppermute(down_first, axis, ring(axis, -1)),
    )


def ring_rest(axis, own, up_second, down_second, from_left, from_right):
    f32, bf16 = jnp.float32, jnp.bfloat16
    half = own.shape[0] // 2
    up_second = (up_second.astype(f32) + from_left[:half].astype(f32)).astype(bf16)
    down_second = (down_second.astype(f32) + from_right[half:].astype(f32)).astype(bf16)
    low_left = lax.ppermute(up_second, axis, ring(axis, 1))
    high_right = lax.ppermute(down_second, axis, ring(axis, -1))
    low = own[:half].astype(f32) + low_left.astype(f32) + from_right[:half].astype(f32)
    high = own[half:].astype(f32) + high_right.astype(f32) + from_left[half:].astype(f32)
    return jnp.concatenate([low, high], axis=0).astype(bf16)


def on_device(
    tokens_in,
    cotangent,
    gate_base,
    up_base,
    lang_delta,
    lang_cell,
    group_lang,
    task_delta,
    task_slab,
    task_cell,
):
    f32, bf16 = jnp.float32, jnp.bfloat16
    fsdp = ("z", "core")
    n_lang, n_z, n_core, n_dp = (lax.axis_size(a) for a in ("lang", "z", "core", "dp"))
    n_fsdp = n_z * n_core
    language = group_lang[0]
    my_lang, my_core, my_dp = (lax.axis_index(a) for a in ("lang", "core", "dp"))
    held = task_delta.shape[0]

    gate_left = lax.ppermute(gate_base, "dp", ring("dp", 1))
    up_right = lax.ppermute(up_base, "dp", ring("dp", -1))
    up_left = lax.ppermute(up_base, "dp", ring("dp", 1))
    gate_right = lax.ppermute(gate_base, "dp", ring("dp", -1))
    step = pace(gate_left, gate_right, up_left, up_right)
    gate_on, up_on, step = lax.optimization_barrier((gate_left, up_right, step))
    gate_far = lax.ppermute(gate_on, "dp", ring("dp", 1))
    up_far = lax.ppermute(up_on, "dp", ring("dp", -1))

    target = task_slab[:, 0]
    send_task = place(target, task_cell[:, 0], task_delta.reshape(held, 2 * BLK, BLK), n_fsdp)
    got_task = lax.all_to_all(send_task, fsdp, split_axis=0, concat_axis=0, tiled=True)
    lang_tiles = lang_delta[0, 0].reshape(lang_delta.shape[2:4] + (2 * BLK, BLK))
    send_lang = with_cells(lang_tiles, lang_cell[0, 0])
    pick = lax.rem(my_lang - language + n_lang, n_lang)
    chosen = None
    for k in range(n_lang):
        piece = lax.dynamic_index_in_dim(send_lang, lax.rem(my_lang + k, n_lang), 0, keepdims=False)
        if k:
            piece = lax.ppermute(piece, "lang", ring("lang", k))
        chosen = piece if chosen is None else jnp.where(pick == k, piece, chosen)

    *pieces, keep, give = device_step(
        jnp.stack([my_dp, my_core, my_lang]).astype(jnp.int32),
        cotangent,
        got_task,
        chosen,
        tokens_in,
        tokens_in.T,
        (gate_base, gate_right, gate_far, gate_left),
        (up_base, up_right, up_far, up_left),
        step,
    )
    got = lax.ppermute(give, "core", ring("core", 1))
    task_first = ring_first("dp", pieces[1], pieces[3])


    def both(first, last):
        first, last = first * n_z // 2, last * n_z // 2
        return (keep[first:last].astype(f32) + got[first:last].astype(f32)).astype(bf16)

    main_up = jnp.concatenate([both(4, 5), both(3, 4)], axis=0)
    main_down = jnp.concatenate([both(6, 7), both(5, 6)], axis=0)
    main_first = ring_first("lang", main_up, main_down)
    mark = pace(main_up, main_down)
    task_left, task_right, mark = lax.optimization_barrier((*task_first, mark))
    tsum = ring_rest("dp", pieces[0], pieces[2], pieces[4], task_left, task_right)
    over_lang = ring_rest("lang", both(0, 2), both(2, 3), both(7, 8), *main_first)
    mark = pace(*main_first, mark, flops=0)
    back = lax.all_to_all(tsum, fsdp, split_axis=0, concat_axis=0, tiled=True)
    mine = take_own(target, back, mark)
    others = [lax.ppermute(mine, "dp", ring("dp", -k)) for k in (2, 1, 3)]
    stacked = jnp.stack([mine, others[1], others[0], others[2]], axis=0)
    stacked = jnp.stack(
        [
            lax.dynamic_index_in_dim(stacked, lax.rem(q - my_dp + n_dp, n_dp), 0, keepdims=False)
            for q in range(n_dp)
        ],
        axis=1,
    )
    task_grad = stacked.astype(f32).reshape(task_delta.shape)

    over_z = lax.all_to_all(over_lang, "z", split_axis=0, concat_axis=0, tiled=True)
    grad_input = jnp.sum(over_z.astype(f32), axis=0).astype(bf16)
    return (grad_input, task_grad)


def solution(mesh):
    lang, fsdp, dp = (mesh.shape[a] for a in ("lang", "fsdp", "dp"))
    fine = Mesh(mesh.devices.reshape(lang, fsdp // 2, 2, dp), ("lang", "z", "core", "dp"))
    cols = ("lang", "z", "core")
    return jax.shard_map(
        on_device,
        mesh=fine,
        in_specs=(
            P("dp", None),
            P("dp", cols),
            P("dp", cols),
            P("dp", cols),
            P("lang", ("z", "core"), None, None, None),
            P("lang", ("z", "core"), None, None),
            P("dp"),
            P(cols, None),
            P(cols, None),
            P(cols, None),
        ),
        out_specs=(P("dp", cols), P(cols, None)),
        check_vma=False,
    )
```

```python
import jax
import jax.numpy as jnp
from jax import lax
from jax.experimental import pallas as pl
from jax.experimental.pallas import tpu as pltpu
from jax.sharding import Mesh, PartitionSpec as P

BLK = 128
CAP = 2
PAD = 16
MIB = 1024 * 1024


def ring(axis, step):
    n = lax.axis_size(axis)
    return [(i, (i + step) % n) for i in range(n)]


def with_cells(tiles, cells):
    rows = jnp.broadcast_to(cells.astype(jnp.bfloat16)[..., None, None], cells.shape + (PAD, BLK))
    return jnp.concatenate([tiles, rows], axis=-2)


def place_kernel(slab_ref, cells_ref, tiles_ref, out_ref, used_ref):
    def clear(i, carry):
        out_ref[i, 2 * BLK :, :] = jnp.full((PAD, BLK), -1.0, jnp.bfloat16)
        return carry

    lax.fori_loop(0, out_ref.shape[0], clear, 0)

    def unused(i, carry):
        used_ref[i] = 0
        return carry

    lax.fori_loop(0, used_ref.shape[0], unused, 0)

    def put(i, carry):
        slab = slab_ref[i]
        slot = slab * CAP + used_ref[slab]
        used_ref[slab] += 1
        out_ref[slot, 0 : 2 * BLK, :] = tiles_ref[i]
        out_ref[slot, 2 * BLK :, :] = jnp.full(
            (PAD, BLK), cells_ref[i].astype(jnp.float32), jnp.float32
        ).astype(jnp.bfloat16)
        return carry

    lax.fori_loop(0, tiles_ref.shape[0], put, 0)


def place(slab, cells, tiles, n_slabs):
    smem = pl.BlockSpec(memory_space=pltpu.SMEM)
    vmem = pl.BlockSpec(memory_space=pltpu.VMEM)
    return pl.pallas_call(
        place_kernel,
        out_shape=jax.ShapeDtypeStruct((n_slabs * CAP, 2 * BLK + PAD, BLK), jnp.bfloat16),
        in_specs=[smem, smem, vmem],
        out_specs=vmem,
        scratch_shapes=[pltpu.SMEM((n_slabs,), jnp.int32)],
        compiler_params=pltpu.CompilerParams(vmem_limit_bytes=16 * MIB),
        cost_estimate=pl.CostEstimate(flops=0, bytes_accessed=3 * MIB, transcendentals=0),
        name="place",
    )(slab, cells, tiles)


def take_own_kernel(slab_ref, back_ref, _mark, out_ref, used_ref):
    def unused(i, carry):
        used_ref[i] = 0
        return carry

    lax.fori_loop(0, used_ref.shape[0], unused, 0)

    def take(i, carry):
        slab = slab_ref[i]
        out_ref[i] = back_ref[slab * CAP + used_ref[slab]]
        used_ref[slab] += 1
        return carry

    lax.fori_loop(0, out_ref.shape[0], take, 0)


def take_own(slab, back, mark):
    smem = pl.BlockSpec(memory_space=pltpu.SMEM)
    vmem = pl.BlockSpec(memory_space=pltpu.VMEM)
    return pl.pallas_call(
        take_own_kernel,
        out_shape=jax.ShapeDtypeStruct(slab.shape + back.shape[1:], back.dtype),
        in_specs=[smem, vmem, pl.BlockSpec(memory_space=pl.ANY)],
        out_specs=vmem,
        scratch_shapes=[pltpu.SMEM((back.shape[0] // CAP,), jnp.int32)],
        compiler_params=pltpu.CompilerParams(vmem_limit_bytes=4 * MIB),
        cost_estimate=pl.CostEstimate(flops=0, bytes_accessed=MIB, transcendentals=0),
        name="take_own",
    )(slab, back, mark)


def spot(cell):
    row = pl.multiple_of(lax.shift_right_logical(cell, 1) * BLK, BLK)
    col = pl.multiple_of(lax.bitwise_and(cell, 1) * BLK, BLK)
    return pl.ds(row, BLK), pl.ds(col, BLK)


def find_leaders(cells_ref, first_ref, leader_ref):
    def no_first(i, carry):
        first_ref[i] = -1
        return carry

    lax.fori_loop(0, first_ref.shape[0], no_first, 0)

    def find(s, carry):
        cell = jnp.maximum(cells_ref[s, 0], 0)
        known = first_ref[cell]
        lead = jnp.where(known < 0, s, known)
        leader_ref[s] = lead

        @pl.when(cells_ref[s, 0] >= 0)
        def _():
            first_ref[cell] = lead

        return carry

    lax.fori_loop(0, leader_ref.shape[0], find, 0)


def compose(cells_ref, leader_ref, task_ref, lang_ref, acc, gate_m, up_m, first_cell):
    f32 = jnp.float32
    n_task, n_cells = task_ref.shape[0], 2 * gate_m.shape[0] // BLK

    def inside(s):
        cell = cells_ref[s, 0] - first_cell
        return (cell >= 0) & (cell < n_cells), cell

    def add_from(tiles, first):
        def step(i, carry):
            s = i + first
            here, cell = inside(s)
            lead = leader_ref[s]

            @pl.when(here & (lead == s))
            def _():
                at = spot(cell)
                acc[s, 0:BLK] = gate_m[at].astype(f32) + tiles[i, 0:BLK].astype(f32)
                acc[s, BLK:] = up_m[at].astype(f32) + tiles[i, BLK : 2 * BLK].astype(f32)

            @pl.when(here & (lead != s))
            def _():
                acc[lead] += tiles[i, 0 : 2 * BLK].astype(f32)

            return carry

        return step

    lax.fori_loop(0, n_task, add_from(task_ref, 0), 0)
    lax.fori_loop(0, lang_ref.shape[0], add_from(lang_ref, n_task), 0)

    def write_back(s, carry):
        here, cell = inside(s)

        @pl.when(here & (leader_ref[s] == s))
        def _():
            at = spot(cell)
            gate_m[at] = acc[s, 0:BLK].astype(gate_m.dtype)
            up_m[at] = acc[s, BLK:].astype(up_m.dtype)

        return carry

    lax.fori_loop(0, leader_ref.shape[0], write_back, 0)


WAYS = 4
EARLY = (0, 3, 1)
LATE = 2


def early_kernel(
    info_ref,
    task_ref,
    lang_ref,
    x_hbm,
    g0,
    g3,
    g1,
    u0,
    u3,
    u1,
    gate_pre,
    up_pre,
    cell_rows,
    gate_out,
    up_out,
    x_ref,
    gate_m,
    up_m,
    acc,
    cells_ref,
    first_ref,
    leader_ref,
    in_sems,
    out_sems,
):
    f32 = jnp.float32
    part = g0.shape[0]
    me = info_ref[0]
    copies = []
    for n, (g, u) in enumerate(((g0, u0), (g3, u3), (g1, u1))):
        copies.append(
            (
                pltpu.make_async_copy(g, gate_m.at[n], in_sems.at[2 * n]),
                pltpu.make_async_copy(u, up_m.at[n], in_sems.at[2 * n + 1]),
            )
        )
    x_copy = pltpu.make_async_copy(x_hbm, x_ref, in_sems.at[6])
    for c in copies[0]:
        c.start()
    x_copy.start()
    for pair in copies[1:]:
        for c in pair:
            c.start()

    n_task = task_ref.shape[0]
    for i in range(leader_ref.shape[0]):
        tiles, j = (task_ref, i) if i < n_task else (lang_ref, i - n_task)
        row = tiles[j, 2 * BLK : 2 * BLK + PAD, :].astype(f32).astype(jnp.int32)
        cell_rows[i : i + 1, :] = row[0:1]
    cell_copy = pltpu.make_async_copy(cell_rows, cells_ref, in_sems.at[7])
    cell_copy.start()
    gate_pre[...] = jnp.zeros_like(gate_pre)
    up_pre[...] = jnp.zeros_like(up_pre)
    cell_copy.wait()
    find_leaders(cells_ref, first_ref, leader_ref)

    depth = 1024
    out_copies = []
    for n, k in enumerate(EARLY):
        start = pl.multiple_of(lax.rem(me + k, WAYS) * part, part)
        for c in copies[n]:
            c.wait()
        compose(
            cells_ref, leader_ref, task_ref, lang_ref, acc, gate_m.at[n], up_m.at[n], start // BLK * 2
        )
        for j, (m, out) in enumerate(((gate_m, gate_out), (up_m, up_out))):
            copy = pltpu.make_async_copy(m.at[n], out.at[n], out_sems.at[2 * n + j])
            copy.start()
            out_copies.append(copy)
        if n == 0:
            x_copy.wait()
        for step in range(part // depth):
            xk = x_ref[:, pl.ds(pl.multiple_of(start + step * depth, depth), depth)]
            rows = pl.ds(step * depth, depth)
            gate_pre[...] += jnp.dot(xk, gate_m[n, rows, :], preferred_element_type=f32)
            up_pre[...] += jnp.dot(xk, up_m[n, rows, :], preferred_element_type=f32)
    for copy in out_copies:
        copy.wait()


def early_step(info, task, lang, x, gates, ups):
    bf16, f32 = jnp.bfloat16, jnp.float32
    n_slots = task.shape[0] + lang.shape[0]
    tokens, width = x.shape
    part, cols = gates[0].shape
    padded = -(-n_slots // 8) * 8
    vmem = pl.BlockSpec(memory_space=pltpu.VMEM)
    hbm = pl.BlockSpec(memory_space=pl.ANY)
    pre = jax.ShapeDtypeStruct((tokens, cols), f32)
    rows = jax.ShapeDtypeStruct((len(EARLY), part, cols), bf16)
    return pl.pallas_call(
        early_kernel,
        out_shape=(pre, pre, jax.ShapeDtypeStruct((padded, BLK), jnp.int32), rows, rows),
        in_specs=[pl.BlockSpec(memory_space=pltpu.SMEM), vmem, vmem] + [hbm] * 7,
        out_specs=[vmem] * 3 + [hbm] * 2,
        scratch_shapes=[
            pltpu.VMEM(x.shape, bf16),
            pltpu.VMEM(rows.shape, bf16),
            pltpu.VMEM(rows.shape, bf16),
            pltpu.VMEM((n_slots, 2 * BLK, BLK), f32),
            pltpu.SMEM((padded, BLK), jnp.int32),
            pltpu.SMEM((width // BLK * cols // BLK,), jnp.int32),
            pltpu.SMEM((n_slots,), jnp.int32),
            pltpu.SemaphoreType.DMA((8,)),
            pltpu.SemaphoreType.DMA((6,)),
        ],
        compiler_params=pltpu.CompilerParams(vmem_limit_bytes=56 * MIB),
        cost_estimate=pl.CostEstimate(
            flops=3 * tokens * width * cols, bytes_accessed=18 * MIB, transcendentals=0
        ),
        name="early_step",
    )(info, task, lang, x, *gates, *ups)


def late_kernel(
    info_ref,
    cells_ref,
    cot_ref,
    task_ref,
    lang_ref,
    gate_pre,
    up_pre,
    x_hbm,
    xt_hbm,
    g2,
    u2,
    _step,
    d_gate,
    d_up,
    own_out,
    up_first,
    up_second,
    down_first,
    down_second,
    gate_out,
    up_out,
    x_ref,
    xt_ref,
    gate_m,
    up_m,
    acc,
    d_cols,
    task_out,
    first_ref,
    leader_ref,
    in_sems,
    out_sems,
):
    f32, bf16 = jnp.float32, jnp.bfloat16
    part = g2.shape[0]
    me = info_ref[0]
    start = pl.multiple_of(lax.rem(me + LATE, WAYS) * part, part)
    copies = [
        pltpu.make_async_copy(g2, gate_m, in_sems.at[0]),
        pltpu.make_async_copy(u2, up_m, in_sems.at[1]),
        pltpu.make_async_copy(x_hbm.at[:, pl.ds(start, part)], x_ref, in_sems.at[2]),
        pltpu.make_async_copy(xt_hbm, xt_ref, in_sems.at[3]),
    ]
    for c in copies:
        c.start()
    find_leaders(cells_ref, first_ref, leader_ref)
    copies[0].wait()
    copies[1].wait()
    compose(cells_ref, leader_ref, task_ref, lang_ref, acc, gate_m, up_m, start // BLK * 2)
    out_copies = [
        pltpu.make_async_copy(gate_m, gate_out, out_sems.at[0]),
        pltpu.make_async_copy(up_m, up_out, out_sems.at[1]),
    ]
    for copy in out_copies:
        copy.start()
    copies[2].wait()
    g = gate_pre[...] + jnp.dot(x_ref[...], gate_m[...], preferred_element_type=f32)
    u = up_pre[...] + jnp.dot(x_ref[...], up_m[...], preferred_element_type=f32)
    s = jax.nn.sigmoid(g)
    c = cot_ref[...].astype(f32)
    dg = (c * u * s * (1.0 + g * (1.0 - s))).astype(bf16)
    du = (c * g * s).astype(bf16)
    d_gate[...] = dg
    d_up[...] = du
    for h in range(2):
        d_cols[h, :, 0:BLK] = dg[:, h * BLK : (h + 1) * BLK]
        d_cols[h, :, BLK:] = du[:, h * BLK : (h + 1) * BLK]
    copies[3].wait()

    def task_step(i, carry):
        cell = jnp.maximum(cells_ref[i, 0], 0)
        row = pl.multiple_of(lax.shift_right_logical(cell, 1) * BLK, BLK)
        side = lax.bitwise_and(cell, 1)
        r = jnp.dot(xt_ref[pl.ds(row, BLK), :], d_cols[side], preferred_element_type=f32)
        r = r.astype(bf16)
        task_out[0, i] = r[0 : BLK // 2, 0:BLK]
        task_out[1, i] = r[BLK // 2 :, 0:BLK]
        task_out[2, i] = r[0 : BLK // 2, BLK:]
        task_out[3, i] = r[BLK // 2 :, BLK:]
        return carry

    n_task = task_ref.shape[0]
    half = n_task // 2
    q = [lax.rem(me + k, WAYS) for k in range(WAYS)]
    low, high = pl.ds(0, half), pl.ds(half, half)
    moves = (
        (
            (task_out.at[q[0], low], own_out.at[low]),
            (task_out.at[q[2], low], up_first.at[low]),
            (task_out.at[q[3], low], down_first.at[low]),
            (task_out.at[q[1], low], up_second),
        ),
        (
            (task_out.at[q[0], high], own_out.at[high]),
            (task_out.at[q[1], high], up_first.at[high]),
            (task_out.at[q[2], high], down_first.at[high]),
            (task_out.at[q[3], high], down_second),
        ),
    )
    for n in range(2):
        lax.fori_loop(n * half, (n + 1) * half, task_step, 0, unroll=8)
        for src, dst in moves[n]:
            copy = pltpu.make_async_copy(src, dst, out_sems.at[len(out_copies)])
            copy.start()
            out_copies.append(copy)
    for copy in out_copies:
        copy.wait()


def late_step(info, cells, cot, task, lang, gate_pre, up_pre, x, xt, gate, up, step):
    bf16, f32 = jnp.bfloat16, jnp.float32
    n_task, n_slots = task.shape[0], task.shape[0] + lang.shape[0]
    tokens, width = x.shape
    part, cols = gate.shape
    smem = pl.BlockSpec(memory_space=pltpu.SMEM)
    vmem = pl.BlockSpec(memory_space=pltpu.VMEM)
    hbm = pl.BlockSpec(memory_space=pl.ANY)
    return pl.pallas_call(
        late_kernel,
        out_shape=(
            *[jax.ShapeDtypeStruct((tokens, cols), bf16)] * 2,
            *[
                jax.ShapeDtypeStruct((n, BLK // 2, BLK), bf16)
                for n in (n_task, n_task, n_task // 2, n_task, n_task // 2)
            ],
            *[jax.ShapeDtypeStruct((part, cols), bf16)] * 2,
        ),
        in_specs=[smem] * 2 + [vmem] * 5 + [hbm] * 5,
        out_specs=[vmem] * 2 + [hbm] * 7,
        scratch_shapes=[
            pltpu.VMEM((tokens, part), bf16),
            pltpu.VMEM(xt.shape, bf16),
            pltpu.VMEM((part, cols), bf16),
            pltpu.VMEM((part, cols), bf16),
            pltpu.VMEM((n_slots, 2 * BLK, BLK), f32),
            pltpu.VMEM((2, tokens, 2 * BLK), bf16),
            pltpu.VMEM((WAYS, n_task, BLK // 2, BLK), bf16),
            pltpu.SMEM((width // BLK * cols // BLK,), jnp.int32),
            pltpu.SMEM((n_slots,), jnp.int32),
            pltpu.SemaphoreType.DMA((4,)),
            pltpu.SemaphoreType.DMA((10,)),
        ],
        compiler_params=pltpu.CompilerParams(vmem_limit_bytes=56 * MIB),
        cost_estimate=pl.CostEstimate(
            flops=3 * tokens * width * cols, bytes_accessed=14 * MIB, transcendentals=tokens * cols
        ),
        name="late_step",
    )(info, cells, cot, task, lang, gate_pre, up_pre, x, xt, gate, up, step)


def back_kernel(
    info_ref,
    d_gate,
    d_up,
    gate_early,
    up_early,
    gate_late,
    up_late,
    _mark,
    keep_out,
    give_out,
    gate_m,
    up_m,
    main_out,
    in_sems,
    out_sems,
):
    f32, bf16 = jnp.float32, jnp.bfloat16
    me, core, lang = info_ref[0], info_ref[1], info_ref[2]
    copies = []
    for n in range(WAYS):
        gate, up = (gate_early.at[n], up_early.at[n]) if n < len(EARLY) else (gate_late, up_late)
        copies.append(
            (
                pltpu.make_async_copy(gate, gate_m.at[n], in_sems.at[2 * n]),
                pltpu.make_async_copy(up, up_m.at[n], in_sems.at[2 * n + 1]),
            )
        )
    for pair in copies:
        for c in pair:
            c.start()
    last = (((1,), (1,)), ((), ()))
    per = keep_out.shape[0] // WAYS
    out_copies = []
    for n, k in enumerate((*EARLY, LATE)):
        for c in copies[n]:
            c.wait()

        def backward(m, carry, n=n):
            rows = pl.ds(pl.multiple_of(m * 2 * BLK, 2 * BLK), 2 * BLK)
            r = lax.dot_general(d_gate[...], gate_m[n, rows, :], last, preferred_element_type=f32)
            r += lax.dot_general(d_up[...], up_m[n, rows, :], last, preferred_element_type=f32)
            r = r.astype(bf16)
            main_out[0, n * per + m] = r[:, 0:BLK]
            main_out[1, n * per + m] = r[:, BLK:]
            return carry

        lax.fori_loop(0, per, backward, 0, unroll=4)
        src = pl.ds(n * per, per)
        dst = pl.ds(lax.rem(me + k + WAYS - lang, WAYS) * per, per)
        for way, out in ((1 - core, give_out), (core, keep_out)):
            copy = pltpu.make_async_copy(
                main_out.at[way, src], out.at[dst], out_sems.at[len(out_copies)]
            )
            copy.start()
            out_copies.append(copy)
    for copy in out_copies:
        copy.wait()


def back_step(info, d_gate, d_up, gate_early, up_early, gate_late, up_late, mark):
    bf16 = jnp.bfloat16
    tokens, cols = d_gate.shape
    part = gate_late.shape[0]
    pairs = WAYS * part // (2 * BLK)
    vmem = pl.BlockSpec(memory_space=pltpu.VMEM)
    hbm = pl.BlockSpec(memory_space=pl.ANY)
    main = jax.ShapeDtypeStruct((pairs, tokens, BLK), bf16)
    return pl.pallas_call(
        back_kernel,
        out_shape=(main, main),
        in_specs=[pl.BlockSpec(memory_space=pltpu.SMEM), vmem, vmem] + [hbm] * 5,
        out_specs=[hbm] * 2,
        scratch_shapes=[
            pltpu.VMEM((WAYS, part, cols), bf16),
            pltpu.VMEM((WAYS, part, cols), bf16),
            pltpu.VMEM((2, pairs, tokens, BLK), bf16),
            pltpu.SemaphoreType.DMA((8,)),
            pltpu.SemaphoreType.DMA((8,)),
        ],
        compiler_params=pltpu.CompilerParams(vmem_limit_bytes=56 * MIB),
        cost_estimate=pl.CostEstimate(
            flops=4 * tokens * WAYS * part * cols, bytes_accessed=12 * MIB, transcendentals=0
        ),
        name="back_step",
    )(info, d_gate, d_up, gate_early, up_early, gate_late, up_late, mark)


def pace_kernel(*refs):
    refs[-1][...] = jnp.zeros_like(refs[-1])


def pace(*arrays, flops=10**11):
    return pl.pallas_call(
        pace_kernel,
        out_shape=jax.ShapeDtypeStruct((8, BLK), jnp.float32),
        in_specs=[pl.BlockSpec(memory_space=pl.ANY)] * len(arrays),
        out_specs=pl.BlockSpec(memory_space=pltpu.VMEM),
        compiler_params=pltpu.CompilerParams(vmem_limit_bytes=MIB),
        cost_estimate=pl.CostEstimate(flops=flops, bytes_accessed=4096, transcendentals=0),
        name="pace",
    )(*arrays)


def ring_first(axis, up_first, down_first):
    return (
        lax.ppermute(up_first, axis, ring(axis, 1)),
        lax.ppermute(down_first, axis, ring(axis, -1)),
    )


def ring_rest(axis, own, up_second, down_second, from_left, from_right):
    f32, bf16 = jnp.float32, jnp.bfloat16
    half = own.shape[0] // 2
    up_second = (up_second.astype(f32) + from_left[:half].astype(f32)).astype(bf16)
    down_second = (down_second.astype(f32) + from_right[half:].astype(f32)).astype(bf16)
    low_left = lax.ppermute(up_second, axis, ring(axis, 1))
    high_right = lax.ppermute(down_second, axis, ring(axis, -1))
    low = own[:half].astype(f32) + low_left.astype(f32) + from_right[:half].astype(f32)
    high = own[half:].astype(f32) + high_right.astype(f32) + from_left[half:].astype(f32)
    return jnp.concatenate([low, high], axis=0).astype(bf16)


def on_device(
    tokens_in,
    cotangent,
    gate_base,
    up_base,
    lang_delta,
    lang_cell,
    group_lang,
    task_delta,
    task_slab,
    task_cell,
):
    f32, bf16 = jnp.float32, jnp.bfloat16
    fsdp = ("z", "core")
    n_lang, n_z, n_core, n_dp = (lax.axis_size(a) for a in ("lang", "z", "core", "dp"))
    n_fsdp = n_z * n_core
    language = group_lang[0]
    my_lang, my_core, my_dp = (lax.axis_index(a) for a in ("lang", "core", "dp"))
    held = task_delta.shape[0]

    gate_left = lax.ppermute(gate_base, "dp", ring("dp", 1))
    up_right = lax.ppermute(up_base, "dp", ring("dp", -1))
    up_left = lax.ppermute(up_base, "dp", ring("dp", 1))
    gate_right = lax.ppermute(gate_base, "dp", ring("dp", -1))
    target = task_slab[:, 0]
    send_task = place(target, task_cell[:, 0], task_delta.reshape(held, 2 * BLK, BLK), n_fsdp)
    got_task = lax.all_to_all(send_task, fsdp, split_axis=0, concat_axis=0, tiled=True)
    lang_tiles = lang_delta[0, 0].reshape(lang_delta.shape[2:4] + (2 * BLK, BLK))
    with_cell = with_cells(lang_tiles, lang_cell[0, 0])
    send_lang = [
        lax.dynamic_index_in_dim(with_cell, lax.rem(my_lang + k, n_lang), 0, keepdims=False)
        for k in range(n_lang)
    ]
    tokens_t = tokens_in.T
    step = pace(gate_left, gate_right, up_left, up_right, tokens_t, *send_lang)
    gate_on, up_on, step, *send_lang = lax.optimization_barrier(
        (gate_left, up_right, step, *send_lang)
    )
    gate_far = lax.ppermute(gate_on, "dp", ring("dp", 1))
    up_far = lax.ppermute(up_on, "dp", ring("dp", -1))
    choice = lax.rem(my_lang - language + n_lang, n_lang)
    chosen = send_lang[0]
    for k in range(1, n_lang):
        chosen = jnp.where(choice == k, lax.ppermute(send_lang[k], "lang", ring("lang", k)), chosen)

    info = jnp.stack([my_dp, my_core, my_lang]).astype(jnp.int32)
    gate_pre, up_pre, cells, gate_early, up_early = early_step(
        info,
        got_task,
        chosen,
        tokens_in,
        (gate_base, gate_left, gate_right),
        (up_base, up_left, up_right),
    )
    d_gate, d_up, *pieces, gate_late, up_late = late_step(
        info,
        cells,
        cotangent,
        got_task,
        chosen,
        gate_pre,
        up_pre,
        tokens_in,
        tokens_t,
        gate_far,
        up_far,
        step,
    )
    task_first = ring_first("dp", pieces[1], pieces[3])
    keep, give = back_step(
        info,
        d_gate,
        d_up,
        gate_early,
        up_early,
        gate_late,
        up_late,
        pace(pieces[1], pieces[3]),
    )
    got = lax.ppermute(give, "core", ring("core", 1))


    def both(first, last):
        first, last = first * n_z // 2, last * n_z // 2
        return (keep[first:last].astype(f32) + got[first:last].astype(f32)).astype(bf16)

    main_up = jnp.concatenate([both(4, 5), both(3, 4)], axis=0)
    main_down = jnp.concatenate([both(6, 7), both(5, 6)], axis=0)
    main_first = ring_first("lang", main_up, main_down)
    mark = pace(main_up, main_down, flops=0)
    task_left, task_right, mark = lax.optimization_barrier((*task_first, mark))
    tsum = ring_rest("dp", pieces[0], pieces[2], pieces[4], task_left, task_right)
    over_lang = ring_rest("lang", both(0, 2), both(2, 3), both(7, 8), *main_first)
    mark = pace(*main_first, mark, flops=0)
    back = lax.all_to_all(tsum, fsdp, split_axis=0, concat_axis=0, tiled=True)
    mine = take_own(target, back, mark)
    others = [lax.ppermute(mine, "dp", ring("dp", -k)) for k in (2, 1, 3)]
    stacked = jnp.stack([mine, others[1], others[0], others[2]], axis=0)
    stacked = jnp.stack(
        [
            lax.dynamic_index_in_dim(stacked, lax.rem(q - my_dp + n_dp, n_dp), 0, keepdims=False)
            for q in range(n_dp)
        ],
        axis=1,
    )
    task_grad = stacked.astype(f32).reshape(task_delta.shape)

    over_z = lax.all_to_all(over_lang, "z", split_axis=0, concat_axis=0, tiled=True)
    grad_input = jnp.sum(over_z.astype(f32), axis=0).astype(bf16)
    return (grad_input, task_grad)


def solution(mesh):
    lang, fsdp, dp = (mesh.shape[a] for a in ("lang", "fsdp", "dp"))
    fine = Mesh(mesh.devices.reshape(lang, fsdp // 2, 2, dp), ("lang", "z", "core", "dp"))
    cols = ("lang", "z", "core")
    return jax.shard_map(
        on_device,
        mesh=fine,
        in_specs=(
            P("dp", None),
            P("dp", cols),
            P("dp", cols),
            P("dp", cols),
            P("lang", ("z", "core"), None, None, None),
            P("lang", ("z", "core"), None, None),
            P("dp"),
            P(cols, None),
            P(cols, None),
            P(cols, None),
        ),
        out_specs=(P("dp", cols), P(cols, None)),
        check_vma=False,
    )
```

```python
import jax
import jax.numpy as jnp
from jax import lax
from jax.experimental import pallas as pl
from jax.experimental.pallas import tpu as pltpu
from jax.sharding import Mesh, PartitionSpec as P

BLK = 128
CAP = 2
PAD = 16
MIB = 1024 * 1024


def ring(axis, step):
    n = lax.axis_size(axis)
    return [(i, (i + step) % n) for i in range(n)]


def with_cells(tiles, cells):
    rows = jnp.broadcast_to(cells.astype(jnp.bfloat16)[..., None, None], cells.shape + (PAD, BLK))
    return jnp.concatenate([tiles, rows], axis=-2)


def place_kernel(slab_ref, cells_ref, tiles_ref, out_ref, used_ref):
    def clear(i, carry):
        out_ref[i, 2 * BLK :, :] = jnp.full((PAD, BLK), -1.0, jnp.bfloat16)
        return carry

    lax.fori_loop(0, out_ref.shape[0], clear, 0)

    def unused(i, carry):
        used_ref[i] = 0
        return carry

    lax.fori_loop(0, used_ref.shape[0], unused, 0)

    def put(i, carry):
        slab = slab_ref[i]
        slot = slab * CAP + used_ref[slab]
        used_ref[slab] += 1
        out_ref[slot, 0 : 2 * BLK, :] = tiles_ref[i]
        out_ref[slot, 2 * BLK :, :] = jnp.full(
            (PAD, BLK), cells_ref[i].astype(jnp.float32), jnp.float32
        ).astype(jnp.bfloat16)
        return carry

    lax.fori_loop(0, tiles_ref.shape[0], put, 0)


def place(slab, cells, tiles, n_slabs):
    smem = pl.BlockSpec(memory_space=pltpu.SMEM)
    vmem = pl.BlockSpec(memory_space=pltpu.VMEM)
    return pl.pallas_call(
        place_kernel,
        out_shape=jax.ShapeDtypeStruct((n_slabs * CAP, 2 * BLK + PAD, BLK), jnp.bfloat16),
        in_specs=[smem, smem, vmem],
        out_specs=vmem,
        scratch_shapes=[pltpu.SMEM((n_slabs,), jnp.int32)],
        compiler_params=pltpu.CompilerParams(vmem_limit_bytes=16 * MIB),
        cost_estimate=pl.CostEstimate(flops=0, bytes_accessed=3 * MIB, transcendentals=0),
        name="place",
    )(slab, cells, tiles)


def take_own_kernel(slab_ref, back_ref, _mark, out_ref, used_ref):
    def unused(i, carry):
        used_ref[i] = 0
        return carry

    lax.fori_loop(0, used_ref.shape[0], unused, 0)

    def take(i, carry):
        slab = slab_ref[i]
        out_ref[i] = back_ref[slab * CAP + used_ref[slab]]
        used_ref[slab] += 1
        return carry

    lax.fori_loop(0, out_ref.shape[0], take, 0)


def take_own(slab, back, mark):
    smem = pl.BlockSpec(memory_space=pltpu.SMEM)
    vmem = pl.BlockSpec(memory_space=pltpu.VMEM)
    return pl.pallas_call(
        take_own_kernel,
        out_shape=jax.ShapeDtypeStruct(slab.shape + back.shape[1:], back.dtype),
        in_specs=[smem, vmem, pl.BlockSpec(memory_space=pl.ANY)],
        out_specs=vmem,
        scratch_shapes=[pltpu.SMEM((back.shape[0] // CAP,), jnp.int32)],
        compiler_params=pltpu.CompilerParams(vmem_limit_bytes=4 * MIB),
        cost_estimate=pl.CostEstimate(flops=0, bytes_accessed=MIB, transcendentals=0),
        name="take_own",
    )(slab, back, mark)


def device_kernel(
    n_task,
    info_ref,
    cot_ref,
    _step,
    task_hbm,
    lang_hbm,
    x_hbm,
    xt_hbm,
    g0,
    g1,
    g2,
    g3,
    u0,
    u1,
    u2,
    u3,
    own_out,
    far_low,
    far_high,
    right_low,
    right_high,
    left_low,
    left_high,
    keep_out,
    give_out,
    tiles,
    x_ref,
    xt_ref,
    gate_m,
    up_m,
    acc,
    gate_pre,
    up_pre,
    d_gate,
    d_up,
    d_cols,
    task_out,
    main_out,
    cell_rows,
    cells_ref,
    first_ref,
    leader_ref,
    shared_ref,
    list_ref,
    count_ref,
    in_sems,
    out_sems,
):
    f32, bf16 = jnp.float32, jnp.bfloat16
    ways = 4
    part = g0.shape[0]
    me, core, lang = info_ref[0], info_ref[1], info_ref[2]
    order = (0, 3, 1, 2)
    x_copy = pltpu.make_async_copy(x_hbm, x_ref, in_sems.at[8])
    xt_copy = pltpu.make_async_copy(xt_hbm, xt_ref, in_sems.at[9])
    n_slots = tiles.shape[0]
    tile_copies = (
        pltpu.make_async_copy(task_hbm, tiles.at[pl.ds(0, n_task)], in_sems.at[11]),
        pltpu.make_async_copy(lang_hbm, tiles.at[pl.ds(n_task, n_slots - n_task)], in_sems.at[12]),
    )
    for c in tile_copies:
        c.start()
    copies, starts = {}, {}
    for k, (g, u) in enumerate(((g0, u0), (g1, u1), (g2, u2), (g3, u3))):
        starts[k] = pl.multiple_of(lax.rem(me + k, ways) * part, part)
        to = pl.ds(starts[k], part)
        copies[k] = (
            pltpu.make_async_copy(g, gate_m.at[to], in_sems.at[k]),
            pltpu.make_async_copy(u, up_m.at[to], in_sems.at[ways + k]),
        )
    for k in order:
        for c in copies[k]:
            c.start()
        if k == order[0]:
            x_copy.start()
    xt_copy.start()

    def no_first(i, carry):
        first_ref[i] = -1
        return carry

    lax.fori_loop(0, first_ref.shape[0], no_first, 0)
    for p in range(ways):
        count_ref[p] = 0
    gate_pre[...] = jnp.zeros_like(gate_pre)
    up_pre[...] = jnp.zeros_like(up_pre)
    for c in tile_copies:
        c.wait()
    for i in range(n_slots):
        row = tiles[i, 2 * BLK : 2 * BLK + PAD, :].astype(f32).astype(jnp.int32)
        cell_rows[i : i + 1, :] = row[0:1]
    cell_copy = pltpu.make_async_copy(cell_rows, cells_ref, in_sems.at[10])
    cell_copy.start()
    cell_copy.wait()
    part_cells = 2 * part // BLK

    def sort_in(s, carry):
        cell = cells_ref[s, 0]

        @pl.when(cell >= 0)
        def _():
            known = first_ref[cell]
            new = known < 0
            lead = jnp.where(new, s, known)
            first_ref[cell] = lead
            leader_ref[s] = lead
            shared_ref[lead] = jnp.where(new, 0, 1)
            p = lax.div(cell, part_cells)
            list_ref[p * n_slots + count_ref[p]] = s
            count_ref[p] += 1

        return carry

    lax.fori_loop(0, n_slots, sort_in, 0)

    def spot(cell):
        row = pl.multiple_of(lax.shift_right_logical(cell, 1) * BLK, BLK)
        col = pl.multiple_of(lax.bitwise_and(cell, 1) * BLK, BLK)
        return pl.ds(row, BLK), pl.ds(col, BLK)

    depth = 1024
    for k in order:
        for c in copies[k]:
            c.wait()
        p = lax.rem(me + k, ways)

        def add(n, carry, p=p):
            s = list_ref[p * n_slots + n]
            at = spot(cells_ref[s, 0])
            lead = leader_ref[s]

            @pl.when((lead == s) & (shared_ref[s] == 0))
            def _():
                gate_m[at] = (gate_m[at].astype(f32) + tiles[s, 0:BLK].astype(f32)).astype(bf16)
                up_m[at] = (up_m[at].astype(f32) + tiles[s, BLK : 2 * BLK].astype(f32)).astype(bf16)

            @pl.when((lead == s) & (shared_ref[s] != 0))
            def _():
                acc[s, 0:BLK] = gate_m[at].astype(f32) + tiles[s, 0:BLK].astype(f32)
                acc[s, BLK:] = up_m[at].astype(f32) + tiles[s, BLK : 2 * BLK].astype(f32)

            @pl.when(lead != s)
            def _():
                acc[lead] += tiles[s, 0 : 2 * BLK].astype(f32)

            return carry

        def write_back(n, carry, p=p):
            s = list_ref[p * n_slots + n]

            @pl.when((leader_ref[s] == s) & (shared_ref[s] != 0))
            def _():
                at = spot(cells_ref[s, 0])
                gate_m[at] = acc[s, 0:BLK].astype(bf16)
                up_m[at] = acc[s, BLK:].astype(bf16)

            return carry

        lax.fori_loop(0, count_ref[p], add, 0)
        lax.fori_loop(0, count_ref[p], write_back, 0)
        if k == order[0]:
            x_copy.wait()
        for step in range(part // depth):
            rows = pl.ds(pl.multiple_of(starts[k] + step * depth, depth), depth)
            xk = x_ref[:, rows]
            gate_pre[...] += jnp.dot(xk, gate_m[rows, :], preferred_element_type=f32)
            up_pre[...] += jnp.dot(xk, up_m[rows, :], preferred_element_type=f32)

    g, u = gate_pre[...], up_pre[...]
    s = jax.nn.sigmoid(g)
    c = cot_ref[...].astype(f32)
    dg = (c * u * s * (1.0 + g * (1.0 - s))).astype(bf16)
    du = (c * g * s).astype(bf16)
    d_gate[...] = dg
    d_up[...] = du
    for h in range(2):
        d_cols[h, :, 0:BLK] = dg[:, h * BLK : (h + 1) * BLK]
        d_cols[h, :, BLK:] = du[:, h * BLK : (h + 1) * BLK]
    xt_copy.wait()

    def task_step(i, carry):
        cell = jnp.maximum(cells_ref[i, 0], 0)
        row = pl.multiple_of(lax.shift_right_logical(cell, 1) * BLK, BLK)
        side = lax.bitwise_and(cell, 1)
        r = jnp.dot(xt_ref[pl.ds(row, BLK), :], d_cols[side], preferred_element_type=f32)
        r = r.astype(bf16)
        task_out[0, i] = r[0 : BLK // 2, 0:BLK]
        task_out[1, i] = r[BLK // 2 :, 0:BLK]
        task_out[2, i] = r[0 : BLK // 2, BLK:]
        task_out[3, i] = r[BLK // 2 :, BLK:]
        return carry

    lax.fori_loop(0, n_task, task_step, 0, unroll=8)
    q = [lax.rem(me + k, ways) for k in range(ways)]
    half = n_task // 2
    low, high = pl.ds(0, half), pl.ds(half, half)
    moves = [
        (task_out.at[q[2], low], far_low),
        (task_out.at[q[2], high], far_high),
        (task_out.at[q[1], high], right_high),
        (task_out.at[q[3], low], left_low),
        (task_out.at[q[1], low], right_low),
        (task_out.at[q[3], high], left_high),
        (task_out.at[q[0]], own_out),
    ]
    out_copies = [
        pltpu.make_async_copy(src, dst, out_sems.at[n]) for n, (src, dst) in enumerate(moves)
    ]
    for copy in out_copies:
        copy.start()

    last = (((1,), (1,)), ((), ()))
    per = keep_out.shape[0] // ways

    def backward(m, carry):
        rows = pl.ds(pl.multiple_of(m * 2 * BLK, 2 * BLK), 2 * BLK)
        r = lax.dot_general(d_gate[...], gate_m[rows, :], last, preferred_element_type=f32)
        r += lax.dot_general(d_up[...], up_m[rows, :], last, preferred_element_type=f32)
        r = r.astype(bf16)
        main_out[0, m] = r[:, 0:BLK]
        main_out[1, m] = r[:, BLK:]
        return carry

    for n in range(ways):
        lax.fori_loop(n * per, (n + 1) * per, backward, 0, unroll=4)
        src = pl.ds(n * per, per)
        dst = pl.ds(lax.rem(n + ways - lang, ways) * per, per)
        for way, out in ((core, keep_out), (1 - core, give_out)):
            copy = pltpu.make_async_copy(
                main_out.at[way, src], out.at[dst], out_sems.at[len(out_copies)]
            )
            copy.start()
            out_copies.append(copy)
    for copy in out_copies:
        copy.wait()


def device_step(info, cot, task, lang, x, xt, gates, ups, step):
    bf16, f32 = jnp.bfloat16, jnp.float32
    n_task, n_slots = task.shape[0], task.shape[0] + lang.shape[0]
    tokens, width = x.shape
    cols = cot.shape[1]
    padded = -(-n_slots // 8) * 8
    vmem = pl.BlockSpec(memory_space=pltpu.VMEM)
    hbm = pl.BlockSpec(memory_space=pl.ANY)
    pairs = width // (2 * BLK)
    main = jax.ShapeDtypeStruct((pairs, tokens, BLK), bf16)
    return pl.pallas_call(
        lambda *refs: device_kernel(n_task, *refs),
        out_shape=(
            *[
                jax.ShapeDtypeStruct((n, BLK // 2, BLK), bf16)
                for n in (n_task, *[n_task // 2] * 6)
            ],
            main,
            main,
        ),
        in_specs=[pl.BlockSpec(memory_space=pltpu.SMEM)] + [vmem] * 2 + [hbm] * 12,
        out_specs=[hbm] * 9,
        scratch_shapes=[
            pltpu.VMEM((n_slots, *task.shape[1:]), bf16),
            pltpu.VMEM(x.shape, bf16),
            pltpu.VMEM(xt.shape, bf16),
            pltpu.VMEM((width, cols), bf16),
            pltpu.VMEM((width, cols), bf16),
            pltpu.VMEM((n_slots, 2 * BLK, BLK), f32),
            pltpu.VMEM((tokens, cols), f32),
            pltpu.VMEM((tokens, cols), f32),
            pltpu.VMEM((tokens, cols), bf16),
            pltpu.VMEM((tokens, cols), bf16),
            pltpu.VMEM((2, tokens, 2 * BLK), bf16),
            pltpu.VMEM((4, n_task, BLK // 2, BLK), bf16),
            pltpu.VMEM((2, pairs, tokens, BLK), bf16),
            pltpu.VMEM((padded, BLK), jnp.int32),
            pltpu.SMEM((padded, BLK), jnp.int32),
            pltpu.SMEM((width // BLK * cols // BLK,), jnp.int32),
            pltpu.SMEM((n_slots,), jnp.int32),
            pltpu.SMEM((n_slots,), jnp.int32),
            pltpu.SMEM((4 * n_slots,), jnp.int32),
            pltpu.SMEM((4,), jnp.int32),
            pltpu.SemaphoreType.DMA((13,)),
            pltpu.SemaphoreType.DMA((15,)),
        ],
        compiler_params=pltpu.CompilerParams(vmem_limit_bytes=56 * MIB),
        cost_estimate=pl.CostEstimate(
            flops=10 * tokens * width * cols, bytes_accessed=24 * MIB, transcendentals=tokens * cols
        ),
        name="device_step",
    )(info, cot, step, task, lang, x, xt, *gates, *ups)


def pace_kernel(*refs):
    refs[-1][...] = jnp.zeros_like(refs[-1])


def pace(*arrays, flops=10**11, vmem=MIB):
    return pl.pallas_call(
        pace_kernel,
        out_shape=jax.ShapeDtypeStruct((8, BLK), jnp.float32),
        in_specs=[pl.BlockSpec(memory_space=pl.ANY)] * len(arrays),
        out_specs=pl.BlockSpec(memory_space=pltpu.VMEM),
        compiler_params=pltpu.CompilerParams(vmem_limit_bytes=vmem),
        cost_estimate=pl.CostEstimate(flops=flops, bytes_accessed=4096, transcendentals=0),
        name="pace",
    )(*arrays)


def ring_first(axis, up_first, down_first):
    return (
        lax.ppermute(up_first, axis, ring(axis, 1)),
        lax.ppermute(down_first, axis, ring(axis, -1)),
    )


def ring_rest(axis, own, up_second, down_second, from_left, from_right):
    f32, bf16 = jnp.float32, jnp.bfloat16
    half = own.shape[0] // 2
    up_second = (up_second.astype(f32) + from_left[:half].astype(f32)).astype(bf16)
    down_second = (down_second.astype(f32) + from_right[half:].astype(f32)).astype(bf16)
    low_left = lax.ppermute(up_second, axis, ring(axis, 1))
    high_right = lax.ppermute(down_second, axis, ring(axis, -1))
    low = own[:half].astype(f32) + low_left.astype(f32) + from_right[:half].astype(f32)
    high = own[half:].astype(f32) + high_right.astype(f32) + from_left[half:].astype(f32)
    return jnp.concatenate([low, high], axis=0).astype(bf16)


def on_device(
    tokens_in,
    cotangent,
    gate_base,
    up_base,
    lang_delta,
    lang_cell,
    group_lang,
    task_delta,
    task_slab,
    task_cell,
):
    f32, bf16 = jnp.float32, jnp.bfloat16
    fsdp = ("z", "core")
    n_lang, n_z, n_core, n_dp = (lax.axis_size(a) for a in ("lang", "z", "core", "dp"))
    n_fsdp = n_z * n_core
    language = group_lang[0]
    my_lang, my_core, my_dp = (lax.axis_index(a) for a in ("lang", "core", "dp"))
    held = task_delta.shape[0]

    gate_left = lax.ppermute(gate_base, "dp", ring("dp", 1))
    up_right = lax.ppermute(up_base, "dp", ring("dp", -1))
    up_left = lax.ppermute(up_base, "dp", ring("dp", 1))
    gate_right = lax.ppermute(gate_base, "dp", ring("dp", -1))
    step = pace(gate_left, gate_right, up_left, up_right, vmem=60 * MIB)
    gate_on, up_on, step = lax.optimization_barrier((gate_left, up_right, step))
    gate_far = lax.ppermute(gate_on, "dp", ring("dp", 1))
    up_far = lax.ppermute(up_on, "dp", ring("dp", -1))

    target = task_slab[:, 0]
    send_task = place(target, task_cell[:, 0], task_delta.reshape(held, 2 * BLK, BLK), n_fsdp)
    got_task = lax.all_to_all(send_task, fsdp, split_axis=0, concat_axis=0, tiled=True)
    lang_tiles = lang_delta[0, 0].reshape(lang_delta.shape[2:4] + (2 * BLK, BLK))
    send_lang = with_cells(lang_tiles, lang_cell[0, 0])
    pick = lax.rem(my_lang - language + n_lang, n_lang)
    chosen = None
    for k in range(n_lang):
        piece = lax.dynamic_index_in_dim(send_lang, lax.rem(my_lang + k, n_lang), 0, keepdims=False)
        if k:
            piece = lax.ppermute(piece, "lang", ring("lang", k))
        chosen = piece if chosen is None else jnp.where(pick == k, piece, chosen)

    *pieces, keep, give = device_step(
        jnp.stack([my_dp, my_core, my_lang]).astype(jnp.int32),
        cotangent,
        got_task,
        chosen,
        tokens_in,
        tokens_in.T,
        (gate_base, gate_right, gate_far, gate_left),
        (up_base, up_right, up_far, up_left),
        step,
    )
    got = lax.ppermute(give, "core", ring("core", 1))
    own, far_low, far_high, right_low, right_high, left_low, left_high = pieces
    far_up = lax.ppermute(far_low, "dp", ring("dp", 1))
    far_down = lax.ppermute(far_high, "dp", ring("dp", -1))
    high_up = lax.ppermute(right_high, "dp", ring("dp", 1))
    low_down = lax.ppermute(left_low, "dp", ring("dp", -1))

    def both(first, last):
        first, last = first * n_z // 2, last * n_z // 2
        return (keep[first:last].astype(f32) + got[first:last].astype(f32)).astype(bf16)

    main_up = jnp.concatenate([both(4, 5), both(3, 4)], axis=0)
    main_down = jnp.concatenate([both(6, 7), both(5, 6)], axis=0)
    main_first = ring_first("lang", main_up, main_down)
    mark = pace(main_up, main_down)
    far_up, far_down, mark = lax.optimization_barrier((far_up, far_down, mark))
    low_up = (right_low.astype(f32) + far_up.astype(f32)).astype(bf16)
    high_down = (left_high.astype(f32) + far_down.astype(f32)).astype(bf16)
    low_up = lax.ppermute(low_up, "dp", ring("dp", 1))
    high_down = lax.ppermute(high_down, "dp", ring("dp", -1))
    half = own.shape[0] // 2
    low = own[:half].astype(f32) + low_up.astype(f32) + low_down.astype(f32)
    high = own[half:].astype(f32) + high_up.astype(f32) + high_down.astype(f32)
    tsum = jnp.concatenate([low, high], axis=0).astype(bf16)
    over_lang = ring_rest("lang", both(0, 2), both(2, 3), both(7, 8), *main_first)
    mark = pace(*main_first, mark, flops=0)
    back = lax.all_to_all(tsum, fsdp, split_axis=0, concat_axis=0, tiled=True)
    mine = take_own(target, back, mark).reshape(held, -1)
    far, right, left = [lax.ppermute(mine, "dp", ring("dp", -k)) for k in (2, 1, 3)]
    stacked = jnp.stack([mine, right, far, left], axis=0)
    task_grad = jnp.concatenate(
        [
            lax.dynamic_index_in_dim(stacked, lax.rem(q - my_dp + n_dp, n_dp), 0, keepdims=False)
            for q in range(n_dp)
        ],
        axis=1,
    ).astype(f32)

    over_z = lax.all_to_all(over_lang, "z", split_axis=0, concat_axis=0, tiled=True)
    grad_input = jnp.sum(over_z.astype(f32), axis=0).astype(bf16)
    return (grad_input, task_grad)


def solution(mesh):
    lang, fsdp, dp = (mesh.shape[a] for a in ("lang", "fsdp", "dp"))
    fine = Mesh(mesh.devices.reshape(lang, fsdp // 2, 2, dp), ("lang", "z", "core", "dp"))
    cols = ("lang", "z", "core")
    return jax.shard_map(
        on_device,
        mesh=fine,
        in_specs=(
            P("dp", None),
            P("dp", cols),
            P("dp", cols),
            P("dp", cols),
            P("lang", ("z", "core"), None, None, None),
            P("lang", ("z", "core"), None, None),
            P("dp"),
            P(cols, None),
            P(cols, None),
            P(cols, None),
        ),
        out_specs=(P("dp", cols), P(cols, None)),
        check_vma=False,
    )
```

```python
import jax
import jax.numpy as jnp
from jax import lax
from jax.experimental import pallas as pl
from jax.experimental.pallas import tpu as pltpu
from jax.sharding import Mesh, PartitionSpec as P

BLK = 128
CAP = 2
PAD = 16
MIB = 1024 * 1024


def ring(axis, step):
    n = lax.axis_size(axis)
    return [(i, (i + step) % n) for i in range(n)]


def with_cells(tiles, cells):
    rows = jnp.broadcast_to(cells.astype(jnp.bfloat16)[..., None, None], cells.shape + (PAD, BLK))
    return jnp.concatenate([tiles, rows], axis=-2)


def place_kernel(slab_ref, cells_ref, tiles_ref, out_ref, used_ref):
    def clear(i, carry):
        out_ref[i, 2 * BLK :, :] = jnp.full((PAD, BLK), -1.0, jnp.bfloat16)
        return carry

    lax.fori_loop(0, out_ref.shape[0], clear, 0)

    def unused(i, carry):
        used_ref[i] = 0
        return carry

    lax.fori_loop(0, used_ref.shape[0], unused, 0)

    def put(i, carry):
        slab = slab_ref[i]
        slot = slab * CAP + used_ref[slab]
        used_ref[slab] += 1
        out_ref[slot, 0 : 2 * BLK, :] = tiles_ref[i]
        out_ref[slot, 2 * BLK :, :] = jnp.full(
            (PAD, BLK), cells_ref[i].astype(jnp.float32), jnp.float32
        ).astype(jnp.bfloat16)
        return carry

    lax.fori_loop(0, tiles_ref.shape[0], put, 0)


def place(slab, cells, tiles, n_slabs):
    smem = pl.BlockSpec(memory_space=pltpu.SMEM)
    vmem = pl.BlockSpec(memory_space=pltpu.VMEM)
    return pl.pallas_call(
        place_kernel,
        out_shape=jax.ShapeDtypeStruct((n_slabs * CAP, 2 * BLK + PAD, BLK), jnp.bfloat16),
        in_specs=[smem, smem, vmem],
        out_specs=vmem,
        scratch_shapes=[pltpu.SMEM((n_slabs,), jnp.int32)],
        compiler_params=pltpu.CompilerParams(vmem_limit_bytes=16 * MIB),
        cost_estimate=pl.CostEstimate(flops=0, bytes_accessed=3 * MIB, transcendentals=0),
        name="place",
    )(slab, cells, tiles)


def take_own_kernel(slab_ref, back_ref, _mark, out_ref, used_ref):
    def unused(i, carry):
        used_ref[i] = 0
        return carry

    lax.fori_loop(0, used_ref.shape[0], unused, 0)

    def take(i, carry):
        slab = slab_ref[i]
        out_ref[i] = back_ref[slab * CAP + used_ref[slab]]
        used_ref[slab] += 1
        return carry

    lax.fori_loop(0, out_ref.shape[0], take, 0)


def take_own(slab, back, mark):
    smem = pl.BlockSpec(memory_space=pltpu.SMEM)
    vmem = pl.BlockSpec(memory_space=pltpu.VMEM)
    return pl.pallas_call(
        take_own_kernel,
        out_shape=jax.ShapeDtypeStruct(slab.shape + back.shape[1:], back.dtype),
        in_specs=[smem, vmem, pl.BlockSpec(memory_space=pl.ANY)],
        out_specs=vmem,
        scratch_shapes=[pltpu.SMEM((back.shape[0] // CAP,), jnp.int32)],
        compiler_params=pltpu.CompilerParams(vmem_limit_bytes=4 * MIB),
        cost_estimate=pl.CostEstimate(flops=0, bytes_accessed=MIB, transcendentals=0),
        name="take_own",
    )(slab, back, mark)


def device_kernel(
    n_task,
    info_ref,
    cot_ref,
    _step,
    task_in,
    lang_hbm,
    x_hbm,
    xt_hbm,
    g0,
    g1,
    g2,
    g3,
    u0,
    u1,
    u2,
    u3,
    own_out,
    far_low,
    far_high,
    right_low,
    right_high,
    left_low,
    left_high,
    keep_out,
    give_out,
    tiles,
    x_ref,
    xt_ref,
    gate_m,
    up_m,
    acc,
    gate_pre,
    up_pre,
    d_gate,
    d_up,
    d_cols,
    task_out,
    main_out,
    cell_rows,
    cells_ref,
    first_ref,
    leader_ref,
    shared_ref,
    list_ref,
    count_ref,
    in_sems,
    out_sems,
):
    f32, bf16 = jnp.float32, jnp.bfloat16
    ways = 4
    part = g0.shape[0]
    me, core, lang = info_ref[0], info_ref[1], info_ref[2]
    order = (0, 3, 1, 2)
    x_copy = pltpu.make_async_copy(x_hbm, x_ref, in_sems.at[8])
    xt_copy = pltpu.make_async_copy(xt_hbm, xt_ref, in_sems.at[9])
    n_slots = tiles.shape[0]
    tile_copies = (
        pltpu.make_async_copy(task_in, tiles.at[pl.ds(0, n_task)], in_sems.at[11]),
        pltpu.make_async_copy(lang_hbm, tiles.at[pl.ds(n_task, n_slots - n_task)], in_sems.at[12]),
    )
    for c in tile_copies:
        c.start()
    copies, starts = {}, {}
    for k, (g, u) in enumerate(((g0, u0), (g1, u1), (g2, u2), (g3, u3))):
        starts[k] = pl.multiple_of(lax.rem(me + k, ways) * part, part)
        to = pl.ds(starts[k], part)
        copies[k] = (
            pltpu.make_async_copy(g, gate_m.at[to], in_sems.at[k]),
            pltpu.make_async_copy(u, up_m.at[to], in_sems.at[ways + k]),
        )
    for k in order:
        for c in copies[k]:
            c.start()
        if k == order[0]:
            x_copy.start()
    xt_copy.start()

    def no_first(i, carry):
        first_ref[i] = -1
        return carry

    lax.fori_loop(0, first_ref.shape[0], no_first, 0)
    for p in range(ways):
        count_ref[p] = 0
    gate_pre[...] = jnp.zeros_like(gate_pre)
    up_pre[...] = jnp.zeros_like(up_pre)
    for c in tile_copies:
        c.wait()
    for i in range(n_slots):
        row = tiles[i, 2 * BLK : 2 * BLK + PAD, :].astype(f32).astype(jnp.int32)
        cell_rows[i : i + 1, :] = row[0:1]
    cell_copy = pltpu.make_async_copy(cell_rows, cells_ref, in_sems.at[10])
    cell_copy.start()
    cell_copy.wait()
    part_cells = 2 * part // BLK

    def sort_in(s, carry):
        cell = cells_ref[s, 0]

        @pl.when(cell >= 0)
        def _():
            known = first_ref[cell]
            new = known < 0
            lead = jnp.where(new, s, known)
            first_ref[cell] = lead
            leader_ref[s] = lead
            shared_ref[lead] = jnp.where(new, 0, 1)
            p = lax.div(cell, part_cells)
            list_ref[p * n_slots + count_ref[p]] = s
            count_ref[p] += 1

        return carry

    lax.fori_loop(0, n_slots, sort_in, 0)

    def spot(cell):
        row = pl.multiple_of(lax.shift_right_logical(cell, 1) * BLK, BLK)
        col = pl.multiple_of(lax.bitwise_and(cell, 1) * BLK, BLK)
        return pl.ds(row, BLK), pl.ds(col, BLK)

    depth = 1024
    for k in order:
        for c in copies[k]:
            c.wait()
        p = lax.rem(me + k, ways)

        def add(n, carry, p=p):
            s = list_ref[p * n_slots + n]
            at = spot(cells_ref[s, 0])
            lead = leader_ref[s]

            @pl.when((lead == s) & (shared_ref[s] == 0))
            def _():
                gate_m[at] = (gate_m[at].astype(f32) + tiles[s, 0:BLK].astype(f32)).astype(bf16)
                up_m[at] = (up_m[at].astype(f32) + tiles[s, BLK : 2 * BLK].astype(f32)).astype(bf16)

            @pl.when((lead == s) & (shared_ref[s] != 0))
            def _():
                acc[s, 0:BLK] = gate_m[at].astype(f32) + tiles[s, 0:BLK].astype(f32)
                acc[s, BLK:] = up_m[at].astype(f32) + tiles[s, BLK : 2 * BLK].astype(f32)

            @pl.when(lead != s)
            def _():
                acc[lead] += tiles[s, 0 : 2 * BLK].astype(f32)

            return carry

        def write_back(n, carry, p=p):
            s = list_ref[p * n_slots + n]

            @pl.when((leader_ref[s] == s) & (shared_ref[s] != 0))
            def _():
                at = spot(cells_ref[s, 0])
                gate_m[at] = acc[s, 0:BLK].astype(bf16)
                up_m[at] = acc[s, BLK:].astype(bf16)

            return carry

        lax.fori_loop(0, count_ref[p], add, 0)
        lax.fori_loop(0, count_ref[p], write_back, 0)
        if k == order[0]:
            x_copy.wait()
        for step in range(part // depth):
            rows = pl.ds(pl.multiple_of(starts[k] + step * depth, depth), depth)
            xk = x_ref[:, rows]
            gate_pre[...] += jnp.dot(xk, gate_m[rows, :], preferred_element_type=f32)
            up_pre[...] += jnp.dot(xk, up_m[rows, :], preferred_element_type=f32)

    g, u = gate_pre[...], up_pre[...]
    s = jax.nn.sigmoid(g)
    c = cot_ref[...].astype(f32)
    dg = (c * u * s * (1.0 + g * (1.0 - s))).astype(bf16)
    du = (c * g * s).astype(bf16)
    d_gate[...] = dg
    d_up[...] = du
    for h in range(2):
        d_cols[h, :, 0:BLK] = dg[:, h * BLK : (h + 1) * BLK]
        d_cols[h, :, BLK:] = du[:, h * BLK : (h + 1) * BLK]
    xt_copy.wait()

    def task_step(i, carry):
        cell = jnp.maximum(cells_ref[i, 0], 0)
        row = pl.multiple_of(lax.shift_right_logical(cell, 1) * BLK, BLK)
        side = lax.bitwise_and(cell, 1)
        r = jnp.dot(xt_ref[pl.ds(row, BLK), :], d_cols[side], preferred_element_type=f32)
        r = r.astype(bf16)
        task_out[0, i] = r[0 : BLK // 2, 0:BLK]
        task_out[1, i] = r[BLK // 2 :, 0:BLK]
        task_out[2, i] = r[0 : BLK // 2, BLK:]
        task_out[3, i] = r[BLK // 2 :, BLK:]
        return carry

    lax.fori_loop(0, n_task, task_step, 0, unroll=8)
    q = [lax.rem(me + k, ways) for k in range(ways)]
    half = n_task // 2
    low, high = pl.ds(0, half), pl.ds(half, half)
    moves = [
        (task_out.at[q[2], low], far_low),
        (task_out.at[q[2], high], far_high),
        (task_out.at[q[1], high], right_high),
        (task_out.at[q[3], low], left_low),
        (task_out.at[q[1], low], right_low),
        (task_out.at[q[3], high], left_high),
        (task_out.at[q[0]], own_out),
    ]
    out_copies = [
        pltpu.make_async_copy(src, dst, out_sems.at[n]) for n, (src, dst) in enumerate(moves)
    ]
    for copy in out_copies:
        copy.start()

    last = (((1,), (1,)), ((), ()))
    per = keep_out.shape[0] // ways

    def backward(m, carry):
        rows = pl.ds(pl.multiple_of(m * 2 * BLK, 2 * BLK), 2 * BLK)
        r = lax.dot_general(d_gate[...], gate_m[rows, :], last, preferred_element_type=f32)
        r += lax.dot_general(d_up[...], up_m[rows, :], last, preferred_element_type=f32)
        r = r.astype(bf16)
        main_out[0, m] = r[:, 0:BLK]
        main_out[1, m] = r[:, BLK:]
        return carry

    for n in range(ways):
        lax.fori_loop(n * per, (n + 1) * per, backward, 0, unroll=4)
        src = pl.ds(n * per, per)
        dst = pl.ds(lax.rem(n + ways - lang, ways) * per, per)
        for way, out in ((core, keep_out), (1 - core, give_out)):
            copy = pltpu.make_async_copy(
                main_out.at[way, src], out.at[dst], out_sems.at[len(out_copies)]
            )
            copy.start()
            out_copies.append(copy)
    for copy in out_copies:
        copy.wait()


def device_step(info, cot, task, lang, x, xt, gates, ups, step):
    bf16, f32 = jnp.bfloat16, jnp.float32
    n_task, n_slots = task.shape[0], task.shape[0] + lang.shape[0]
    tokens, width = x.shape
    cols = cot.shape[1]
    padded = -(-n_slots // 8) * 8
    vmem = pl.BlockSpec(memory_space=pltpu.VMEM)
    hbm = pl.BlockSpec(memory_space=pl.ANY)
    pairs = width // (2 * BLK)
    main = jax.ShapeDtypeStruct((pairs, tokens, BLK), bf16)
    return pl.pallas_call(
        lambda *refs: device_kernel(n_task, *refs),
        out_shape=(
            *[
                jax.ShapeDtypeStruct((n, BLK // 2, BLK), bf16)
                for n in (n_task, *[n_task // 2] * 6)
            ],
            main,
            main,
        ),
        in_specs=[pl.BlockSpec(memory_space=pltpu.SMEM)] + [vmem] * 2 + [hbm] * 12,
        out_specs=[hbm] * 9,
        scratch_shapes=[
            pltpu.VMEM((n_slots, *task.shape[1:]), bf16),
            pltpu.VMEM(x.shape, bf16),
            pltpu.VMEM(xt.shape, bf16),
            pltpu.VMEM((width, cols), bf16),
            pltpu.VMEM((width, cols), bf16),
            pltpu.VMEM((n_slots, 2 * BLK, BLK), f32),
            pltpu.VMEM((tokens, cols), f32),
            pltpu.VMEM((tokens, cols), f32),
            pltpu.VMEM((tokens, cols), bf16),
            pltpu.VMEM((tokens, cols), bf16),
            pltpu.VMEM((2, tokens, 2 * BLK), bf16),
            pltpu.VMEM((4, n_task, BLK // 2, BLK), bf16),
            pltpu.VMEM((2, pairs, tokens, BLK), bf16),
            pltpu.VMEM((padded, BLK), jnp.int32),
            pltpu.SMEM((padded, BLK), jnp.int32),
            pltpu.SMEM((width // BLK * cols // BLK,), jnp.int32),
            pltpu.SMEM((n_slots,), jnp.int32),
            pltpu.SMEM((n_slots,), jnp.int32),
            pltpu.SMEM((4 * n_slots,), jnp.int32),
            pltpu.SMEM((4,), jnp.int32),
            pltpu.SemaphoreType.DMA((13,)),
            pltpu.SemaphoreType.DMA((15,)),
        ],
        compiler_params=pltpu.CompilerParams(vmem_limit_bytes=56 * MIB),
        cost_estimate=pl.CostEstimate(
            flops=10 * tokens * width * cols, bytes_accessed=24 * MIB, transcendentals=tokens * cols
        ),
        name="device_step",
    )(info, cot, step, task, lang, x, xt, *gates, *ups)


def pace_kernel(*refs):
    refs[-1][...] = jnp.zeros_like(refs[-1])


def pace(*arrays, flops=10**11, vmem=MIB):
    return pl.pallas_call(
        pace_kernel,
        out_shape=jax.ShapeDtypeStruct((8, BLK), jnp.float32),
        in_specs=[pl.BlockSpec(memory_space=pl.ANY)] * len(arrays),
        out_specs=pl.BlockSpec(memory_space=pltpu.VMEM),
        compiler_params=pltpu.CompilerParams(vmem_limit_bytes=vmem),
        cost_estimate=pl.CostEstimate(flops=flops, bytes_accessed=4096, transcendentals=0),
        name="pace",
    )(*arrays)


def ring_first(axis, up_first, down_first):
    return (
        lax.ppermute(up_first, axis, ring(axis, 1)),
        lax.ppermute(down_first, axis, ring(axis, -1)),
    )


def ring_rest(axis, own, up_second, down_second, from_left, from_right):
    f32, bf16 = jnp.float32, jnp.bfloat16
    half = own.shape[0] // 2
    up_second = (up_second.astype(f32) + from_left[:half].astype(f32)).astype(bf16)
    down_second = (down_second.astype(f32) + from_right[half:].astype(f32)).astype(bf16)
    low_left = lax.ppermute(up_second, axis, ring(axis, 1))
    high_right = lax.ppermute(down_second, axis, ring(axis, -1))
    low = own[:half].astype(f32) + low_left.astype(f32) + from_right[:half].astype(f32)
    high = own[half:].astype(f32) + high_right.astype(f32) + from_left[half:].astype(f32)
    return jnp.concatenate([low, high], axis=0).astype(bf16)


def on_device(
    tokens_in,
    cotangent,
    gate_base,
    up_base,
    lang_delta,
    lang_cell,
    group_lang,
    task_delta,
    task_slab,
    task_cell,
):
    f32, bf16 = jnp.float32, jnp.bfloat16
    fsdp = ("z", "core")
    n_lang, n_z, n_core, n_dp = (lax.axis_size(a) for a in ("lang", "z", "core", "dp"))
    n_fsdp = n_z * n_core
    language = group_lang[0]
    my_lang, my_core, my_dp = (lax.axis_index(a) for a in ("lang", "core", "dp"))
    held = task_delta.shape[0]

    gate_left = lax.ppermute(gate_base, "dp", ring("dp", 1))
    up_right = lax.ppermute(up_base, "dp", ring("dp", -1))
    up_left = lax.ppermute(up_base, "dp", ring("dp", 1))
    gate_right = lax.ppermute(gate_base, "dp", ring("dp", -1))
    target = task_slab[:, 0]
    send_task = place(target, task_cell[:, 0], task_delta.reshape(held, 2 * BLK, BLK), n_fsdp)
    got_task = lax.all_to_all(send_task, fsdp, split_axis=0, concat_axis=0, tiled=True)
    lang_tiles = lang_delta[0, 0].reshape(lang_delta.shape[2:4] + (2 * BLK, BLK))
    with_cell = with_cells(lang_tiles, lang_cell[0, 0])
    send_lang = [
        lax.dynamic_index_in_dim(with_cell, lax.rem(my_lang + k, n_lang), 0, keepdims=False)
        for k in range(n_lang)
    ]
    step = pace(gate_left, gate_right, up_left, up_right, *send_lang, vmem=62 * MIB)
    gate_on, up_on, step, *send_lang = lax.optimization_barrier(
        (gate_left, up_right, step, *send_lang)
    )
    gate_far = lax.ppermute(gate_on, "dp", ring("dp", 1))
    up_far = lax.ppermute(up_on, "dp", ring("dp", -1))
    choice = lax.rem(my_lang - language + n_lang, n_lang)
    chosen = send_lang[0]
    for k in range(1, n_lang):
        chosen = jnp.where(choice == k, lax.ppermute(send_lang[k], "lang", ring("lang", k)), chosen)

    tokens_t = tokens_in.T
    step = pace(step, tokens_t, flops=0, vmem=62 * MIB)
    *pieces, keep, give = device_step(
        jnp.stack([my_dp, my_core, my_lang]).astype(jnp.int32),
        cotangent,
        got_task,
        chosen,
        tokens_in,
        tokens_t,
        (gate_base, gate_right, gate_far, gate_left),
        (up_base, up_right, up_far, up_left),
        step,
    )
    got = lax.ppermute(give, "core", ring("core", 1))
    own, far_low, far_high, right_low, right_high, left_low, left_high = pieces
    far_up = lax.ppermute(far_low, "dp", ring("dp", 1))
    far_down = lax.ppermute(far_high, "dp", ring("dp", -1))
    high_up = lax.ppermute(right_high, "dp", ring("dp", 1))
    low_down = lax.ppermute(left_low, "dp", ring("dp", -1))

    def both(first, last):
        first, last = first * n_z // 2, last * n_z // 2
        return (keep[first:last].astype(f32) + got[first:last].astype(f32)).astype(bf16)

    main_up = jnp.concatenate([both(4, 5), both(3, 4)], axis=0)
    main_down = jnp.concatenate([both(6, 7), both(5, 6)], axis=0)
    main_first = ring_first("lang", main_up, main_down)
    mark = pace(main_up, main_down)
    far_up, far_down, mark = lax.optimization_barrier((far_up, far_down, mark))
    low_up = (right_low.astype(f32) + far_up.astype(f32)).astype(bf16)
    high_down = (left_high.astype(f32) + far_down.astype(f32)).astype(bf16)
    low_up = lax.ppermute(low_up, "dp", ring("dp", 1))
    high_down = lax.ppermute(high_down, "dp", ring("dp", -1))
    half = own.shape[0] // 2
    low = own[:half].astype(f32) + low_up.astype(f32) + low_down.astype(f32)
    high = own[half:].astype(f32) + high_up.astype(f32) + high_down.astype(f32)
    tsum = jnp.concatenate([low, high], axis=0).astype(bf16)
    over_lang = ring_rest("lang", both(0, 2), both(2, 3), both(7, 8), *main_first)
    mark = pace(over_lang, mark, flops=0)
    back = lax.all_to_all(tsum, fsdp, split_axis=0, concat_axis=0, tiled=True)
    mine = take_own(target, back, mark).reshape(held, -1)
    far, right, left = [lax.ppermute(mine, "dp", ring("dp", -k)) for k in (2, 1, 3)]
    stacked = jnp.stack([mine, right, far, left], axis=0)
    task_grad = jnp.concatenate(
        [
            lax.dynamic_index_in_dim(stacked, lax.rem(q - my_dp + n_dp, n_dp), 0, keepdims=False)
            for q in range(n_dp)
        ],
        axis=1,
    ).astype(f32)

    over_z = lax.all_to_all(over_lang, "z", split_axis=0, concat_axis=0, tiled=True)
    grad_input = jnp.sum(over_z.astype(f32), axis=0).astype(bf16)
    return (grad_input, task_grad)


def solution(mesh):
    lang, fsdp, dp = (mesh.shape[a] for a in ("lang", "fsdp", "dp"))
    fine = Mesh(mesh.devices.reshape(lang, fsdp // 2, 2, dp), ("lang", "z", "core", "dp"))
    cols = ("lang", "z", "core")
    return jax.shard_map(
        on_device,
        mesh=fine,
        in_specs=(
            P("dp", None),
            P("dp", cols),
            P("dp", cols),
            P("dp", cols),
            P("lang", ("z", "core"), None, None, None),
            P("lang", ("z", "core"), None, None),
            P("dp"),
            P(cols, None),
            P(cols, None),
            P(cols, None),
        ),
        out_specs=(P("dp", cols), P(cols, None)),
        check_vma=False,
    )
```

```python
import jax
import jax.numpy as jnp
from jax import lax
from jax.experimental import pallas as pl
from jax.experimental.pallas import tpu as pltpu
from jax.sharding import Mesh, PartitionSpec as P

BLK = 128
CAP = 2
PAD = 16
MIB = 1024 * 1024


def ring(axis, step):
    n = lax.axis_size(axis)
    return [(i, (i + step) % n) for i in range(n)]


def with_cells(tiles, cells):
    rows = jnp.broadcast_to(cells.astype(jnp.bfloat16)[..., None, None], cells.shape + (PAD, BLK))
    return jnp.concatenate([tiles, rows], axis=-2)


def place_kernel(slab_ref, cells_ref, tiles_ref, out_ref, used_ref):
    def clear(i, carry):
        out_ref[i, 2 * BLK :, :] = jnp.full((PAD, BLK), -1.0, jnp.bfloat16)
        return carry

    lax.fori_loop(0, out_ref.shape[0], clear, 0)

    def unused(i, carry):
        used_ref[i] = 0
        return carry

    lax.fori_loop(0, used_ref.shape[0], unused, 0)

    def put(i, carry):
        slab = slab_ref[i]
        slot = slab * CAP + used_ref[slab]
        used_ref[slab] += 1
        out_ref[slot, 0 : 2 * BLK, :] = tiles_ref[i]
        out_ref[slot, 2 * BLK :, :] = jnp.full(
            (PAD, BLK), cells_ref[i].astype(jnp.float32), jnp.float32
        ).astype(jnp.bfloat16)
        return carry

    lax.fori_loop(0, tiles_ref.shape[0], put, 0)


def place(slab, cells, tiles, n_slabs):
    smem = pl.BlockSpec(memory_space=pltpu.SMEM)
    vmem = pl.BlockSpec(memory_space=pltpu.VMEM)
    return pl.pallas_call(
        place_kernel,
        out_shape=jax.ShapeDtypeStruct((n_slabs * CAP, 2 * BLK + PAD, BLK), jnp.bfloat16),
        in_specs=[smem, smem, vmem],
        out_specs=vmem,
        scratch_shapes=[pltpu.SMEM((n_slabs,), jnp.int32)],
        compiler_params=pltpu.CompilerParams(vmem_limit_bytes=16 * MIB),
        cost_estimate=pl.CostEstimate(flops=0, bytes_accessed=3 * MIB, transcendentals=0),
        name="place",
    )(slab, cells, tiles)


def take_own_kernel(slab_ref, back_ref, _mark, out_ref, used_ref):
    def unused(i, carry):
        used_ref[i] = 0
        return carry

    lax.fori_loop(0, used_ref.shape[0], unused, 0)

    def take(i, carry):
        slab = slab_ref[i]
        out_ref[i] = back_ref[slab * CAP + used_ref[slab]]
        used_ref[slab] += 1
        return carry

    lax.fori_loop(0, out_ref.shape[0], take, 0)


def take_own(slab, back, mark):
    smem = pl.BlockSpec(memory_space=pltpu.SMEM)
    vmem = pl.BlockSpec(memory_space=pltpu.VMEM)
    return pl.pallas_call(
        take_own_kernel,
        out_shape=jax.ShapeDtypeStruct(slab.shape + back.shape[1:], back.dtype),
        in_specs=[smem, vmem, pl.BlockSpec(memory_space=pl.ANY)],
        out_specs=vmem,
        scratch_shapes=[pltpu.SMEM((back.shape[0] // CAP,), jnp.int32)],
        compiler_params=pltpu.CompilerParams(vmem_limit_bytes=4 * MIB),
        cost_estimate=pl.CostEstimate(flops=0, bytes_accessed=MIB, transcendentals=0),
        name="take_own",
    )(slab, back, mark)


def device_kernel(
    n_task,
    info_ref,
    cot_ref,
    _step,
    task_in,
    lang_hbm,
    x_hbm,
    xt_hbm,
    g0,
    g1,
    g2,
    g3,
    u0,
    u1,
    u2,
    u3,
    own_out,
    far_low,
    far_high,
    right_low,
    right_high,
    left_low,
    left_high,
    keep_out,
    give_out,
    tiles,
    x_ref,
    xt_ref,
    gate_m,
    up_m,
    acc,
    gate_pre,
    up_pre,
    d_gate,
    d_up,
    d_cols,
    task_out,
    main_out,
    cell_rows,
    cells_ref,
    first_ref,
    leader_ref,
    shared_ref,
    list_ref,
    count_ref,
    in_sems,
    out_sems,
):
    f32, bf16 = jnp.float32, jnp.bfloat16
    ways = 4
    part = g0.shape[0]
    me, core, lang = info_ref[0], info_ref[1], info_ref[2]
    order = (0, 3, 1, 2)
    x_copy = pltpu.make_async_copy(x_hbm, x_ref, in_sems.at[8])
    xt_copy = pltpu.make_async_copy(xt_hbm, xt_ref, in_sems.at[9])
    n_slots = tiles.shape[0]
    tile_copies = (
        pltpu.make_async_copy(task_in, tiles.at[pl.ds(0, n_task)], in_sems.at[11]),
        pltpu.make_async_copy(lang_hbm, tiles.at[pl.ds(n_task, n_slots - n_task)], in_sems.at[12]),
    )
    for c in tile_copies:
        c.start()
    copies, starts = {}, {}
    for k, (g, u) in enumerate(((g0, u0), (g1, u1), (g2, u2), (g3, u3))):
        starts[k] = pl.multiple_of(lax.rem(me + k, ways) * part, part)
        to = pl.ds(starts[k], part)
        copies[k] = (
            pltpu.make_async_copy(g, gate_m.at[to], in_sems.at[k]),
            pltpu.make_async_copy(u, up_m.at[to], in_sems.at[ways + k]),
        )
    for k in order:
        for c in copies[k]:
            c.start()
        if k == order[0]:
            x_copy.start()
    xt_copy.start()

    def no_first(i, carry):
        first_ref[i] = -1
        return carry

    lax.fori_loop(0, first_ref.shape[0], no_first, 0)
    for p in range(ways):
        count_ref[p] = 0
    gate_pre[...] = jnp.zeros_like(gate_pre)
    up_pre[...] = jnp.zeros_like(up_pre)
    for c in tile_copies:
        c.wait()
    for i in range(n_slots):
        row = tiles[i, 2 * BLK : 2 * BLK + PAD, :].astype(f32).astype(jnp.int32)
        cell_rows[i : i + 1, :] = row[0:1]
    cell_copy = pltpu.make_async_copy(cell_rows, cells_ref, in_sems.at[10])
    cell_copy.start()
    cell_copy.wait()
    part_cells = 2 * part // BLK

    def sort_in(s, carry):
        cell = cells_ref[s, 0]

        @pl.when(cell >= 0)
        def _():
            known = first_ref[cell]
            new = known < 0
            lead = jnp.where(new, s, known)
            first_ref[cell] = lead
            leader_ref[s] = lead
            shared_ref[lead] = jnp.where(new, 0, 1)
            p = lax.div(cell, part_cells)
            list_ref[p * n_slots + count_ref[p]] = s
            count_ref[p] += 1

        return carry

    lax.fori_loop(0, n_slots, sort_in, 0)

    def spot(cell):
        row = pl.multiple_of(lax.shift_right_logical(cell, 1) * BLK, BLK)
        col = pl.multiple_of(lax.bitwise_and(cell, 1) * BLK, BLK)
        return pl.ds(row, BLK), pl.ds(col, BLK)

    depth = 1024
    for k in order:
        for c in copies[k]:
            c.wait()
        p = lax.rem(me + k, ways)

        def add(n, carry, p=p):
            s = list_ref[p * n_slots + n]
            at = spot(cells_ref[s, 0])
            lead = leader_ref[s]

            @pl.when((lead == s) & (shared_ref[s] == 0))
            def _():
                gate_m[at] = (gate_m[at].astype(f32) + tiles[s, 0:BLK].astype(f32)).astype(bf16)
                up_m[at] = (up_m[at].astype(f32) + tiles[s, BLK : 2 * BLK].astype(f32)).astype(bf16)

            @pl.when((lead == s) & (shared_ref[s] != 0))
            def _():
                acc[s, 0:BLK] = gate_m[at].astype(f32) + tiles[s, 0:BLK].astype(f32)
                acc[s, BLK:] = up_m[at].astype(f32) + tiles[s, BLK : 2 * BLK].astype(f32)

            @pl.when(lead != s)
            def _():
                acc[lead] += tiles[s, 0 : 2 * BLK].astype(f32)

            return carry

        def write_back(n, carry, p=p):
            s = list_ref[p * n_slots + n]

            @pl.when((leader_ref[s] == s) & (shared_ref[s] != 0))
            def _():
                at = spot(cells_ref[s, 0])
                gate_m[at] = acc[s, 0:BLK].astype(bf16)
                up_m[at] = acc[s, BLK:].astype(bf16)

            return carry

        lax.fori_loop(0, count_ref[p], add, 0)
        lax.fori_loop(0, count_ref[p], write_back, 0)
        if k == order[0]:
            x_copy.wait()
        for step in range(part // depth):
            rows = pl.ds(pl.multiple_of(starts[k] + step * depth, depth), depth)
            xk = x_ref[:, rows]
            gate_pre[...] += jnp.dot(xk, gate_m[rows, :], preferred_element_type=f32)
            up_pre[...] += jnp.dot(xk, up_m[rows, :], preferred_element_type=f32)

    g, u = gate_pre[...], up_pre[...]
    s = jax.nn.sigmoid(g)
    c = cot_ref[...].astype(f32)
    dg = (c * u * s * (1.0 + g * (1.0 - s))).astype(bf16)
    du = (c * g * s).astype(bf16)
    d_gate[...] = dg
    d_up[...] = du
    for h in range(2):
        d_cols[h, :, 0:BLK] = dg[:, h * BLK : (h + 1) * BLK]
        d_cols[h, :, BLK:] = du[:, h * BLK : (h + 1) * BLK]
    xt_copy.wait()

    def task_step(i, carry):
        cell = jnp.maximum(cells_ref[i, 0], 0)
        row = pl.multiple_of(lax.shift_right_logical(cell, 1) * BLK, BLK)
        side = lax.bitwise_and(cell, 1)
        r = jnp.dot(xt_ref[pl.ds(row, BLK), :], d_cols[side], preferred_element_type=f32)
        r = r.astype(bf16)
        task_out[0, i] = r[0 : BLK // 2, 0:BLK]
        task_out[1, i] = r[BLK // 2 :, 0:BLK]
        task_out[2, i] = r[0 : BLK // 2, BLK:]
        task_out[3, i] = r[BLK // 2 :, BLK:]
        return carry

    lax.fori_loop(0, n_task, task_step, 0, unroll=8)
    q = [lax.rem(me + k, ways) for k in range(ways)]
    half = n_task // 2
    low, high = pl.ds(0, half), pl.ds(half, half)
    moves = [
        (task_out.at[q[2], low], far_low),
        (task_out.at[q[2], high], far_high),
        (task_out.at[q[1], high], right_high),
        (task_out.at[q[3], low], left_low),
        (task_out.at[q[1], low], right_low),
        (task_out.at[q[3], high], left_high),
        (task_out.at[q[0]], own_out),
    ]
    out_copies = [
        pltpu.make_async_copy(src, dst, out_sems.at[n]) for n, (src, dst) in enumerate(moves)
    ]
    for copy in out_copies:
        copy.start()

    last = (((1,), (1,)), ((), ()))
    per = keep_out.shape[0] // ways

    def backward(m, carry):
        rows = pl.ds(pl.multiple_of(m * 2 * BLK, 2 * BLK), 2 * BLK)
        r = lax.dot_general(d_gate[...], gate_m[rows, :], last, preferred_element_type=f32)
        r += lax.dot_general(d_up[...], up_m[rows, :], last, preferred_element_type=f32)
        r = r.astype(bf16)
        main_out[0, m] = r[:, 0:BLK]
        main_out[1, m] = r[:, BLK:]
        return carry

    for n in range(ways):
        lax.fori_loop(n * per, (n + 1) * per, backward, 0, unroll=4)
        src = pl.ds(n * per, per)
        dst = pl.ds(lax.rem(n + ways - lang, ways) * per, per)
        for way, out in ((core, keep_out), (1 - core, give_out)):
            copy = pltpu.make_async_copy(
                main_out.at[way, src], out.at[dst], out_sems.at[len(out_copies)]
            )
            copy.start()
            out_copies.append(copy)
    for copy in out_copies:
        copy.wait()


def device_step(info, cot, task, lang, x, xt, gates, ups, step):
    bf16, f32 = jnp.bfloat16, jnp.float32
    n_task, n_slots = task.shape[0], task.shape[0] + lang.shape[0]
    tokens, width = x.shape
    cols = cot.shape[1]
    padded = -(-n_slots // 8) * 8
    vmem = pl.BlockSpec(memory_space=pltpu.VMEM)
    hbm = pl.BlockSpec(memory_space=pl.ANY)
    pairs = width // (2 * BLK)
    main = jax.ShapeDtypeStruct((pairs, tokens, BLK), bf16)
    return pl.pallas_call(
        lambda *refs: device_kernel(n_task, *refs),
        out_shape=(
            *[
                jax.ShapeDtypeStruct((n, BLK // 2, BLK), bf16)
                for n in (n_task, *[n_task // 2] * 6)
            ],
            main,
            main,
        ),
        in_specs=[pl.BlockSpec(memory_space=pltpu.SMEM)] + [vmem] * 2 + [hbm] * 12,
        out_specs=[hbm] * 9,
        scratch_shapes=[
            pltpu.VMEM((n_slots, *task.shape[1:]), bf16),
            pltpu.VMEM(x.shape, bf16),
            pltpu.VMEM(xt.shape, bf16),
            pltpu.VMEM((width, cols), bf16),
            pltpu.VMEM((width, cols), bf16),
            pltpu.VMEM((n_slots, 2 * BLK, BLK), f32),
            pltpu.VMEM((tokens, cols), f32),
            pltpu.VMEM((tokens, cols), f32),
            pltpu.VMEM((tokens, cols), bf16),
            pltpu.VMEM((tokens, cols), bf16),
            pltpu.VMEM((2, tokens, 2 * BLK), bf16),
            pltpu.VMEM((4, n_task, BLK // 2, BLK), bf16),
            pltpu.VMEM((2, pairs, tokens, BLK), bf16),
            pltpu.VMEM((padded, BLK), jnp.int32),
            pltpu.SMEM((padded, BLK), jnp.int32),
            pltpu.SMEM((width // BLK * cols // BLK,), jnp.int32),
            pltpu.SMEM((n_slots,), jnp.int32),
            pltpu.SMEM((n_slots,), jnp.int32),
            pltpu.SMEM((4 * n_slots,), jnp.int32),
            pltpu.SMEM((4,), jnp.int32),
            pltpu.SemaphoreType.DMA((13,)),
            pltpu.SemaphoreType.DMA((15,)),
        ],
        compiler_params=pltpu.CompilerParams(vmem_limit_bytes=56 * MIB),
        cost_estimate=pl.CostEstimate(
            flops=10 * tokens * width * cols, bytes_accessed=24 * MIB, transcendentals=tokens * cols
        ),
        name="device_step",
    )(info, cot, step, task, lang, x, xt, *gates, *ups)


def add_pair_kernel(a_ref, b_ref, _mark, out_ref):
    f32 = jnp.float32
    out_ref[...] = (a_ref[...].astype(f32) + b_ref[...].astype(f32)).astype(out_ref.dtype)


def add_pair(a, b, mark):
    vmem = pl.BlockSpec(memory_space=pltpu.VMEM)
    return pl.pallas_call(
        add_pair_kernel,
        out_shape=jax.ShapeDtypeStruct(a.shape, a.dtype),
        in_specs=[vmem, vmem, pl.BlockSpec(memory_space=pl.ANY)],
        out_specs=vmem,
        compiler_params=pltpu.CompilerParams(vmem_limit_bytes=4 * MIB),
        cost_estimate=pl.CostEstimate(flops=a.size, bytes_accessed=MIB, transcendentals=0),
        name="add_pair",
    )(a, b, mark)


def pace_kernel(*refs):
    refs[-1][...] = jnp.zeros_like(refs[-1])


def pace(*arrays, flops=10**11, vmem=MIB):
    return pl.pallas_call(
        pace_kernel,
        out_shape=jax.ShapeDtypeStruct((8, BLK), jnp.float32),
        in_specs=[pl.BlockSpec(memory_space=pl.ANY)] * len(arrays),
        out_specs=pl.BlockSpec(memory_space=pltpu.VMEM),
        compiler_params=pltpu.CompilerParams(vmem_limit_bytes=vmem),
        cost_estimate=pl.CostEstimate(flops=flops, bytes_accessed=4096, transcendentals=0),
        name="pace",
    )(*arrays)


def ring_first(axis, up_first, down_first):
    return (
        lax.ppermute(up_first, axis, ring(axis, 1)),
        lax.ppermute(down_first, axis, ring(axis, -1)),
    )


def ring_rest(axis, own, up_second, down_second, from_left, from_right):
    f32, bf16 = jnp.float32, jnp.bfloat16
    half = own.shape[0] // 2
    up_second = (up_second.astype(f32) + from_left[:half].astype(f32)).astype(bf16)
    down_second = (down_second.astype(f32) + from_right[half:].astype(f32)).astype(bf16)
    low_left = lax.ppermute(up_second, axis, ring(axis, 1))
    high_right = lax.ppermute(down_second, axis, ring(axis, -1))
    low = own[:half].astype(f32) + low_left.astype(f32) + from_right[:half].astype(f32)
    high = own[half:].astype(f32) + high_right.astype(f32) + from_left[half:].astype(f32)
    return jnp.concatenate([low, high], axis=0).astype(bf16)


def on_device(
    tokens_in,
    cotangent,
    gate_base,
    up_base,
    lang_delta,
    lang_cell,
    group_lang,
    task_delta,
    task_slab,
    task_cell,
):
    f32, bf16 = jnp.float32, jnp.bfloat16
    fsdp = ("z_far", "z_near", "core")
    n_lang, n_far, n_near, n_core, n_dp = (
        lax.axis_size(a) for a in ("lang", "z_far", "z_near", "core", "dp")
    )
    n_z = n_far * n_near
    n_fsdp = n_z * n_core
    language = group_lang[0]
    my_lang, my_core, my_dp = (lax.axis_index(a) for a in ("lang", "core", "dp"))
    held = task_delta.shape[0]

    gate_left = lax.ppermute(gate_base, "dp", ring("dp", 1))
    up_right = lax.ppermute(up_base, "dp", ring("dp", -1))
    up_left = lax.ppermute(up_base, "dp", ring("dp", 1))
    gate_right = lax.ppermute(gate_base, "dp", ring("dp", -1))
    target = task_slab[:, 0]
    send_task = place(target, task_cell[:, 0], task_delta.reshape(held, 2 * BLK, BLK), n_fsdp)
    got_task = lax.all_to_all(send_task, fsdp, split_axis=0, concat_axis=0, tiled=True)
    lang_tiles = lang_delta[0, 0].reshape(lang_delta.shape[2:4] + (2 * BLK, BLK))
    with_cell = with_cells(lang_tiles, lang_cell[0, 0])
    send_lang = [
        lax.dynamic_index_in_dim(with_cell, lax.rem(my_lang + k, n_lang), 0, keepdims=False)
        for k in range(n_lang)
    ]
    step = pace(gate_left, gate_right, up_left, up_right, *send_lang, vmem=62 * MIB)
    gate_on, up_on, step, *send_lang = lax.optimization_barrier(
        (gate_left, up_right, step, *send_lang)
    )
    gate_far = lax.ppermute(gate_on, "dp", ring("dp", 1))
    up_far = lax.ppermute(up_on, "dp", ring("dp", -1))
    choice = lax.rem(my_lang - language + n_lang, n_lang)
    chosen = send_lang[0]
    for k in range(1, n_lang):
        chosen = jnp.where(choice == k, lax.ppermute(send_lang[k], "lang", ring("lang", k)), chosen)

    tokens_t = tokens_in.T
    step = pace(step, tokens_t, flops=0, vmem=62 * MIB)
    *pieces, keep, give = device_step(
        jnp.stack([my_dp, my_core, my_lang]).astype(jnp.int32),
        cotangent,
        got_task,
        chosen,
        tokens_in,
        tokens_t,
        (gate_base, gate_right, gate_far, gate_left),
        (up_base, up_right, up_far, up_left),
        step,
    )
    got = lax.ppermute(give, "core", ring("core", 1))
    own, far_low, far_high, right_low, right_high, left_low, left_high = pieces
    far_up = lax.ppermute(far_low, "dp", ring("dp", 1))
    far_down = lax.ppermute(far_high, "dp", ring("dp", -1))
    high_up = lax.ppermute(right_high, "dp", ring("dp", 1))
    low_down = lax.ppermute(left_low, "dp", ring("dp", -1))

    def both(first, last):
        first, last = first * n_z // 2, last * n_z // 2
        return (keep[first:last].astype(f32) + got[first:last].astype(f32)).astype(bf16)

    main_up = jnp.concatenate([both(4, 5), both(3, 4)], axis=0)
    main_down = jnp.concatenate([both(6, 7), both(5, 6)], axis=0)
    main_first = ring_first("lang", main_up, main_down)
    mark = pace(main_up, main_down)
    far_up, far_down, mark = lax.optimization_barrier((far_up, far_down, mark))
    low_up = (right_low.astype(f32) + far_up.astype(f32)).astype(bf16)
    high_down = (left_high.astype(f32) + far_down.astype(f32)).astype(bf16)
    low_up = lax.ppermute(low_up, "dp", ring("dp", 1))
    high_down = lax.ppermute(high_down, "dp", ring("dp", -1))
    half = own.shape[0] // 2
    low = own[:half].astype(f32) + low_up.astype(f32) + low_down.astype(f32)
    high = own[half:].astype(f32) + high_up.astype(f32) + high_down.astype(f32)
    tsum = jnp.concatenate([low, high], axis=0).astype(bf16)
    over_lang = ring_rest("lang", both(0, 2), both(2, 3), both(7, 8), *main_first)
    my_near = lax.axis_index("z_near")
    by_near = over_lang.reshape(n_far, n_near, *over_lang.shape[1:])
    keep_z = lax.dynamic_index_in_dim(by_near, my_near, 1, keepdims=False)
    give_z = lax.dynamic_index_in_dim(by_near, 1 - my_near, 1, keepdims=False)
    got_z = lax.ppermute(give_z, "z_near", ring("z_near", 1))
    mark = pace(give_z, mark)
    back = lax.all_to_all(tsum, fsdp, split_axis=0, concat_axis=0, tiled=True)
    mine = take_own(target, back, mark).reshape(held, -1)
    far, right, left = [lax.ppermute(mine, "dp", ring("dp", -k)) for k in (2, 1, 3)]
    stacked = jnp.stack([mine, right, far, left], axis=0)
    task_grad = jnp.concatenate(
        [
            lax.dynamic_index_in_dim(stacked, lax.rem(q - my_dp + n_dp, n_dp), 0, keepdims=False)
            for q in range(n_dp)
        ],
        axis=1,
    ).astype(f32)

    near_sum = add_pair(keep_z, got_z, mine)
    over_z = lax.all_to_all(near_sum, "z_far", split_axis=0, concat_axis=0, tiled=True)
    grad_input = jnp.sum(over_z.astype(f32), axis=0).astype(bf16)
    return (grad_input, task_grad)


def solution(mesh):
    lang, fsdp, dp = (mesh.shape[a] for a in ("lang", "fsdp", "dp"))
    sizes = (lang, fsdp // 4, 2, 2, dp)
    fine = Mesh(mesh.devices.reshape(sizes), ("lang", "z_far", "z_near", "core", "dp"))
    cols = ("lang", "z_far", "z_near", "core")
    return jax.shard_map(
        on_device,
        mesh=fine,
        in_specs=(
            P("dp", None),
            P("dp", cols),
            P("dp", cols),
            P("dp", cols),
            P("lang", cols[1:], None, None, None),
            P("lang", cols[1:], None, None),
            P("dp"),
            P(cols, None),
            P(cols, None),
            P(cols, None),
        ),
        out_specs=(P("dp", cols), P(cols, None)),
        check_vma=False,
    )
```

```python
import jax
import jax.numpy as jnp
from jax import lax
from jax.experimental import pallas as pl
from jax.experimental.pallas import tpu as pltpu
from jax.sharding import Mesh, PartitionSpec as P

BLK = 128
CAP = 2
PAD = 16
MIB = 1024 * 1024


def ring(axis, step):
    n = lax.axis_size(axis)
    return [(i, (i + step) % n) for i in range(n)]


def with_cells(tiles, cells):
    rows = jnp.broadcast_to(cells.astype(jnp.bfloat16)[..., None, None], cells.shape + (PAD, BLK))
    return jnp.concatenate([tiles, rows], axis=-2)


def place_kernel(slab_ref, cells_ref, tiles_ref, out_ref, used_ref):
    def clear(i, carry):
        out_ref[i, 2 * BLK :, :] = jnp.full((PAD, BLK), -1.0, jnp.bfloat16)
        return carry

    lax.fori_loop(0, out_ref.shape[0], clear, 0)

    def unused(i, carry):
        used_ref[i] = 0
        return carry

    lax.fori_loop(0, used_ref.shape[0], unused, 0)

    def put(i, carry):
        slab = slab_ref[i]
        slot = slab * CAP + used_ref[slab]
        used_ref[slab] += 1
        out_ref[slot, 0 : 2 * BLK, :] = tiles_ref[i]
        out_ref[slot, 2 * BLK :, :] = jnp.full(
            (PAD, BLK), cells_ref[i].astype(jnp.float32), jnp.float32
        ).astype(jnp.bfloat16)
        return carry

    lax.fori_loop(0, tiles_ref.shape[0], put, 0)


def place(slab, cells, tiles, n_slabs):
    smem = pl.BlockSpec(memory_space=pltpu.SMEM)
    vmem = pl.BlockSpec(memory_space=pltpu.VMEM)
    return pl.pallas_call(
        place_kernel,
        out_shape=jax.ShapeDtypeStruct((n_slabs * CAP, 2 * BLK + PAD, BLK), jnp.bfloat16),
        in_specs=[smem, smem, vmem],
        out_specs=vmem,
        scratch_shapes=[pltpu.SMEM((n_slabs,), jnp.int32)],
        compiler_params=pltpu.CompilerParams(vmem_limit_bytes=16 * MIB),
        cost_estimate=pl.CostEstimate(flops=0, bytes_accessed=3 * MIB, transcendentals=0),
        name="place",
    )(slab, cells, tiles)


def take_own_kernel(slab_ref, back_ref, _mark, out_ref, used_ref):
    def unused(i, carry):
        used_ref[i] = 0
        return carry

    lax.fori_loop(0, used_ref.shape[0], unused, 0)

    def take(i, carry):
        slab = slab_ref[i]
        out_ref[i] = back_ref[slab * CAP + used_ref[slab]]
        used_ref[slab] += 1
        return carry

    lax.fori_loop(0, out_ref.shape[0], take, 0)


def take_own(slab, back, mark):
    smem = pl.BlockSpec(memory_space=pltpu.SMEM)
    vmem = pl.BlockSpec(memory_space=pltpu.VMEM)
    return pl.pallas_call(
        take_own_kernel,
        out_shape=jax.ShapeDtypeStruct(slab.shape + back.shape[1:], back.dtype),
        in_specs=[smem, vmem, pl.BlockSpec(memory_space=pl.ANY)],
        out_specs=vmem,
        scratch_shapes=[pltpu.SMEM((back.shape[0] // CAP,), jnp.int32)],
        compiler_params=pltpu.CompilerParams(vmem_limit_bytes=4 * MIB),
        cost_estimate=pl.CostEstimate(flops=0, bytes_accessed=MIB, transcendentals=0),
        name="take_own",
    )(slab, back, mark)


def device_kernel(
    n_task,
    info_ref,
    cot_ref,
    _step,
    task_in,
    lang_hbm,
    x_hbm,
    xt_hbm,
    g0,
    g1,
    g2,
    g3,
    u0,
    u1,
    u2,
    u3,
    own_out,
    far_low,
    far_high,
    right_low,
    right_high,
    left_low,
    left_high,
    keep_out,
    give_out,
    tiles,
    x_ref,
    xt_ref,
    gate_m,
    up_m,
    acc,
    gate_pre,
    up_pre,
    d_gate,
    d_up,
    d_cols,
    task_out,
    main_out,
    cell_rows,
    cells_ref,
    first_ref,
    leader_ref,
    shared_ref,
    list_ref,
    count_ref,
    in_sems,
    out_sems,
):
    f32, bf16 = jnp.float32, jnp.bfloat16
    ways = 4
    part = g0.shape[0]
    me, core, lang = info_ref[0], info_ref[1], info_ref[2]
    order = (0, 3, 1, 2)
    x_copy = pltpu.make_async_copy(x_hbm, x_ref, in_sems.at[8])
    xt_copy = pltpu.make_async_copy(xt_hbm, xt_ref, in_sems.at[9])
    n_slots = tiles.shape[0]
    tile_copies = (
        pltpu.make_async_copy(task_in, tiles.at[pl.ds(0, n_task)], in_sems.at[11]),
        pltpu.make_async_copy(lang_hbm, tiles.at[pl.ds(n_task, n_slots - n_task)], in_sems.at[12]),
    )
    for c in tile_copies:
        c.start()
    copies, starts = {}, {}
    for k, (g, u) in enumerate(((g0, u0), (g1, u1), (g2, u2), (g3, u3))):
        starts[k] = pl.multiple_of(lax.rem(me + k, ways) * part, part)
        to = pl.ds(starts[k], part)
        copies[k] = (
            pltpu.make_async_copy(g, gate_m.at[to], in_sems.at[k]),
            pltpu.make_async_copy(u, up_m.at[to], in_sems.at[ways + k]),
        )
    for k in order:
        for c in copies[k]:
            c.start()
        if k == order[0]:
            x_copy.start()
    xt_copy.start()

    def no_first(i, carry):
        first_ref[i] = -1
        return carry

    lax.fori_loop(0, first_ref.shape[0], no_first, 0)
    for p in range(ways):
        count_ref[p] = 0
    gate_pre[...] = jnp.zeros_like(gate_pre)
    up_pre[...] = jnp.zeros_like(up_pre)
    for c in tile_copies:
        c.wait()
    for i in range(n_slots):
        row = tiles[i, 2 * BLK : 2 * BLK + PAD, :].astype(f32).astype(jnp.int32)
        cell_rows[i : i + 1, :] = row[0:1]
    cell_copy = pltpu.make_async_copy(cell_rows, cells_ref, in_sems.at[10])
    cell_copy.start()
    cell_copy.wait()
    part_cells = 2 * part // BLK

    def sort_in(s, carry):
        cell = cells_ref[s, 0]

        @pl.when(cell >= 0)
        def _():
            known = first_ref[cell]
            new = known < 0
            lead = jnp.where(new, s, known)
            first_ref[cell] = lead
            leader_ref[s] = lead
            shared_ref[lead] = jnp.where(new, 0, 1)
            p = lax.div(cell, part_cells)
            list_ref[p * n_slots + count_ref[p]] = s
            count_ref[p] += 1

        return carry

    lax.fori_loop(0, n_slots, sort_in, 0)

    def spot(cell):
        row = pl.multiple_of(lax.shift_right_logical(cell, 1) * BLK, BLK)
        col = pl.multiple_of(lax.bitwise_and(cell, 1) * BLK, BLK)
        return pl.ds(row, BLK), pl.ds(col, BLK)

    depth = 1024
    for k in order:
        for c in copies[k]:
            c.wait()
        p = lax.rem(me + k, ways)

        def add(n, carry, p=p):
            s = list_ref[p * n_slots + n]
            at = spot(cells_ref[s, 0])
            lead = leader_ref[s]

            @pl.when((lead == s) & (shared_ref[s] == 0))
            def _():
                gate_m[at] = (gate_m[at].astype(f32) + tiles[s, 0:BLK].astype(f32)).astype(bf16)
                up_m[at] = (up_m[at].astype(f32) + tiles[s, BLK : 2 * BLK].astype(f32)).astype(bf16)

            @pl.when((lead == s) & (shared_ref[s] != 0))
            def _():
                acc[s, 0:BLK] = gate_m[at].astype(f32) + tiles[s, 0:BLK].astype(f32)
                acc[s, BLK:] = up_m[at].astype(f32) + tiles[s, BLK : 2 * BLK].astype(f32)

            @pl.when(lead != s)
            def _():
                acc[lead] += tiles[s, 0 : 2 * BLK].astype(f32)

            return carry

        def write_back(n, carry, p=p):
            s = list_ref[p * n_slots + n]

            @pl.when((leader_ref[s] == s) & (shared_ref[s] != 0))
            def _():
                at = spot(cells_ref[s, 0])
                gate_m[at] = acc[s, 0:BLK].astype(bf16)
                up_m[at] = acc[s, BLK:].astype(bf16)

            return carry

        lax.fori_loop(0, count_ref[p], add, 0)
        lax.fori_loop(0, count_ref[p], write_back, 0)
        if k == order[0]:
            x_copy.wait()
        for step in range(part // depth):
            rows = pl.ds(pl.multiple_of(starts[k] + step * depth, depth), depth)
            xk = x_ref[:, rows]
            gate_pre[...] += jnp.dot(xk, gate_m[rows, :], preferred_element_type=f32)
            up_pre[...] += jnp.dot(xk, up_m[rows, :], preferred_element_type=f32)

    g, u = gate_pre[...], up_pre[...]
    s = jax.nn.sigmoid(g)
    c = cot_ref[...].astype(f32)
    dg = (c * u * s * (1.0 + g * (1.0 - s))).astype(bf16)
    du = (c * g * s).astype(bf16)
    d_gate[...] = dg
    d_up[...] = du
    for h in range(2):
        d_cols[h, :, 0:BLK] = dg[:, h * BLK : (h + 1) * BLK]
        d_cols[h, :, BLK:] = du[:, h * BLK : (h + 1) * BLK]
    xt_copy.wait()

    def task_step(i, carry):
        cell = jnp.maximum(cells_ref[i, 0], 0)
        row = pl.multiple_of(lax.shift_right_logical(cell, 1) * BLK, BLK)
        side = lax.bitwise_and(cell, 1)
        r = jnp.dot(xt_ref[pl.ds(row, BLK), :], d_cols[side], preferred_element_type=f32)
        r = r.astype(bf16)
        task_out[0, i] = r[0 : BLK // 2, 0:BLK]
        task_out[1, i] = r[BLK // 2 :, 0:BLK]
        task_out[2, i] = r[0 : BLK // 2, BLK:]
        task_out[3, i] = r[BLK // 2 :, BLK:]
        return carry

    lax.fori_loop(0, n_task, task_step, 0, unroll=8)
    q = [lax.rem(me + k, ways) for k in range(ways)]
    half = n_task // 2
    low, high = pl.ds(0, half), pl.ds(half, half)
    moves = [
        (task_out.at[q[2], low], far_low),
        (task_out.at[q[2], high], far_high),
        (task_out.at[q[1], high], right_high),
        (task_out.at[q[3], low], left_low),
        (task_out.at[q[1], low], right_low),
        (task_out.at[q[3], high], left_high),
        (task_out.at[q[0]], own_out),
    ]
    out_copies = [
        pltpu.make_async_copy(src, dst, out_sems.at[n]) for n, (src, dst) in enumerate(moves)
    ]
    for copy in out_copies:
        copy.start()

    last = (((1,), (1,)), ((), ()))
    per = keep_out.shape[0] // ways

    def backward(m, carry):
        rows = pl.ds(pl.multiple_of(m * 2 * BLK, 2 * BLK), 2 * BLK)
        r = lax.dot_general(d_gate[...], gate_m[rows, :], last, preferred_element_type=f32)
        r += lax.dot_general(d_up[...], up_m[rows, :], last, preferred_element_type=f32)
        r = r.astype(bf16)
        main_out[0, m] = r[:, 0:BLK]
        main_out[1, m] = r[:, BLK:]
        return carry

    for n in range(ways):
        lax.fori_loop(n * per, (n + 1) * per, backward, 0, unroll=4)
        src = pl.ds(n * per, per)
        dst = pl.ds(lax.rem(n + ways - lang, ways) * per, per)
        for way, out in ((core, keep_out), (1 - core, give_out)):
            copy = pltpu.make_async_copy(
                main_out.at[way, src], out.at[dst], out_sems.at[len(out_copies)]
            )
            copy.start()
            out_copies.append(copy)
    for copy in out_copies:
        copy.wait()


def device_step(info, cot, task, lang, x, xt, gates, ups, step):
    bf16, f32 = jnp.bfloat16, jnp.float32
    n_task, n_slots = task.shape[0], task.shape[0] + lang.shape[0]
    tokens, width = x.shape
    cols = cot.shape[1]
    padded = -(-n_slots // 8) * 8
    vmem = pl.BlockSpec(memory_space=pltpu.VMEM)
    hbm = pl.BlockSpec(memory_space=pl.ANY)
    pairs = width // (2 * BLK)
    main = jax.ShapeDtypeStruct((pairs, tokens, BLK), bf16)
    return pl.pallas_call(
        lambda *refs: device_kernel(n_task, *refs),
        out_shape=(
            *[
                jax.ShapeDtypeStruct((n, BLK // 2, BLK), bf16)
                for n in (n_task, *[n_task // 2] * 6)
            ],
            main,
            main,
        ),
        in_specs=[pl.BlockSpec(memory_space=pltpu.SMEM)] + [vmem] * 2 + [hbm] * 12,
        out_specs=[hbm] * 9,
        scratch_shapes=[
            pltpu.VMEM((n_slots, *task.shape[1:]), bf16),
            pltpu.VMEM(x.shape, bf16),
            pltpu.VMEM(xt.shape, bf16),
            pltpu.VMEM((width, cols), bf16),
            pltpu.VMEM((width, cols), bf16),
            pltpu.VMEM((n_slots, 2 * BLK, BLK), f32),
            pltpu.VMEM((tokens, cols), f32),
            pltpu.VMEM((tokens, cols), f32),
            pltpu.VMEM((tokens, cols), bf16),
            pltpu.VMEM((tokens, cols), bf16),
            pltpu.VMEM((2, tokens, 2 * BLK), bf16),
            pltpu.VMEM((4, n_task, BLK // 2, BLK), bf16),
            pltpu.VMEM((2, pairs, tokens, BLK), bf16),
            pltpu.VMEM((padded, BLK), jnp.int32),
            pltpu.SMEM((padded, BLK), jnp.int32),
            pltpu.SMEM((width // BLK * cols // BLK,), jnp.int32),
            pltpu.SMEM((n_slots,), jnp.int32),
            pltpu.SMEM((n_slots,), jnp.int32),
            pltpu.SMEM((4 * n_slots,), jnp.int32),
            pltpu.SMEM((4,), jnp.int32),
            pltpu.SemaphoreType.DMA((13,)),
            pltpu.SemaphoreType.DMA((15,)),
        ],
        compiler_params=pltpu.CompilerParams(vmem_limit_bytes=56 * MIB),
        cost_estimate=pl.CostEstimate(
            flops=10 * tokens * width * cols, bytes_accessed=24 * MIB, transcendentals=tokens * cols
        ),
        name="device_step",
    )(info, cot, step, task, lang, x, xt, *gates, *ups)


def add_pair_kernel(a_ref, b_ref, _mark, out_ref):
    f32 = jnp.float32
    out_ref[...] = (a_ref[...].astype(f32) + b_ref[...].astype(f32)).astype(out_ref.dtype)


def add_pair(a, b, mark):
    vmem = pl.BlockSpec(memory_space=pltpu.VMEM)
    return pl.pallas_call(
        add_pair_kernel,
        out_shape=jax.ShapeDtypeStruct(a.shape, a.dtype),
        in_specs=[vmem, vmem, pl.BlockSpec(memory_space=pl.ANY)],
        out_specs=vmem,
        compiler_params=pltpu.CompilerParams(vmem_limit_bytes=4 * MIB),
        cost_estimate=pl.CostEstimate(flops=a.size, bytes_accessed=MIB, transcendentals=0),
        name="add_pair",
    )(a, b, mark)


def pace_kernel(*refs):
    refs[-1][...] = jnp.zeros_like(refs[-1])


def pace(*arrays, flops=10**11, vmem=MIB):
    return pl.pallas_call(
        pace_kernel,
        out_shape=jax.ShapeDtypeStruct((8, BLK), jnp.float32),
        in_specs=[pl.BlockSpec(memory_space=pl.ANY)] * len(arrays),
        out_specs=pl.BlockSpec(memory_space=pltpu.VMEM),
        compiler_params=pltpu.CompilerParams(vmem_limit_bytes=vmem),
        cost_estimate=pl.CostEstimate(flops=flops, bytes_accessed=4096, transcendentals=0),
        name="pace",
    )(*arrays)


def ring_first(axis, up_first, down_first):
    return (
        lax.ppermute(up_first, axis, ring(axis, 1)),
        lax.ppermute(down_first, axis, ring(axis, -1)),
    )


def ring_rest(axis, own, up_second, down_second, from_left, from_right):
    f32, bf16 = jnp.float32, jnp.bfloat16
    half = own.shape[0] // 2
    up_second = (up_second.astype(f32) + from_left[:half].astype(f32)).astype(bf16)
    down_second = (down_second.astype(f32) + from_right[half:].astype(f32)).astype(bf16)
    low_left = lax.ppermute(up_second, axis, ring(axis, 1))
    high_right = lax.ppermute(down_second, axis, ring(axis, -1))
    low = own[:half].astype(f32) + low_left.astype(f32) + from_right[:half].astype(f32)
    high = own[half:].astype(f32) + high_right.astype(f32) + from_left[half:].astype(f32)
    return jnp.concatenate([low, high], axis=0).astype(bf16)


def on_device(
    tokens_in,
    cotangent,
    gate_base,
    up_base,
    lang_delta,
    lang_cell,
    group_lang,
    task_delta,
    task_slab,
    task_cell,
):
    f32, bf16 = jnp.float32, jnp.bfloat16
    fsdp = ("z_far", "z_near", "core")
    n_lang, n_far, n_near, n_core, n_dp = (
        lax.axis_size(a) for a in ("lang", "z_far", "z_near", "core", "dp")
    )
    n_z = n_far * n_near
    n_fsdp = n_z * n_core
    language = group_lang[0]
    my_lang, my_core, my_dp = (lax.axis_index(a) for a in ("lang", "core", "dp"))
    held = task_delta.shape[0]

    gate_left = lax.ppermute(gate_base, "dp", ring("dp", 1))
    up_right = lax.ppermute(up_base, "dp", ring("dp", -1))
    up_left = lax.ppermute(up_base, "dp", ring("dp", 1))
    gate_right = lax.ppermute(gate_base, "dp", ring("dp", -1))
    target = task_slab[:, 0]
    send_task = place(target, task_cell[:, 0], task_delta.reshape(held, 2 * BLK, BLK), n_fsdp)
    got_task = lax.all_to_all(send_task, fsdp, split_axis=0, concat_axis=0, tiled=True)
    lang_tiles = lang_delta[0, 0].reshape(lang_delta.shape[2:4] + (2 * BLK, BLK))
    with_cell = with_cells(lang_tiles, lang_cell[0, 0])
    send_lang = [
        lax.dynamic_index_in_dim(with_cell, lax.rem(my_lang + k, n_lang), 0, keepdims=False)
        for k in range(n_lang)
    ]
    step = pace(gate_left, gate_right, up_left, up_right, *send_lang, vmem=62 * MIB)
    gate_on, up_on, step, *send_lang = lax.optimization_barrier(
        (gate_left, up_right, step, *send_lang)
    )
    gate_far = lax.ppermute(gate_on, "dp", ring("dp", 1))
    up_far = lax.ppermute(up_on, "dp", ring("dp", -1))
    choice = lax.rem(my_lang - language + n_lang, n_lang)
    chosen = send_lang[0]
    for k in range(1, n_lang):
        chosen = jnp.where(choice == k, lax.ppermute(send_lang[k], "lang", ring("lang", k)), chosen)

    tokens_t = tokens_in.T
    step = pace(step, tokens_t, flops=0, vmem=62 * MIB)
    *pieces, keep, give = device_step(
        jnp.stack([my_dp, my_core, my_lang]).astype(jnp.int32),
        cotangent,
        got_task,
        chosen,
        tokens_in,
        tokens_t,
        (gate_base, gate_right, gate_far, gate_left),
        (up_base, up_right, up_far, up_left),
        step,
    )
    got = lax.ppermute(give, "core", ring("core", 1))
    own, far_low, far_high, right_low, right_high, left_low, left_high = pieces
    far_up = lax.ppermute(far_low, "dp", ring("dp", 1))
    far_down = lax.ppermute(far_high, "dp", ring("dp", -1))
    high_up = lax.ppermute(right_high, "dp", ring("dp", 1))
    low_down = lax.ppermute(left_low, "dp", ring("dp", -1))

    def both(first, last):
        first, last = first * n_z // 2, last * n_z // 2
        return (keep[first:last].astype(f32) + got[first:last].astype(f32)).astype(bf16)

    main_up = jnp.concatenate([both(4, 5), both(3, 4)], axis=0)
    main_down = jnp.concatenate([both(6, 7), both(5, 6)], axis=0)
    main_first = ring_first("lang", main_up, main_down)
    mark = pace(main_up, main_down)
    far_up, far_down, mark = lax.optimization_barrier((far_up, far_down, mark))
    low_up = (right_low.astype(f32) + far_up.astype(f32)).astype(bf16)
    high_down = (left_high.astype(f32) + far_down.astype(f32)).astype(bf16)
    low_up = lax.ppermute(low_up, "dp", ring("dp", 1))
    high_down = lax.ppermute(high_down, "dp", ring("dp", -1))
    half = own.shape[0] // 2
    low = own[:half].astype(f32) + low_up.astype(f32) + low_down.astype(f32)
    high = own[half:].astype(f32) + high_up.astype(f32) + high_down.astype(f32)
    tsum = jnp.concatenate([low, high], axis=0).astype(bf16)
    over_lang = ring_rest("lang", both(0, 2), both(2, 3), both(7, 8), *main_first)
    my_near = lax.axis_index("z_near")
    by_near = over_lang.reshape(n_far, n_near, *over_lang.shape[1:])
    keep_z = lax.dynamic_index_in_dim(by_near, my_near, 1, keepdims=False)
    give_z = lax.dynamic_index_in_dim(by_near, 1 - my_near, 1, keepdims=False)
    got_z = lax.ppermute(give_z, "z_near", ring("z_near", 1))
    mark = pace(give_z, mark, flops=0)
    back = lax.all_to_all(tsum, fsdp, split_axis=0, concat_axis=0, tiled=True)
    mine = take_own(target, back, mark).reshape(held, -1)
    far, right, left = [lax.ppermute(mine, "dp", ring("dp", -k)) for k in (2, 1, 3)]
    stacked = jnp.stack([mine, right, far, left], axis=0)
    task_grad = jnp.concatenate(
        [
            lax.dynamic_index_in_dim(stacked, lax.rem(q - my_dp + n_dp, n_dp), 0, keepdims=False)
            for q in range(n_dp)
        ],
        axis=1,
    ).astype(f32)

    near_sum = add_pair(keep_z, got_z, mine)
    over_z = lax.all_to_all(near_sum, "z_far", split_axis=0, concat_axis=0, tiled=True)
    grad_input = jnp.sum(over_z.astype(f32), axis=0).astype(bf16)
    return (grad_input, task_grad)


def solution(mesh):
    lang, fsdp, dp = (mesh.shape[a] for a in ("lang", "fsdp", "dp"))
    sizes = (lang, fsdp // 4, 2, 2, dp)
    fine = Mesh(mesh.devices.reshape(sizes), ("lang", "z_far", "z_near", "core", "dp"))
    cols = ("lang", "z_far", "z_near", "core")
    return jax.shard_map(
        on_device,
        mesh=fine,
        in_specs=(
            P("dp", None),
            P("dp", cols),
            P("dp", cols),
            P("dp", cols),
            P("lang", cols[1:], None, None, None),
            P("lang", cols[1:], None, None),
            P("dp"),
            P(cols, None),
            P(cols, None),
            P(cols, None),
        ),
        out_specs=(P("dp", cols), P(cols, None)),
        check_vma=False,
    )
```
